128 devices in a mesh: lat: 8 (over y, z_lo), lon: 16 (over z_hi, x, core).
Axes of the slice: x: 4, y: 4, z: 4 (z_hi: 2, z_lo: 2; z = z_hi * 2 + z_lo), core: 2. Of those that a mesh axis runs over, the one named last changes fastest.
Arguments:
- tokens: bfloat16 [224, 448, 4, 256], P('lat', 'lon'), may hold values from -36 to 36
- out_grad: bfloat16 [224, 448, 4, 256], P('lat', 'lon'), may hold values from -6 to 6
- gains: float32 [2, 256], replicated, may hold values from 0.25 to 1.75
- shifts: float32 [2, 256], replicated, may hold values from -3 to 3
- w_qkv: bfloat16 [256, 768], replicated, may hold values from -0.375 to 0.375
- b_qkv: float32 [768], replicated, may hold values from -3 to 3
- w_proj: bfloat16 [256, 256], replicated, may hold values from -0.375 to 0.375
- w_in: bfloat16 [256, 1024], replicated, may hold values from -0.375 to 0.375
- w_out: bfloat16 [1024, 256], replicated, may hold values from -0.1875 to 0.1875
- rel_bias: float32 [8, 507], replicated, may hold values from -4 to 320
Outputs:
- result: bfloat16 [224, 448, 4, 256], P('lat', 'lon')
- in_grad: bfloat16 [224, 448, 4, 256], P('lat', 'lon')
- grad_gains: float32 [2, 256], replicated
- grad_shifts: float32 [2, 256], replicated
- grad_w_qkv: float32 [256, 768], replicated
- grad_b_qkv: float32 [768], replicated
- grad_w_proj: float32 [256, 256], replicated
- grad_w_in: float32 [256, 1024], replicated
- grad_w_out: float32 [1024, 256], replicated
- grad_rel_bias: float32 [8, 507], replicated
The draws below stay inside these ranges and needn't reach their ends.
All inputs are finite; a program needn't handle non-finite values.
Results may differ from the reference program's by a relative error of at most 0.012.
Values may be sent and summed in bfloat16 or wider, within the bound.
A program may use at most 192 MiB of HBM per device.

```python
import math
import jax
import jax.numpy as jnp
from jax import lax

C = 256
HEADS = 8
FF = 1024
WIN = 7
LEV = 4
WLEV = 2
SHIFT = 3
NLAT = 224
NLON = 448
WTOK = 98
NREL = 507
TOKENS = 401408


def draw_tokens(key, part):
    key = jax.random.fold_in(key, 11)
    noise_key, row_key, col_key = jax.random.split(key, 3)
    full_shape = (NLAT, NLON, LEV, C)
    noise_base = jax.random.truncated_normal(noise_key, -4.0, 4.0, full_shape, jnp.float32)
    row_scale = jnp.exp(jax.random.uniform(row_key, (NLAT, NLON, LEV, 1), jnp.float32, math.log(0.3), math.log(3.0)))
    col_scale = jnp.exp(jax.random.uniform(col_key, (C,), jnp.float32, math.log(0.3), math.log(3.0)))
    return (noise_base * row_scale * col_scale).astype(jnp.bfloat16)


def draw_rel_bias(key, part):
    key = jax.random.fold_in(key, 23)
    full_shape = (HEADS, NREL)
    table = 0.7 * jax.random.truncated_normal(key, -4.0, 4.0, full_shape, jnp.float32)
    return table.astype(jnp.float32)


def level_of(own_key, shape, shards, low, high):
    level = 1.0
    for dim, parts in shards:
        heights = jax.random.uniform(jax.random.fold_in(jax.random.fold_in(own_key, 6), dim), (parts,), jnp.float32, low / len(shards), high / len(shards))
        level = level * jnp.repeat(jnp.exp(heights), shape[dim] // parts).reshape((-1,) + (1,) * (len(shape) - 1 - dim))
    return level


def noise(key, shape, deviation, most, cuts=(), held_as=jnp.bfloat16):
    loudness = level_of(key, shape, cuts, -0.22, 0.18) if cuts else 1.0
    entries = jax.random.normal(key, shape, jnp.float32) * deviation * loudness
    return jnp.minimum(jnp.maximum(entries, -most), most).astype(held_as)


def setup_inputs(seed: int = 0) -> dict:
    keys = jax.random.split(jax.random.key(seed), 11)
    tokens = draw_tokens(jax.random.fold_in(keys[10], 71), 0)
    out_grad = noise(keys[1], (NLAT, NLON, LEV, C), 1.0, 6.0, ((0, 8), (1, 16)))
    gains = jnp.clip(1.0 + 0.15 * jax.random.normal(keys[2], (2, C), jnp.float32), 0.25, 1.75)
    shifts = noise(keys[3], (2, C), 0.5, 3.0, (), jnp.float32)
    w_qkv = noise(keys[4], (C, 3 * C), C ** -0.5, 0.375)
    b_qkv = noise(keys[5], (3 * C,), 0.5, 3.0, (), jnp.float32)
    w_proj = noise(keys[6], (C, C), C ** -0.5, 0.375)
    w_in = noise(keys[7], (C, FF), C ** -0.5, 0.375)
    w_out = noise(keys[8], (FF, C), FF ** -0.5, 0.1875)
    rel_bias = draw_rel_bias(jax.random.fold_in(keys[10], 71), 0)
    return dict(tokens=tokens, out_grad=out_grad, gains=gains, shifts=shifts, w_qkv=w_qkv, b_qkv=b_qkv, w_proj=w_proj, w_in=w_in, w_out=w_out, rel_bias=rel_bias)


EPSILON = 1e-05
NEG_LARGE = -1e+30

def norm_forward(values, gain, offset):
    center = values - lax.optimization_barrier(jnp.mean(values, -1, keepdims=True))
    variance = lax.optimization_barrier(jnp.mean(center * center, -1, keepdims=True))
    inv_std = lax.rsqrt(variance + EPSILON)
    normed = center * inv_std
    return (normed, inv_std, (normed * gain + offset).astype(jnp.bfloat16))

def norm_backward(upstream, normed, inv_std, gain):
    scaled = upstream * gain
    return inv_std * (scaled - lax.optimization_barrier(jnp.mean(scaled, -1, keepdims=True)) - normed * lax.optimization_barrier(jnp.mean(scaled * normed, -1, keepdims=True)))

def relative_table():
    positions = jnp.arange(WTOK, dtype=jnp.int32)
    lat_pos = positions // (WIN * WLEV)
    lon_pos = positions // WLEV % WIN
    lev_pos = positions % WLEV
    offsets = ((lat_pos[:, None] - lat_pos[None, :] + WIN - 1) * (2 * WIN - 1) + lon_pos[:, None] - lon_pos[None, :] + WIN - 1) * (2 * WLEV - 1) + lev_pos[:, None] - lev_pos[None, :] + WLEV - 1
    return (offsets.reshape(-1)[:, None] == jnp.arange(NREL, dtype=jnp.int32)[None, :]).astype(jnp.float32)

def to_windows(block):
    rows_n, cols_n, levels, channels = block.shape
    tiled = block.reshape(rows_n // WIN, WIN, cols_n // WIN, WIN, levels // WLEV, WLEV, channels)
    return tiled.transpose(0, 2, 4, 1, 3, 5, 6).reshape(-1, WIN * WIN * WLEV, channels)

def from_windows(windows, rows_n, cols_n):
    channels = windows.shape[-1]
    tiled = windows.reshape(rows_n // WIN, cols_n // WIN, LEV // WLEV, WIN, WIN, WLEV, channels)
    return tiled.transpose(0, 3, 1, 4, 2, 5, 6).reshape(rows_n, cols_n, LEV, channels)

def forward(windows, allowed, onehot, params):
    gains, shifts, w_qkv, b_qkv, w_proj, w_in, w_out, rel_bias = params
    count, width_tok, channels = windows.shape
    heads = rel_bias.shape[0]
    head_dim = channels // heads
    flat = windows.reshape(count * width_tok, channels).astype(jnp.float32)
    normed1, inv_std1, hidden1 = norm_forward(flat, gains[0], shifts[0])
    projected = (jnp.dot(hidden1, w_qkv, preferred_element_type=jnp.float32) + b_qkv).astype(jnp.bfloat16)
    projected = projected.reshape(count, width_tok, 3, heads, head_dim)
    queries = projected[:, :, 0]
    keys_in = projected[:, :, 1]
    values_in = projected[:, :, 2]
    bias_full = jnp.dot(rel_bias, onehot.T, precision=lax.Precision.HIGHEST).reshape(heads, width_tok, width_tok)
    scores = jnp.einsum('bqhd,bkhd->bhqk', queries.astype(jnp.float32), keys_in.astype(jnp.float32)) * head_dim ** (-0.5) + bias_full[None]
    scores = jnp.where(allowed[:, None], scores, NEG_LARGE)
    highest = lax.optimization_barrier(jnp.max(scores, -1, keepdims=True))
    weights_raw = jnp.exp(scores - highest)
    attention = weights_raw / lax.optimization_barrier(jnp.sum(weights_raw, -1, keepdims=True))
    attention_low = attention.astype(jnp.bfloat16)
    mixed = jnp.einsum('bhqk,bkhd->bqhd', attention_low.astype(jnp.float32), values_in.astype(jnp.float32))
    mixed = mixed.astype(jnp.bfloat16).reshape(count * width_tok, channels)
    residual = flat + jnp.dot(mixed, w_proj, preferred_element_type=jnp.float32)
    normed2, inv_std2, hidden2 = norm_forward(residual, gains[1], shifts[1])
    pre_gelu = jnp.dot(hidden2, w_in, preferred_element_type=jnp.float32)
    activated = jax.nn.gelu(pre_gelu).astype(jnp.bfloat16)
    block_out = (residual + jnp.dot(activated, w_out, preferred_element_type=jnp.float32)).astype(jnp.bfloat16)
    saved = (normed1, inv_std1, hidden1, queries, keys_in, values_in, attention, attention_low, mixed, normed2, inv_std2, hidden2, pre_gelu, activated)
    return (block_out.reshape(count, width_tok, channels), saved)

def mlp_backward(grad_windows, saved, params):
    gains, shifts, w_qkv, b_qkv, w_proj, w_in, w_out, rel_bias = params
    normed2, inv_std2, hidden2, pre_gelu, activated = (saved[9], saved[10], saved[11], saved[12], saved[13])
    grad_low = grad_windows.reshape(-1, grad_windows.shape[-1])
    grad_w_out = jnp.dot(activated.T, grad_low, preferred_element_type=jnp.float32)
    grad_act = jnp.dot(grad_low, w_out.T, preferred_element_type=jnp.float32)
    unused, pullback = jax.vjp(jax.nn.gelu, pre_gelu)
    grad_pre = pullback(grad_act)[0].astype(jnp.bfloat16)
    grad_w_in = jnp.dot(hidden2.T, grad_pre, preferred_element_type=jnp.float32)
    grad_hidden2 = jnp.dot(grad_pre, w_in.T, preferred_element_type=jnp.float32)
    grad_gain2 = lax.optimization_barrier(jnp.sum(grad_hidden2 * normed2, 0))
    grad_shift2 = lax.optimization_barrier(jnp.sum(grad_hidden2, 0))
    grad_resid = grad_low.astype(jnp.float32) + norm_backward(grad_hidden2, normed2, inv_std2, gains[1])
    return (grad_resid, (grad_w_in, grad_w_out, grad_gain2, grad_shift2))

def attention_backward(grad_resid, saved, params, onehot):
    gains, shifts, w_qkv, b_qkv, w_proj, w_in, w_out, rel_bias = params
    normed1, inv_std1, hidden1, queries, keys_in, values_in, attention, attention_low, mixed = saved[:9]
    count, width_tok, heads, head_dim = queries.shape
    channels = heads * head_dim
    grad_low = grad_resid.astype(jnp.bfloat16)
    grad_w_proj = jnp.dot(mixed.T, grad_low, preferred_element_type=jnp.float32)
    grad_mixed = jnp.dot(grad_low, w_proj.T, preferred_element_type=jnp.float32).astype(jnp.bfloat16)
    grad_mixed = grad_mixed.reshape(count, width_tok, heads, head_dim).astype(jnp.float32)
    grad_attn = jnp.einsum('bqhd,bkhd->bhqk', grad_mixed, values_in.astype(jnp.float32))
    grad_values = jnp.einsum('bhqk,bqhd->bkhd', attention_low.astype(jnp.float32), grad_mixed).astype(jnp.bfloat16)
    grad_scores = attention * (grad_attn - lax.optimization_barrier(jnp.sum(grad_attn * attention, -1, keepdims=True)))
    grad_bias = lax.optimization_barrier(jnp.sum(grad_scores, 0)).reshape(heads, width_tok * width_tok)
    grad_table = jnp.dot(grad_bias, onehot, precision=lax.Precision.HIGHEST)
    grad_scaled = (grad_scores * head_dim ** (-0.5)).astype(jnp.bfloat16).astype(jnp.float32)
    grad_queries = jnp.einsum('bhqk,bkhd->bqhd', grad_scaled, keys_in.astype(jnp.float32)).astype(jnp.bfloat16)
    grad_keys = jnp.einsum('bhqk,bqhd->bkhd', grad_scaled, queries.astype(jnp.float32)).astype(jnp.bfloat16)
    grad_proj = jnp.stack([grad_queries, grad_keys, grad_values], 2).reshape(count * width_tok, 3 * channels)
    grad_w_qkv = jnp.dot(hidden1.T, grad_proj, preferred_element_type=jnp.float32)
    grad_b_qkv = lax.optimization_barrier(jnp.sum(grad_proj, 0, dtype=jnp.float32))
    grad_hidden1 = jnp.dot(grad_proj, w_qkv.T, preferred_element_type=jnp.float32)
    grad_gain1 = lax.optimization_barrier(jnp.sum(grad_hidden1 * normed1, 0))
    grad_shift1 = lax.optimization_barrier(jnp.sum(grad_hidden1, 0))
    grad_input = (grad_resid + norm_backward(grad_hidden1, normed1, inv_std1, gains[0])).astype(jnp.bfloat16)
    return (grad_input.reshape(count, width_tok, channels), (grad_w_qkv, grad_b_qkv, grad_w_proj, grad_gain1, grad_shift1, grad_table))

def reference(tokens, out_grad, gains, shifts, w_qkv, b_qkv, w_proj, w_in, w_out, rel_bias):
    params = (gains, shifts, w_qkv, b_qkv, w_proj, w_in, w_out, rel_bias)
    onehot = relative_table()
    rolled = jnp.roll(tokens, (-SHIFT, -SHIFT), (0, 1))
    grad_rolled = jnp.roll(out_grad, (-SHIFT, -SHIFT), (0, 1))
    bands = NLAT // WIN
    band_tokens = rolled.reshape(bands, WIN, NLON, LEV, C)
    band_grads = grad_rolled.reshape(bands, WIN, NLON, LEV, C)

    def band_step(totals, inputs):
        band_index, tok_band, grad_band = inputs
        windows = to_windows(tok_band)
        row_ids = band_index * WIN + jnp.arange(WIN, dtype=jnp.int32)
        group_tok = jnp.repeat(row_ids >= NLAT - SHIFT, WIN * WLEV)
        allowed = jnp.broadcast_to((group_tok[:, None] == group_tok[None, :])[None], (windows.shape[0], WTOK, WTOK))
        block_out, saved = forward(windows, allowed, onehot, params)
        grad_resid, mlp_terms = mlp_backward(to_windows(grad_band), saved, params)
        grad_input, attn_terms = attention_backward(grad_resid, saved, params, onehot)
        totals = tuple((total + term for total, term in zip(totals, mlp_terms + attn_terms)))
        return (totals, (from_windows(block_out, WIN, NLON), from_windows(grad_input, WIN, NLON)))
    zeros = (jnp.zeros((C, FF), jnp.float32), jnp.zeros((FF, C), jnp.float32), jnp.zeros((C,), jnp.float32), jnp.zeros((C,), jnp.float32), jnp.zeros((C, 3 * C), jnp.float32), jnp.zeros((3 * C,), jnp.float32), jnp.zeros((C, C), jnp.float32), jnp.zeros((C,), jnp.float32), jnp.zeros((C,), jnp.float32), jnp.zeros((HEADS, NREL), jnp.float32))
    totals, outputs = lax.scan(band_step, zeros, (jnp.arange(bands, dtype=jnp.int32), band_tokens, band_grads))
    block_all = outputs[0].reshape(NLAT, NLON, LEV, C)
    grad_all = outputs[1].reshape(NLAT, NLON, LEV, C)
    result = jnp.roll(block_all, (SHIFT, SHIFT), (0, 1))
    in_grad = jnp.roll(grad_all, (SHIFT, SHIFT), (0, 1))
    grad_w_in, grad_w_out, grad_gain2, grad_shift2, grad_w_qkv, grad_b_qkv, grad_w_proj, grad_gain1, grad_shift1, grad_table = totals
    scale = TOKENS ** (-0.5)
    return (result, in_grad, jnp.stack([grad_gain1, grad_gain2]) * scale, jnp.stack([grad_shift1, grad_shift2]) * scale, grad_w_qkv * scale, grad_b_qkv * scale, grad_w_proj * scale, grad_w_in * scale, grad_w_out * scale, grad_table * scale)
```

```python
import functools

import jax
import jax.numpy as jnp
import numpy as np
from jax import lax
from jax.experimental import pallas as pl
from jax.experimental.pallas import tpu as pltpu
from jax.sharding import PartitionSpec as P

WIN = 7
LEV = 4
WLEV = 2
SHIFT = 3
EPS = 1e-05
NEG = -1e30
HEADS = 8
HD = 32
C = 256
FF = 1024
SLAB = 16
WROWS = WIN * SLAB
HALF = HEADS // 2
PAIR = 2 * 128
NREL = 507
BF = jnp.bfloat16
F32 = jnp.float32

NN = (((1,), (0,)), ((), ()))
NT = (((1,), (1,)), ((), ()))
TN = (((0,), (0,)), ((), ()))


def dot(a, b, dims=NN):
    return lax.dot_general(a, b, dims, preferred_element_type=F32)


def placement():
    matrix = np.zeros((128, 128), np.float32)
    for wc in range(4):
        for lw in range(2):
            for b in range(WIN):
                for l in range(WLEV):
                    row = (wc * 2 + lw) * SLAB + b * WLEV + l
                    matrix[row, (wc * WIN + SHIFT + b) * LEV + lw * WLEV + l] = 1.0
    return matrix


def strip_map():
    index = np.full((SLAB, 256), -1, np.int32)
    for bk in range(WIN):
        for lk in range(WLEV):
            for da in range(13):
                for bq in range(WIN):
                    for lq in range(WLEV):
                        index[bk * WLEV + lk, da * SLAB + bq * WLEV + lq] = (
                            (da * 13 + bq - bk + 6) * 3 + lq - lk + 1
                        )
    return index


def layer_norm(x, gain, shift):
    center = x - jnp.mean(x, -1, keepdims=True)
    istd = lax.rsqrt(jnp.mean(center * center, -1, keepdims=True) + EPS)
    xhat = center * istd
    return xhat, istd, (xhat * gain + shift).astype(BF)


def norm_backward(up, xhat, istd, gain):
    n = up * gain
    return istd * (n - jnp.mean(n, -1, keepdims=True) - xhat * jnp.mean(n * xhat, -1, keepdims=True))


def gelu_both(p):
    c0 = np.float32(np.sqrt(2.0 / np.pi))
    c1 = np.float32(0.044715 * np.sqrt(2.0 / np.pi))
    p2 = p * p
    t = jnp.tanh(p * (c0 + c1 * p2))
    h = 0.5 * p
    half = 0.5 + 0.5 * t
    act = p * half
    slope = half + h * (1.0 - t * t) * (c0 + (3.0 * c1) * p2)
    return act, slope


def head_masks():
    lane = lax.broadcasted_iota(jnp.int32, (1, C), 1) // HD
    pair = [((lane % HALF) == j) for j in range(HALF)]
    group = [((lane // HALF) == g) for g in range(2)]
    return pair, group


def stack_pairs(v, pair):
    return jnp.concatenate([v * m.astype(BF) for m in pair], 0)


def stack_groups(v, group):
    pad = jnp.zeros((128 - WROWS, C), BF)
    return jnp.concatenate([v * group[0].astype(BF), pad, v * group[1].astype(BF), pad], 0)


def pick_pairs(r, pair):
    out = r[3 * WROWS:4 * WROWS]
    for j in range(3):
        out = jnp.where(pair[j], r[j * WROWS:(j + 1) * WROWS], out)
    return out


def down_keys(vt, low):
    parts = [None] * HEADS
    for j in range(HALF):
        lhs = jnp.concatenate([vt[j * HD:(j + 1) * HD], vt[(j + HALF) * HD:(j + HALF + 1) * HD]], 0)
        out = dot(lhs, low[j * WROWS:(j + 1) * WROWS])
        parts[j] = out[:HD, :128]
        parts[j + HALF] = out[HD:, 128:]
    return jnp.concatenate(parts, 0).T[:WROWS]


def compute(refs, s, chunk_windows=4):
    pair, group = head_masks()
    scale = np.float32(HD ** -0.5)
    CH = chunk_windows * WROWS
    nwin = 32

    def gather(src, dst):
        def row(r, _):
            y = dot(s.pm[...], src[r]).astype(BF)
            wr, a = r // WIN, r % WIN
            for c in range(8):
                dst[pl.ds(pl.multiple_of((wr * 8 + c) * WROWS + a * SLAB, SLAB), SLAB), :] = y[c * SLAB:(c + 1) * SLAB]
            return 0
        lax.fori_loop(0, 28, row, 0, unroll=2)

    gather(s.x, s.z)
    gather(s.g, s.gz)

    key_row = lax.broadcasted_iota(jnp.int32, (WROWS, 256), 0)
    lane = lax.broadcasted_iota(jnp.int32, (WROWS, 256), 1)
    qa, ka = (lane % 128) // SLAB, key_row // SLAB
    empty = (key_row % SLAB) >= WIN * WLEV
    cut = jnp.logical_and((qa >= WIN - SHIFT) != (ka >= WIN - SHIFT), s.last)
    for j in range(HALF):
        tiles = []
        for g in range(2):
            strip = s.strip[j + HALF * g]
            rows = [strip[:, (6 - ak) * SLAB:(6 - ak) * SLAB + WROWS] for ak in range(WIN)]
            tile = jnp.concatenate(rows, 0)
            tiles.append(jnp.concatenate([tile, jnp.zeros((WROWS, 128 - WROWS), F32)], 1))
        full = jnp.where(empty, NEG, jnp.concatenate(tiles, 1))
        s.bias[0, j * WROWS:(j + 1) * WROWS] = full
        s.bias[1, j * WROWS:(j + 1) * WROWS] = jnp.where(cut, NEG, full)
    s.dbias[...] = jnp.zeros_like(s.dbias)
    s.gw_in[...] = jnp.zeros_like(s.gw_in)
    s.gw_out[...] = jnp.zeros_like(s.gw_out)
    s.gw_qkv[...] = jnp.zeros_like(s.gw_qkv)
    s.gw_proj[...] = jnp.zeros_like(s.gw_proj)
    s.small[...] = jnp.zeros_like(s.small)

    def forward_window(w):
        rows = pl.ds(pl.multiple_of(w * WROWS, WROWS), WROWS)
        arows = pl.multiple_of(w * (HALF * WROWS), HALF * WROWS)
        q, k, v = s.p[rows, 0:C], s.p[rows, C:2 * C], s.p[rows, 2 * C:3 * C]
        scores = dot(stack_pairs(k, pair), stack_groups(q, group), NT)
        which = (w >= 24).astype(jnp.int32)
        vt = v.T
        lows = []
        for j in range(HALF):
            t = scores[j * WROWS:(j + 1) * WROWS] * scale + s.bias[which, j * WROWS:(j + 1) * WROWS]
            e = jnp.exp(t - jnp.max(t, 0, keepdims=True))
            att = e * (1.0 / jnp.sum(e, 0, keepdims=True))
            s.att[pl.ds(arows + j * WROWS, WROWS), :] = att
            lows.append(att.astype(BF))
        s.mixed[rows, :] = down_keys(vt, jnp.concatenate(lows, 0)).astype(BF)

    def phase_a(i, _):
        rows = pl.ds(pl.multiple_of(i * CH, CH), CH)
        x = s.z[rows, :].astype(F32)
        _, _, hidden1 = layer_norm(x, s.gains[0:1], s.shifts[0:1])
        s.p[rows, :] = (dot(hidden1, s.w_qkv[...]) + s.b_qkv[...]).astype(BF)

        def win(w, _):
            forward_window(i * chunk_windows + 2 * w)
            forward_window(i * chunk_windows + 2 * w + 1)
            return 0
        lax.fori_loop(0, chunk_windows // 2, win, 0)

        mixed = s.mixed[rows, :]
        resid = s.z[rows, :].astype(F32) + dot(mixed, s.w_proj[...])
        xhat2, istd2, hidden2 = layer_norm(resid, s.gains[1:2], s.shifts[1:2])
        act, slope = gelu_both(dot(hidden2, s.w_in[...]))
        act = act.astype(BF)
        s.out[rows, :] = (resid + dot(act, s.w_out[...])).astype(BF)
        gr = s.gz[rows, :]
        s.gw_out[...] += dot(gr, act, TN)
        gp = (dot(gr, s.w_out[...], NT) * slope).astype(BF)
        s.gw_in[...] += dot(hidden2, gp, TN)
        gh = dot(gp, s.w_in[...], NT)
        s.small[1:2, 0:C] += jnp.sum(gh * xhat2, 0, keepdims=True)
        s.small[3:4, 0:C] += jnp.sum(gh, 0, keepdims=True)
        gres = gr.astype(F32) + norm_backward(gh, xhat2, istd2, s.gains[1:2])
        s.gres[rows, :] = gres
        low = gres.astype(BF)
        s.gw_proj[...] += dot(mixed, low, TN)
        s.gm[rows, :] = dot(low, s.w_proj[...], NT).astype(BF)
        return 0

    lax.fori_loop(0, nwin // chunk_windows, phase_a, 0)

    def backward_window(w):
        rows = pl.ds(pl.multiple_of(w * WROWS, WROWS), WROWS)
        arows = pl.multiple_of(w * (HALF * WROWS), HALF * WROWS)
        q, k, v = s.p[rows, 0:C], s.p[rows, C:2 * C], s.p[rows, 2 * C:3 * C]
        gm2 = stack_groups(s.gm[rows, :], group)
        ga = dot(stack_pairs(v, pair), gm2, NT)
        lows, dlows = [], []
        for j in range(HALF):
            att = s.att[pl.ds(arows + j * WROWS, WROWS), :]
            t = att * ga[j * WROWS:(j + 1) * WROWS]
            ds = t - att * jnp.sum(t, 0, keepdims=True)
            s.dbias[j * WROWS:(j + 1) * WROWS] += ds
            lows.append(att.astype(BF))
            dlows.append((ds * scale).astype(BF))
        low, dlow = jnp.concatenate(lows, 0), jnp.concatenate(dlows, 0)
        gv = pick_pairs(dot(low, gm2), pair).astype(BF)
        gk = pick_pairs(dot(dlow, stack_groups(q, group)), pair).astype(BF)
        gq = down_keys(k.T, dlow).astype(BF)
        s.p[rows, 0:C] = gq
        s.p[rows, C:2 * C] = gk
        s.p[rows, 2 * C:3 * C] = gv

    def phase_b(i, _):
        rows = pl.ds(pl.multiple_of(i * CH, CH), CH)

        def win(w, _):
            backward_window(i * chunk_windows + 2 * w)
            backward_window(i * chunk_windows + 2 * w + 1)
            return 0
        lax.fori_loop(0, chunk_windows // 2, win, 0)
        xhat, istd, hidden = layer_norm(s.z[rows, :].astype(F32), s.gains[0:1], s.shifts[0:1])
        gp = s.p[rows, :]
        s.gw_qkv[...] += dot(hidden, gp, TN)
        s.small[4:5, :] += jnp.sum(gp.astype(F32), 0, keepdims=True)
        gh = dot(gp, s.w_qkv[...], NT)
        s.small[0:1, 0:C] += jnp.sum(gh * xhat, 0, keepdims=True)
        s.small[2:3, 0:C] += jnp.sum(gh, 0, keepdims=True)
        s.gout[rows, :] = (s.gres[rows, :] + norm_backward(gh, xhat, istd, s.gains[0:1])).astype(BF)
        return 0

    lax.fori_loop(0, nwin // chunk_windows, phase_b, 0)

    for h in range(HEADS):
        j, g = h % HALF, h // HALF
        total = None
        for ak in range(WIN):
            piece = s.dbias[j * WROWS + ak * SLAB:j * WROWS + (ak + 1) * SLAB, g * 128:g * 128 + WROWS]
            before = (6 - ak) * SLAB
            parts = []
            if before:
                parts.append(jnp.zeros((SLAB, before), F32))
            parts.append(piece)
            parts.append(jnp.zeros((SLAB, 256 - before - WROWS), F32))
            moved = jnp.concatenate(parts, 1)
            total = moved if total is None else total + moved
        s.dstrip[h] = total

    def scatter(src, dst):
        def row(r, _):
            wr, a = r // WIN, r % WIN
            y = jnp.concatenate(
                [src[pl.ds(pl.multiple_of((wr * 8 + c) * WROWS + a * SLAB, SLAB), SLAB), :] for c in range(8)], 0
            )
            dst[r] = dot(s.pm[...], y, TN).astype(BF)
            return 0
        lax.fori_loop(0, 28, row, 0, unroll=2)

    scatter(s.out, s.res)
    scatter(s.gout, s.ing)


class Refs:
    pass


INS = ("x", "g", "pm", "strip", "gains", "shifts", "w_qkv", "b_qkv", "w_proj", "w_in", "w_out")
OUTS = ("res", "ing", "gw_in", "gw_out", "gw_qkv", "gw_proj", "small", "dstrip")
SCR = ("z", "gz", "p", "att", "mixed", "out", "gout", "gres", "gm", "bias", "dbias")


def kernel(*refs):
    s = Refs()
    for name, ref in zip(INS + OUTS + SCR, refs):
        setattr(s, name, ref)
    s.last = lax.axis_index("lat") == lax.axis_size("lat") - 1
    compute(refs, s)


def fused(x, g, pm, strip, gains, shifts, w_qkv, b_qkv, w_proj, w_in, w_out):
    T = 32 * WROWS
    sds = jax.ShapeDtypeStruct
    vm = pl.BlockSpec(memory_space=pltpu.VMEM)
    return pl.pallas_call(
        kernel,
        out_shape=(
            sds((28, 128, C), BF), sds((28, 128, C), BF), sds((C, FF), F32), sds((C, FF), F32),
            sds((C, 3 * C), F32), sds((C, C), F32), sds((8, 3 * C), F32), sds((HEADS, SLAB, 256), F32),
        ),
        in_specs=[vm] * len(INS),
        out_specs=[vm] * len(OUTS),
        scratch_shapes=[
            pltpu.VMEM((T, C), BF), pltpu.VMEM((T, C), BF), pltpu.VMEM((T, 3 * C), BF),
            pltpu.VMEM((T * HALF, 256), F32), pltpu.VMEM((T, C), BF), pltpu.VMEM((T, C), BF),
            pltpu.VMEM((T, C), BF), pltpu.VMEM((T, C), F32), pltpu.VMEM((T, C), BF),
            pltpu.VMEM((2, HALF * WROWS, 256), F32), pltpu.VMEM((HALF * WROWS, 256), F32),
        ],
        compiler_params=pltpu.CompilerParams(vmem_limit_bytes=60 * 1024 * 1024),
        name="windows",
    )(x, g, pm, strip, gains, shifts, w_qkv, b_qkv, w_proj, w_in, w_out)


def shifted(value, axis, steps):
    count = lax.axis_size(axis)
    return lax.ppermute(value, axis, [(i, (i + steps) % count) for i in range(count)])


def roll_in(block):
    wide = jnp.concatenate([block, shifted(block[:, :16], "lon", -1)], 1)
    return jnp.concatenate([wide[SHIFT:], shifted(wide[:SHIFT], "lat", -1)], 0)


def roll_out(block):
    tall = jnp.concatenate([shifted(block[-SHIFT:], "lat", 1), block[:-SHIFT]], 0)
    got = shifted(tall[:, 112:], "lon", 1)
    return jnp.concatenate([tall[:, :16] + got, tall[:, 16:112]], 1)


def local(tokens, out_grad, gains, shifts, w_qkv, b_qkv, w_proj, w_in, w_out, rel_bias):
    rows_n, cols_n, levels, channels = tokens.shape
    total = rows_n * lax.axis_size("lat") * cols_n * lax.axis_size("lon") * levels
    x = roll_in(tokens.reshape(rows_n, cols_n * levels, channels))
    g = roll_in(out_grad.reshape(rows_n, cols_n * levels, channels))
    index = jnp.asarray(strip_map().reshape(-1))
    onehot = (index[:, None] == jnp.arange(NREL, dtype=jnp.int32)[None, :]).astype(F32)
    strip = lax.dot_general(rel_bias, onehot, NT, precision=lax.Precision.HIGHEST).reshape(HEADS, SLAB, 256)
    pm = jnp.asarray(placement(), BF)
    res, ing, gw_in, gw_out, gw_qkv, gw_proj, small, dstrip = fused(
        x, g, pm, strip, gains, shifts, w_qkv, b_qkv[None], w_proj, w_in, w_out
    )
    table = lax.dot_general(dstrip.reshape(HEADS, -1), onehot, NN, precision=lax.Precision.HIGHEST)
    sums = lax.psum((gw_in, gw_out, gw_qkv, gw_proj, small, table), ("lat", "lon"))
    gw_in, gw_out, gw_qkv, gw_proj, small, table = [v * float(total) ** -0.5 for v in sums]
    shape = tokens.shape
    return (
        roll_out(res).reshape(shape), roll_out(ing).reshape(shape),
        small[0:2, :C], small[2:4, :C], gw_qkv, small[4], gw_proj, gw_in, gw_out.T, table,
    )


def solution(mesh):
    big = P("lat", "lon", None, None)
    return jax.shard_map(
        local, mesh=mesh, in_specs=(big, big) + (P(),) * 8, out_specs=(big, big) + (P(),) * 8, check_vma=False
    )
```

```python
import functools

import jax
import jax.numpy as jnp
import numpy as np
from jax import lax
from jax.experimental import pallas as pl
from jax.experimental.pallas import tpu as pltpu
from jax.sharding import PartitionSpec as P

WIN = 7
LEV = 4
WLEV = 2
SHIFT = 3
EPS = 1e-05
NEG = -1e30
HEADS = 8
HD = 32
C = 256
FF = 1024
SLAB = 16
WROWS = WIN * SLAB
HALF = HEADS // 2
PAIR = 2 * 128
NREL = 507
BF = jnp.bfloat16
F32 = jnp.float32

NN = (((1,), (0,)), ((), ()))
NT = (((1,), (1,)), ((), ()))
TN = (((0,), (0,)), ((), ()))


def dot(a, b, dims=NN):
    return lax.dot_general(a, b, dims, preferred_element_type=F32)


def placement():
    matrix = np.zeros((128, 128), np.float32)
    for wc in range(4):
        for lw in range(2):
            for b in range(WIN):
                for l in range(WLEV):
                    row = (wc * 2 + lw) * SLAB + b * WLEV + l
                    matrix[row, (wc * WIN + SHIFT + b) * LEV + lw * WLEV + l] = 1.0
    return matrix


def strip_map():
    index = np.full((SLAB, 256), -1, np.int32)
    for bk in range(WIN):
        for lk in range(WLEV):
            for da in range(13):
                for bq in range(WIN):
                    for lq in range(WLEV):
                        index[bk * WLEV + lk, da * SLAB + bq * WLEV + lq] = (
                            (da * 13 + bq - bk + 6) * 3 + lq - lk + 1
                        )
    return index


def layer_norm(x, gain, shift):
    center = x - jnp.mean(x, -1, keepdims=True)
    istd = lax.rsqrt(jnp.mean(center * center, -1, keepdims=True) + EPS)
    xhat = center * istd
    return xhat, istd, (xhat * gain + shift).astype(BF)


def norm_backward(up, xhat, istd, gain):
    n = up * gain
    return istd * (n - jnp.mean(n, -1, keepdims=True) - xhat * jnp.mean(n * xhat, -1, keepdims=True))


def gelu_both(p):
    c0 = np.float32(np.sqrt(2.0 / np.pi))
    c1 = np.float32(0.044715 * np.sqrt(2.0 / np.pi))
    p2 = p * p
    t = jnp.tanh(p * (c0 + c1 * p2))
    h = 0.5 * p
    half = 0.5 + 0.5 * t
    act = p * half
    slope = half + h * (1.0 - t * t) * (c0 + (3.0 * c1) * p2)
    return act, slope


def head_masks():
    lane = lax.broadcasted_iota(jnp.int32, (1, C), 1) // HD
    pair = [((lane % HALF) == j) for j in range(HALF)]
    group = [((lane // HALF) == g) for g in range(2)]
    return pair, group


def stack_pairs(v, pair):
    return jnp.concatenate([v * m.astype(BF) for m in pair], 0)


def stack_groups(v, group):
    pad = jnp.zeros((128 - WROWS, C), BF)
    return jnp.concatenate([v * group[0].astype(BF), pad, v * group[1].astype(BF), pad], 0)


def pick_pairs(r, pair):
    out = r[3 * WROWS:4 * WROWS]
    for j in range(3):
        out = jnp.where(pair[j], r[j * WROWS:(j + 1) * WROWS], out)
    return out


def down_keys(vt, low):
    parts = [None] * HEADS
    for j in range(HALF):
        lhs = jnp.concatenate([vt[j * HD:(j + 1) * HD], vt[(j + HALF) * HD:(j + HALF + 1) * HD]], 0)
        out = dot(lhs, low[j * WROWS:(j + 1) * WROWS])
        parts[j] = out[:HD, :128]
        parts[j + HALF] = out[HD:, 128:]
    return jnp.concatenate(parts, 0).T[:WROWS]


EARLY, LATE = (0, 2304), (2304, 3200)
W_IN, W_OUT, W_PROJ, W_QKV, STRIP = slice(0, 1024), slice(1024, 2048), slice(2048, 2304), slice(2304, 3072), slice(3072, 3200)
COLS = 3200
MESH = pl.DeviceIdType.MESH


def send(src, dst, sems, index, device):
    return pltpu.make_async_remote_copy(
        src_ref=src, dst_ref=dst, send_sem=sems[0].at[index], recv_sem=sems[1].at[index],
        device_id=device, device_id_type=MESH,
    )


def greet(s):
    barrier = pltpu.get_barrier_semaphore()
    peers = [((s.lat + d) % 8, s.lon) for d in range(1, 8)] + [(s.lat, (s.lon + d) % 16) for d in range(1, 16)]
    peers += [((s.lat + d) % 8, (s.lon + d) % 16) for d in (1, -1)]
    for peer in peers:
        pl.semaphore_signal(barrier, inc=1, device_id=peer, device_id_type=MESH)
    pl.semaphore_wait(barrier, len(peers))


def halo_in(s):
    west, north = (s.lon + 15) % 16, (s.lat + 7) % 8
    far, near = [], []
    for n, (src, dst) in enumerate(((s.x_in, s.x), (s.g_in, s.g))):
        near.append(pltpu.make_async_copy(src, dst.at[0:28, 0:112], s.near_sem.at[n]))
        far.append(send(src.at[:, 0:16], dst.at[0:28, 112:128], s.halo, 3 * n, (s.lat, west)))
        far.append(send(src.at[0:SHIFT], dst.at[28:31, 0:112], s.halo, 3 * n + 1, (north, s.lon)))
        far.append(send(src.at[0:SHIFT, 0:16], dst.at[28:31, 112:128], s.halo, 3 * n + 2, (north, west)))
    for copy in near:
        copy.start()
    greet(s)
    for copy in far:
        copy.start()
    for copy in near + far:
        copy.wait()


def halo_out_copies(s, n):
    east, south = (s.lon + 1) % 16, (s.lat + 1) % 8
    return [
        send(s.side.at[n, SHIFT:28], s.land_side.at[n, SHIFT:28], s.halo, 6 + 3 * n, (s.lat, east)),
        send(s.foot.at[n, :, 0:112], s.land_foot.at[n], s.halo, 7 + 3 * n, (south, s.lon)),
        send(s.foot.at[n, :, 112:128], s.land_side.at[n, 0:SHIFT], s.halo, 8 + 3 * n, (south, east)),
    ]


def scatter(s, src, dst, n):
    def grid_row(r):
        wr, a = r // WIN, r % WIN
        y = jnp.concatenate(
            [src[pl.ds(pl.multiple_of((wr * 8 + c) * WROWS + a * SLAB, SLAB), SLAB), :] for c in range(8)], 0
        )
        return dot(s.pm[...], y, TN).astype(BF)

    for r in range(25, 28):
        s.foot[n, r - 25] = grid_row(r)

    def row(r, _):
        y = grid_row(r)
        dst[r + SHIFT] = y[:112]
        s.side[n, r + SHIFT] = y[112:]
        return 0
    lax.fori_loop(0, 25, row, 0, unroll=5)
    for copy in halo_out_copies(s, n):
        copy.start()


def halo_out_done(s, dst, n):
    for copy in halo_out_copies(s, n):
        copy.wait()
    dst[0:SHIFT] = s.land_foot[n]
    dst[:, 0:16] = dst[:, 0:16] + s.land_side[n]


class Exchange:
    def __init__(self, s, cols, number, small=False):
        self.s, self.cols, self.sems, self.small = s, slice(*cols), s.sums[number], small
        self.core, self.chip = s.lon % 2, s.lon // 2
        self.half = pl.ds(pl.multiple_of(self.core * 128, 128), 128)
        self.other = pl.ds(pl.multiple_of((1 - self.core) * 128, 128), 128)
        self.share = pl.ds(pl.multiple_of(self.core * 128 + self.chip * 16, 16), 16)
        self.twin = (s.lat, s.lon + 1 - 2 * self.core)

    def core_copies(self):
        s = self.s
        out = [send(s.sent.at[self.other, self.cols], s.land_core.at[:, self.cols], self.sems, 0, self.twin)]
        if self.small:
            out.append(send(s.small, s.small_core, self.sems, 24, self.twin))
        return out

    def lon_copies(self):
        s, out = self.s, []
        for d in range(1, 8):
            peer = (self.chip + d) % 8
            to = (s.lat, peer * 2 + self.core)
            rows = pl.ds(pl.multiple_of(peer * 16, 16), 16)
            out.append(send(s.part.at[rows, self.cols], s.land_lon.at[self.chip, :, self.cols], self.sems, d, to))
            if self.small:
                out.append(send(s.small_lon.at[self.chip], s.small_lon.at[self.chip], self.sems, 24 + d, to))
        return out

    def lat_copies(self):
        s, out = self.s, []
        for d in range(1, 8):
            to = ((s.lat + d) % 8, s.lon)
            mine = s.land_lat.at[s.lat, :, self.cols]
            out.append(send(mine, mine, self.sems, 8 + d, to))
            if self.small:
                out.append(send(s.small_lat.at[s.lat], s.small_lat.at[s.lat], self.sems, 32 + d, to))
        return out

    def gather_copies(self):
        s, out = self.s, []
        for d in range(1, 8):
            to = (s.lat, ((self.chip + d) % 8) * 2 + self.core)
            mine = s.total.at[self.share, self.cols]
            out.append(send(mine, mine, self.sems, 16 + d, to))
        return out

    def pair_copies(self):
        mine = self.s.total.at[self.half, self.cols]
        return [send(mine, mine, self.sems, 16, self.twin)]

    def core_start(self):
        s = self.s
        s.sent[self.other, self.cols] = s.acc[self.other, self.cols].astype(BF)
        for copy in self.core_copies():
            copy.start()

    def lon_start(self):
        s = self.s
        for copy in self.core_copies():
            copy.wait()
        both = s.acc[self.half, self.cols] + s.land_core[:, self.cols].astype(F32)
        s.acc[self.half, self.cols] = both
        s.part[:, self.cols] = both.astype(BF)
        if self.small:
            s.small_lon[self.chip] = s.small[...] + s.small_core[...]
        for copy in self.lon_copies():
            copy.start()

    def lat_start(self):
        s = self.s
        for copy in self.lon_copies():
            copy.wait()
        total = s.acc[self.share, self.cols]
        for d in range(1, 8):
            total += s.land_lon[(self.chip + d) % 8, :, self.cols].astype(F32)
        s.land_lat[s.lat, :, self.cols] = total.astype(BF)
        if self.small:
            s.small_lat[s.lat] = sum(s.small_lon[i] for i in range(8))
        for copy in self.lat_copies():
            copy.start()

    def gather_start(self):
        s = self.s
        for copy in self.lat_copies():
            copy.wait()
        total = s.land_lat[0, :, self.cols].astype(F32)
        for i in range(1, 8):
            total += s.land_lat[i, :, self.cols].astype(F32)
        s.total[self.share, self.cols] = total.astype(BF)
        if self.small:
            s.small_out[...] = sum(s.small_lat[i] for i in range(8))
        for copy in self.gather_copies():
            copy.start()

    def pair_start(self):
        for copy in self.gather_copies():
            copy.wait()
        for copy in self.pair_copies():
            copy.start()

    def pair_done(self):
        for copy in self.pair_copies():
            copy.wait()


def compute(s, chunk_windows=4):
    pair, group = head_masks()
    scale = np.float32(HD ** -0.5)
    CH = chunk_windows * WROWS
    nwin = 32

    def gather(src, dst):
        def row(r, _):
            y = dot(s.pm[...], src[r + SHIFT]).astype(BF)
            wr, a = r // WIN, r % WIN
            for c in range(8):
                dst[pl.ds(pl.multiple_of((wr * 8 + c) * WROWS + a * SLAB, SLAB), SLAB), :] = y[c * SLAB:(c + 1) * SLAB]
            return 0
        lax.fori_loop(0, 28, row, 0, unroll=2)

    halo_in(s)
    gather(s.x, s.z)
    gather(s.g, s.gz)

    key_row = lax.broadcasted_iota(jnp.int32, (WROWS, 256), 0)
    lane = lax.broadcasted_iota(jnp.int32, (WROWS, 256), 1)
    qa, ka = (lane % 128) // SLAB, key_row // SLAB
    empty = (key_row % SLAB) >= WIN * WLEV
    cut = jnp.logical_and((qa >= WIN - SHIFT) != (ka >= WIN - SHIFT), s.last)
    for j in range(HALF):
        tiles = []
        for g in range(2):
            strip = s.strip[j + HALF * g]
            rows = [strip[:, (6 - ak) * SLAB:(6 - ak) * SLAB + WROWS] for ak in range(WIN)]
            tile = jnp.concatenate(rows, 0)
            tiles.append(jnp.concatenate([tile, jnp.zeros((WROWS, 128 - WROWS), F32)], 1))
        full = jnp.where(empty, NEG, jnp.concatenate(tiles, 1))
        s.bias[0, j * WROWS:(j + 1) * WROWS] = full
        s.bias[1, j * WROWS:(j + 1) * WROWS] = jnp.where(cut, NEG, full)
    s.dbias[...] = jnp.zeros_like(s.dbias)
    s.acc[...] = jnp.zeros_like(s.acc)
    s.small[...] = jnp.zeros_like(s.small)

    def forward_window(w):
        rows = pl.ds(pl.multiple_of(w * WROWS, WROWS), WROWS)
        arows = pl.multiple_of(w * (HALF * WROWS), HALF * WROWS)
        q, k, v = s.p[rows, 0:C], s.p[rows, C:2 * C], s.p[rows, 2 * C:3 * C]
        scores = dot(stack_pairs(k, pair), stack_groups(q, group), NT)
        which = (w >= 24).astype(jnp.int32)
        vt = v.T
        lows = []
        for j in range(HALF):
            t = scores[j * WROWS:(j + 1) * WROWS] * scale + s.bias[which, j * WROWS:(j + 1) * WROWS]
            e = jnp.exp(t - jnp.max(t, 0, keepdims=True))
            att = e * (1.0 / jnp.sum(e, 0, keepdims=True))
            s.att[pl.ds(arows + j * WROWS, WROWS), :] = att
            lows.append(att.astype(BF))
        s.mixed[rows, :] = down_keys(vt, jnp.concatenate(lows, 0)).astype(BF)

    def phase_a(i, _):
        rows = pl.ds(pl.multiple_of(i * CH, CH), CH)
        x = s.z[rows, :].astype(F32)
        _, _, hidden1 = layer_norm(x, s.gains[0:1], s.shifts[0:1])
        s.p[rows, :] = (dot(hidden1, s.w_qkv[...]) + s.b_qkv[...]).astype(BF)

        def win(w, _):
            forward_window(i * chunk_windows + 2 * w)
            forward_window(i * chunk_windows + 2 * w + 1)
            return 0
        lax.fori_loop(0, chunk_windows // 2, win, 0)

        mixed = s.mixed[rows, :]
        resid = s.z[rows, :].astype(F32) + dot(mixed, s.w_proj[...])
        xhat2, istd2, hidden2 = layer_norm(resid, s.gains[1:2], s.shifts[1:2])
        act, slope = gelu_both(dot(hidden2, s.w_in[...]))
        act = act.astype(BF)
        out = (resid + dot(act, s.w_out[...])).astype(BF)
        gr = s.gz[rows, :]
        s.gz[rows, :] = out
        s.acc[:, W_OUT] += dot(gr, act, TN)
        gp = (dot(gr, s.w_out[...], NT) * slope).astype(BF)
        s.acc[:, W_IN] += dot(hidden2, gp, TN)
        gh = dot(gp, s.w_in[...], NT)
        s.small[1:2] += jnp.sum(gh * xhat2, 0, keepdims=True)
        s.small[3:4] += jnp.sum(gh, 0, keepdims=True)
        gres = gr.astype(F32) + norm_backward(gh, xhat2, istd2, s.gains[1:2])
        s.gres[rows, :] = gres
        low = gres.astype(BF)
        s.acc[:, W_PROJ] += dot(mixed, low, TN)
        s.mixed[rows, :] = dot(low, s.w_proj[...], NT).astype(BF)
        return 0

    lax.fori_loop(0, nwin // chunk_windows, phase_a, 0)

    def backward_window(w):
        rows = pl.ds(pl.multiple_of(w * WROWS, WROWS), WROWS)
        arows = pl.multiple_of(w * (HALF * WROWS), HALF * WROWS)
        q, k, v = s.p[rows, 0:C], s.p[rows, C:2 * C], s.p[rows, 2 * C:3 * C]
        gm2 = stack_groups(s.mixed[rows, :], group)
        ga = dot(stack_pairs(v, pair), gm2, NT)
        lows, dlows = [], []
        for j in range(HALF):
            att = s.att[pl.ds(arows + j * WROWS, WROWS), :]
            t = att * ga[j * WROWS:(j + 1) * WROWS]
            ds = t - att * jnp.sum(t, 0, keepdims=True)
            s.dbias[j * WROWS:(j + 1) * WROWS] += ds
            lows.append(att.astype(BF))
            dlows.append((ds * scale).astype(BF))
        low, dlow = jnp.concatenate(lows, 0), jnp.concatenate(dlows, 0)
        gv = pick_pairs(dot(low, gm2), pair).astype(BF)
        gk = pick_pairs(dot(dlow, stack_groups(q, group)), pair).astype(BF)
        gq = down_keys(k.T, dlow).astype(BF)
        s.p[rows, 0:C] = gq
        s.p[rows, C:2 * C] = gk
        s.p[rows, 2 * C:3 * C] = gv

    scatter(s, s.gz, s.res, 0)
    early = Exchange(s, EARLY, 0)
    early.core_start()

    def phase_b(i, _):
        rows = pl.ds(pl.multiple_of(i * CH, CH), CH)
        for at, step in ((1, early.lon_start), (3, early.lat_start), (5, early.gather_start), (7, early.pair_start)):
            pl.when(i == at)(step)

        def win(w, _):
            backward_window(i * chunk_windows + 2 * w)
            backward_window(i * chunk_windows + 2 * w + 1)
            return 0
        lax.fori_loop(0, chunk_windows // 2, win, 0)
        xhat, istd, hidden = layer_norm(s.z[rows, :].astype(F32), s.gains[0:1], s.shifts[0:1])
        gp = s.p[rows, :]
        s.acc[:, W_QKV] += dot(hidden, gp, TN)
        sums = jnp.sum(gp.astype(F32), 0, keepdims=True)
        for part in range(3):
            s.small[4 + part:5 + part] += sums[:, part * C:(part + 1) * C]
        gh = dot(gp, s.w_qkv[...], NT)
        s.small[0:1] += jnp.sum(gh * xhat, 0, keepdims=True)
        s.small[2:3] += jnp.sum(gh, 0, keepdims=True)
        s.z[rows, :] = (s.gres[rows, :] + norm_backward(gh, xhat, istd, s.gains[0:1])).astype(BF)
        return 0

    lax.fori_loop(0, nwin // chunk_windows, phase_b, 0)

    for h in range(HEADS):
        j, g = h % HALF, h // HALF
        total = None
        for ak in range(WIN):
            piece = s.dbias[j * WROWS + ak * SLAB:j * WROWS + (ak + 1) * SLAB, g * 128:g * 128 + WROWS]
            before = (6 - ak) * SLAB
            parts = []
            if before:
                parts.append(jnp.zeros((SLAB, before), F32))
            parts.append(piece)
            parts.append(jnp.zeros((SLAB, 256 - before - WROWS), F32))
            moved = jnp.concatenate(parts, 1)
            total = moved if total is None else total + moved
        for half in range(2):
            s.acc[half * 128 + h * SLAB:half * 128 + (h + 1) * SLAB, STRIP] = total[:, half * 128:(half + 1) * 128]

    late = Exchange(s, LATE, 1, small=True)
    late.core_start()
    scatter(s, s.z, s.ing, 1)
    late.lon_start()
    early.pair_done()
    late.lat_start()
    halo_out_done(s, s.res, 0)
    late.gather_start()
    halo_out_done(s, s.ing, 1)
    late.pair_start()
    late.pair_done()


class Refs:
    pass


T = 32 * WROWS
INS = ("x_in", "g_in", "pm", "strip", "gains", "shifts", "w_qkv", "b_qkv", "w_proj", "w_in", "w_out")
OUTS = {
    "res": ((28, 112, C), BF), "ing": ((28, 112, C), BF), "total": ((256, COLS), BF), "small_out": ((8, C), F32),
}
SCRATCH = {
    "x": ((31, 128, C), BF), "g": ((31, 128, C), BF),
    "z": ((T, C), BF), "gz": ((T, C), BF), "p": ((T, 3 * C), BF), "att": ((T * HALF, 256), F32), "mixed": ((T, C), BF),
    "gres": ((T, C), F32), "bias": ((2, HALF * WROWS, 256), F32), "dbias": ((HALF * WROWS, 256), F32),
    "acc": ((256, COLS), F32), "small": ((8, C), F32), "small_core": ((8, C), F32), "small_lon": ((8, 8, C), F32),
    "small_lat": ((8, 8, C), F32), "sent": ((256, COLS), BF), "land_core": ((128, COLS), BF), "part": ((128, COLS), BF),
    "land_lon": ((8, 16, COLS), BF), "land_lat": ((8, 16, COLS), BF),
    "side": ((2, 28, 16, C), BF), "foot": ((2, 3, 128, C), BF), "land_side": ((2, 28, 16, C), BF),
    "land_foot": ((2, 3, 112, C), BF),
}
SEMS = (2, 12, 12, 24, 24, 40, 40)


def kernel(*refs):
    s = Refs()
    names = INS + tuple(OUTS) + tuple(SCRATCH)
    for name, ref in zip(names, refs):
        setattr(s, name, ref)
    s.near_sem, h0, h1, a0, a1, b0, b1 = refs[len(names):]
    s.halo, s.sums = (h0, h1), ((a0, a1), (b0, b1))
    s.lat, s.lon = lax.axis_index("lat"), lax.axis_index("lon")
    s.last = s.lat == 7
    compute(s)


def fused(*args):
    vm = pl.BlockSpec(memory_space=pltpu.VMEM)
    return pl.pallas_call(
        kernel,
        out_shape=tuple(jax.ShapeDtypeStruct(*v) for v in OUTS.values()),
        in_specs=[pl.BlockSpec(memory_space=pl.ANY)] * 2 + [vm] * (len(INS) - 2),
        out_specs=[vm] * len(OUTS),
        scratch_shapes=[pltpu.VMEM(*v) for v in SCRATCH.values()] + [pltpu.SemaphoreType.DMA((n,)) for n in SEMS],
        compiler_params=pltpu.CompilerParams(
            vmem_limit_bytes=63 * 1024 * 1024, collective_id=0, has_side_effects=True
        ),
        name="windows",
    )(*args)


def local(tokens, out_grad, gains, shifts, w_qkv, b_qkv, w_proj, w_in, w_out, rel_bias):
    rows_n, cols_n, levels, channels = tokens.shape
    scale = float(rows_n * lax.axis_size("lat") * cols_n * lax.axis_size("lon") * levels) ** -0.5
    index = jnp.asarray(strip_map().reshape(-1))
    onehot = (index[:, None] == jnp.arange(NREL, dtype=jnp.int32)[None, :]).astype(F32)
    strip = lax.dot_general(rel_bias, onehot, NT, precision=lax.Precision.HIGHEST).reshape(HEADS, SLAB, 256)
    pm = jnp.asarray(placement(), BF)
    flat = (rows_n, cols_n * levels, channels)
    res, ing, total, small = fused(
        tokens.reshape(flat), out_grad.reshape(flat), pm, strip, gains, shifts, w_qkv, b_qkv[None], w_proj, w_in, w_out
    )
    total = total.astype(F32) * scale
    small = small * scale
    dstrip = total[:, STRIP].reshape(2, HEADS, SLAB, 128).transpose(1, 2, 0, 3).reshape(HEADS, -1)
    table = lax.dot_general(dstrip, onehot, NN, precision=lax.Precision.HIGHEST)
    return (
        res.reshape(tokens.shape), ing.reshape(tokens.shape), small[0:2], small[2:4], total[:, W_QKV],
        small[4:7].reshape(3 * C), total[:, W_PROJ], total[:, W_IN], total[:, W_OUT].T, table,
    )


def solution(mesh):
    big = P("lat", "lon", None, None)
    return jax.shard_map(
        local, mesh=mesh, in_specs=(big, big) + (P(),) * 8, out_specs=(big, big) + (P(),) * 8, check_vma=False
    )
```

```python
import functools

import jax
import jax.numpy as jnp
import numpy as np
from jax import lax
from jax.experimental import pallas as pl
from jax.experimental.pallas import tpu as pltpu
from jax.sharding import PartitionSpec as P

WIN = 7
LEV = 4
WLEV = 2
SHIFT = 3
EPS = 1e-05
NEG = -1e30
HEADS = 8
HD = 32
C = 256
FF = 1024
SLAB = 16
WROWS = WIN * SLAB
HALF = HEADS // 2
PAIR = 2 * 128
NREL = 507
BF = jnp.bfloat16
F32 = jnp.float32

NN = (((1,), (0,)), ((), ()))
NT = (((1,), (1,)), ((), ()))
TN = (((0,), (0,)), ((), ()))


def dot(a, b, dims=NN):
    return lax.dot_general(a, b, dims, preferred_element_type=F32)


def placement():
    matrix = np.zeros((128, 128), np.float32)
    for wc in range(4):
        for lw in range(2):
            for b in range(WIN):
                for l in range(WLEV):
                    row = (wc * 2 + lw) * SLAB + b * WLEV + l
                    matrix[row, (wc * WIN + SHIFT + b) * LEV + lw * WLEV + l] = 1.0
    return matrix


def strip_map():
    index = np.full((SLAB, 256), -1, np.int32)
    for bk in range(WIN):
        for lk in range(WLEV):
            for da in range(13):
                for bq in range(WIN):
                    for lq in range(WLEV):
                        index[bk * WLEV + lk, da * SLAB + bq * WLEV + lq] = (
                            (da * 13 + bq - bk + 6) * 3 + lq - lk + 1
                        )
    return index


def layer_norm(x, gain, shift):
    center = x - jnp.mean(x, -1, keepdims=True)
    istd = lax.rsqrt(jnp.mean(center * center, -1, keepdims=True) + EPS)
    xhat = center * istd
    return xhat, istd, (xhat * gain + shift).astype(BF)


def norm_backward(up, xhat, istd, gain):
    n = up * gain
    return istd * (n - jnp.mean(n, -1, keepdims=True) - xhat * jnp.mean(n * xhat, -1, keepdims=True))


def gelu_both(p):
    c0 = np.float32(np.sqrt(2.0 / np.pi))
    c1 = np.float32(0.044715 * np.sqrt(2.0 / np.pi))
    p2 = p * p
    t = jnp.tanh(p * (c0 + c1 * p2))
    h = 0.5 * p
    half = 0.5 + 0.5 * t
    act = p * half
    slope = half + h * (1.0 - t * t) * (c0 + (3.0 * c1) * p2)
    return act, slope


def head_masks():
    lane = lax.broadcasted_iota(jnp.int32, (1, C), 1) // HD
    pair = [((lane % HALF) == j) for j in range(HALF)]
    group = [((lane // HALF) == g) for g in range(2)]
    return pair, group


def stack_pairs(v, pair):
    return jnp.concatenate([v * m.astype(BF) for m in pair], 0)


def stack_groups(v, group):
    pad = jnp.zeros((128 - WROWS, C), BF)
    return jnp.concatenate([v * group[0].astype(BF), pad, v * group[1].astype(BF), pad], 0)


def pick_pairs(r, pair):
    out = r[3 * WROWS:4 * WROWS]
    for j in range(3):
        out = jnp.where(pair[j], r[j * WROWS:(j + 1) * WROWS], out)
    return out


def down_keys(vt, low):
    parts = [None] * HEADS
    for j in range(HALF):
        lhs = jnp.concatenate([vt[j * HD:(j + 1) * HD], vt[(j + HALF) * HD:(j + HALF + 1) * HD]], 0)
        out = dot(lhs, low[j * WROWS:(j + 1) * WROWS])
        parts[j] = out[:HD, :128]
        parts[j + HALF] = out[HD:, 128:]
    return jnp.concatenate(parts, 0).T[:WROWS]


FIRST, SECOND, LATE = (0, 1024), (1024, 2304), (2304, 3072)
W_IN, W_PROJ, W_QKV = slice(0, 1024), slice(2048, 2304), slice(2304, 3072)
COLS = 3072
LOG2E = np.float32(1.4426950408889634)
MESH = pl.DeviceIdType.MESH


def send(src, dst, sems, index, device):
    return pltpu.make_async_remote_copy(
        src_ref=src, dst_ref=dst, send_sem=sems[0].at[index], recv_sem=sems[1].at[index],
        device_id=device, device_id_type=MESH,
    )


def greet(s):
    barrier = pltpu.get_barrier_semaphore()
    peers = [((s.lat + d) % 8, s.lon) for d in range(1, 8)] + [(s.lat, (s.lon + d) % 16) for d in range(1, 16)]
    peers += [((s.lat + d) % 8, (s.lon + d) % 16) for d in (1, -1)]
    for peer in peers:
        pl.semaphore_signal(barrier, inc=1, device_id=peer, device_id_type=MESH)
    pl.semaphore_wait(barrier, len(peers))


def near_copies(s):
    return [
        pltpu.make_async_copy(src, dst.at[0:28, 0:28], s.near_sem.at[n])
        for n, (src, dst) in enumerate(((s.x_in, s.x), (s.g_in, s.g)))
    ]


def halo_in_copies(s):
    west, north = (s.lon + 15) % 16, (s.lat + 7) % 8
    far = []
    for n, (src, dst) in enumerate(((s.x_in, s.x), (s.g_in, s.g))):
        far.append(send(src.at[:, 0:4], dst.at[0:28, 28:32], s.halo, 3 * n, (s.lat, west)))
        far.append(send(src.at[0:SHIFT], dst.at[28:31, 0:28], s.halo, 3 * n + 1, (north, s.lon)))
        far.append(send(src.at[0:SHIFT, 0:4], dst.at[28:31, 28:32], s.halo, 3 * n + 2, (north, west)))
    return far


def halo_start(s):
    for copy in near_copies(s):
        copy.start()
    greet(s)
    for copy in halo_in_copies(s):
        copy.start()


def near_done(s):
    for copy in near_copies(s):
        copy.wait()


def halo_in_done(s):
    for copy in halo_in_copies(s):
        copy.wait()


def slab(wr, c, a):
    return pl.ds(pl.multiple_of((wr * 8 + c) * WROWS + a * SLAB, SLAB), SLAB)


def gather_own(s, src, dst):
    def row(r, _):
        y = dot(s.pm[0:96, 0:112], src[r + SHIFT, 0:28].reshape(112, C)).astype(BF)
        for c in range(6):
            dst[slab(r // WIN, c, r % WIN), :] = y[c * SLAB:(c + 1) * SLAB]
        return 0
    lax.fori_loop(0, 25, row, 0, unroll=5)


def gather_rest(s, src, dst):
    def row(r, _):
        y = dot(s.pm[96:128], src[r + SHIFT].reshape(128, C)).astype(BF)
        for c in range(2):
            dst[slab(r // WIN, 6 + c, r % WIN), :] = y[c * SLAB:(c + 1) * SLAB]
        return 0
    lax.fori_loop(0, 25, row, 0, unroll=5)
    for r in range(25, 28):
        y = dot(s.pm[...], src[r + SHIFT].reshape(128, C)).astype(BF)
        for c in range(8):
            dst[slab(r // WIN, c, r % WIN), :] = y[c * SLAB:(c + 1) * SLAB]


def halo_out_copies(s, n):
    east, south = (s.lon + 1) % 16, (s.lat + 1) % 8
    return [
        send(s.side.at[n, SHIFT:28], s.land_side.at[n, SHIFT:28], s.halo, 6 + 3 * n, (s.lat, east)),
        send(s.foot.at[n, :, 0:28], s.land_foot.at[n], s.halo, 7 + 3 * n, (south, s.lon)),
        send(s.foot.at[n, :, 28:32], s.land_side.at[n, 0:SHIFT], s.halo, 8 + 3 * n, (south, east)),
    ]


def grid_row(s, src, r, low, high):
    y = jnp.concatenate([src[slab(r // WIN, c, r % WIN), :] for c in range(low, high)], 0)
    return dot(s.pm[low * SLAB:high * SLAB], y, TN).astype(BF).reshape(32, LEV, C)


def scatter_foot(s, src, n):
    for r in range(25, 28):
        s.foot[n, r - 25] = grid_row(s, src, r, 0, 8)


def scatter_all(s, src, dst, n):
    scatter_foot(s, src, n)

    def row(r, _):
        y = grid_row(s, src, r, 0, 8)
        dst[r + SHIFT] = y[:28]
        s.side[n, r + SHIFT] = y[28:]
        return 0
    lax.fori_loop(0, 25, row, 0, unroll=5)
    for copy in halo_out_copies(s, n):
        copy.start()


def scatter_sent(s, src, dst, n):
    scatter_foot(s, src, n)

    def row(r, _):
        y = grid_row(s, src, r, 4, 8)
        dst[r + SHIFT] = y[:28]
        s.side[n, r + SHIFT] = y[28:]
        return 0
    lax.fori_loop(0, 25, row, 0, unroll=5)
    for copy in halo_out_copies(s, n):
        copy.start()


def scatter_own(s, src, dst):
    def row(r, _):
        y = grid_row(s, src, r, 0, 4)
        dst[r + SHIFT, 0:16] = y[:16]
        seam = dst[r + SHIFT, 16:20].reshape(16, C) + y[16:20].reshape(16, C)
        dst[r + SHIFT, 16:20] = seam.reshape(4, LEV, C)
        return 0
    lax.fori_loop(0, 25, row, 0, unroll=5)


def halo_out_done(s, dst, n):
    for copy in halo_out_copies(s, n):
        copy.wait()
    dst[0:SHIFT] = s.land_foot[n]

    def row(r, _):
        both = dst[r, 0:4].reshape(16, C) + s.land_side[n, r].reshape(16, C)
        dst[r, 0:4] = both.reshape(4, LEV, C)
        return 0
    lax.fori_loop(0, 28, row, 0, unroll=7)


def thirds(value):
    high = value.astype(BF)
    rest = value - high.astype(F32)
    mid = rest.astype(BF)
    return jnp.concatenate([v.astype(F32) for v in (high, mid, (rest - mid.astype(F32)))], 0).astype(BF)


def chosen(s, i):
    slots = lax.broadcasted_iota(jnp.int32, (512, 256), 0)
    return jnp.where(slots == s.index[i:i + 1, :], 1.0, 0.0).astype(BF)


def expand_table(s):
    s.rel[...] = jnp.zeros_like(s.rel)
    s.rel[:, 0:NREL] = s.rel_bias[...]
    table = thirds(s.rel[...])
    s.strip[...] = jnp.zeros_like(s.strip)
    for i in range(WIN * WLEV):
        out = dot(table, chosen(s, i))
        s.strip[i] = out[0:8] + out[8:16] + out[16:24]


def collect_table(s):
    for h in range(HEADS):
        j, g = h % HALF, h // HALF
        total = None
        for ak in range(WIN):
            piece = s.dbias[j * WROWS + ak * SLAB:j * WROWS + (ak + 1) * SLAB, g * 128:g * 128 + WROWS]
            before = (6 - ak) * SLAB
            parts = [jnp.zeros((SLAB, before), F32)] if before else []
            moved = jnp.concatenate(parts + [piece, jnp.zeros((SLAB, 256 - before - WROWS), F32)], 1)
            total = moved if total is None else total + moved
        s.dstrip[h] = total
    table = None
    for i in range(WIN * WLEV):
        part = dot(thirds(s.dstrip[:, i, :]), chosen(s, i), NT)
        table = part if table is None else table + part
    table = table[0:8] + table[8:16] + table[16:24]
    s.small[0:8] = table[:, 0:256]
    s.small[8:16] = table[:, 256:512]


def tail_lon_copies(s):
    mine, out = s.tail_lon.at[s.lon], []
    for d in range(1, 16):
        out.append(send(mine, mine, s.tails, d, (s.lat, (s.lon + d) % 16)))
    return out


def tail_lat_copies(s):
    mine, out = s.tail_lat.at[s.lat], []
    for d in range(1, 8):
        out.append(send(mine, mine, s.tails, 15 + d, ((s.lat + d) % 8, s.lon)))
    return out


def tail_lon_start(s):
    s.tail_lon[s.lon] = s.tail[...]
    for copy in tail_lon_copies(s):
        copy.start()


def tail_lat_start(s):
    for copy in tail_lon_copies(s):
        copy.wait()
    s.tail_lat[s.lat] = sum(s.tail_lon[i] for i in range(16))
    for copy in tail_lat_copies(s):
        copy.start()


def tail_done(s):
    for copy in tail_lat_copies(s):
        copy.wait()
    s.tail_out[...] = sum(s.tail_lat[i] for i in range(8))


class Exchange:
    def __init__(self, s, cols, number, small=False):
        self.s, self.cols, self.sems, self.small = s, slice(*cols), s.sums[number], small
        self.core, self.chip = s.lon % 2, s.lon // 2
        self.half = pl.ds(pl.multiple_of(self.core * 128, 128), 128)
        self.other = pl.ds(pl.multiple_of((1 - self.core) * 128, 128), 128)
        self.share = pl.ds(pl.multiple_of(self.core * 128 + self.chip * 16, 16), 16)
        self.twin = (s.lat, s.lon + 1 - 2 * self.core)

    def core_copies(self):
        s = self.s
        out = [send(s.sent.at[self.other, self.cols], s.land_core.at[:, self.cols], self.sems, 0, self.twin)]
        if self.small:
            out.append(send(s.small, s.small_core, self.sems, 24, self.twin))
        return out

    def lon_copies(self):
        s, out = self.s, []
        for d in range(1, 8):
            peer = (self.chip + d) % 8
            to = (s.lat, peer * 2 + self.core)
            rows = pl.ds(pl.multiple_of(peer * 16, 16), 16)
            out.append(send(s.part.at[rows, self.cols], s.land_lon.at[self.chip, :, self.cols], self.sems, d, to))
            if self.small:
                out.append(send(s.small_lon.at[self.chip], s.small_lon.at[self.chip], self.sems, 24 + d, to))
        return out

    def lat_copies(self):
        s, out = self.s, []
        for d in range(1, 8):
            to = ((s.lat + d) % 8, s.lon)
            mine = s.land_lat.at[s.lat, :, self.cols]
            out.append(send(mine, mine, self.sems, 8 + d, to))
            if self.small:
                out.append(send(s.small_lat.at[s.lat], s.small_lat.at[s.lat], self.sems, 32 + d, to))
        return out

    def gather_copies(self):
        s, out = self.s, []
        for d in range(1, 8):
            to = (s.lat, ((self.chip + d) % 8) * 2 + self.core)
            mine = s.total.at[self.share, self.cols]
            out.append(send(mine, mine, self.sems, 16 + d, to))
        return out

    def pair_copies(self):
        mine = self.s.total.at[self.half, self.cols]
        return [send(mine, mine, self.sems, 16, self.twin)]

    def core_start(self):
        s = self.s
        s.sent[self.other, self.cols] = s.acc[self.other, self.cols].astype(BF)
        for copy in self.core_copies():
            copy.start()

    def lon_start(self):
        s = self.s
        for copy in self.core_copies():
            copy.wait()
        both = s.acc[self.half, self.cols] + s.land_core[:, self.cols].astype(F32)
        s.acc[self.half, self.cols] = both
        s.part[:, self.cols] = both.astype(BF)
        if self.small:
            s.small_lon[self.chip] = s.small[...] + s.small_core[...]
        for copy in self.lon_copies():
            copy.start()

    def lat_start(self):
        s = self.s
        for copy in self.lon_copies():
            copy.wait()
        total = s.acc[self.share, self.cols]
        for d in range(1, 8):
            total += s.land_lon[(self.chip + d) % 8, :, self.cols].astype(F32)
        s.land_lat[s.lat, :, self.cols] = total.astype(BF)
        if self.small:
            s.small_lat[s.lat] = sum(s.small_lon[i] for i in range(8))
        for copy in self.lat_copies():
            copy.start()

    def gather_start(self):
        s = self.s
        for copy in self.lat_copies():
            copy.wait()
        total = s.land_lat[0, :, self.cols].astype(F32)
        for i in range(1, 8):
            total += s.land_lat[i, :, self.cols].astype(F32)
        s.total[self.share, self.cols] = total.astype(BF)
        if self.small:
            s.small_out[...] = sum(s.small_lat[i] for i in range(8))
        for copy in self.gather_copies():
            copy.start()

    def pair_start(self):
        for copy in self.gather_copies():
            copy.wait()
        for copy in self.pair_copies():
            copy.start()

    def pair_done(self):
        for copy in self.pair_copies():
            copy.wait()


def compute(s, chunk_windows=4):
    pair, group = head_masks()
    scale = np.float32(HD ** -0.5)
    CH = chunk_windows * WROWS
    nwin = 32

    halo_start(s)

    expand_table(s)
    key_row = lax.broadcasted_iota(jnp.int32, (WROWS, 256), 0)
    lane = lax.broadcasted_iota(jnp.int32, (WROWS, 256), 1)
    qa, ka = (lane % 128) // SLAB, key_row // SLAB
    empty = (key_row % SLAB) >= WIN * WLEV
    cut = jnp.logical_and((qa >= WIN - SHIFT) != (ka >= WIN - SHIFT), s.last)
    for j in range(HALF):
        tiles = []
        for g in range(2):
            strip = s.strip[:, j + HALF * g, :] * LOG2E
            rows = [strip[:, (6 - ak) * SLAB:(6 - ak) * SLAB + WROWS] for ak in range(WIN)]
            tile = jnp.concatenate(rows, 0)
            tiles.append(jnp.concatenate([tile, jnp.zeros((WROWS, 128 - WROWS), F32)], 1))
        full = jnp.where(empty, NEG, jnp.concatenate(tiles, 1))
        s.bias[0, j * WROWS:(j + 1) * WROWS] = full
        s.bias[1, j * WROWS:(j + 1) * WROWS] = jnp.where(cut, NEG, full)
    s.dbias[...] = jnp.zeros_like(s.dbias)
    s.tail[...] = jnp.zeros_like(s.tail)
    s.acc[...] = jnp.zeros_like(s.acc)
    s.small[...] = jnp.zeros_like(s.small)
    near_done(s)
    for src, dst in ((s.x, s.z), (s.g, s.gz)):
        gather_own(s, src, dst)

    def rest():
        halo_in_done(s)
        for src, dst in ((s.x, s.z), (s.g, s.gz)):
            gather_rest(s, src, dst)

    def forward_window(w):
        rows = pl.ds(pl.multiple_of(w * WROWS, WROWS), WROWS)
        arows = pl.multiple_of(w * (HALF * WROWS), HALF * WROWS)
        q, k, v = s.p[rows, 0:C], s.p[rows, C:2 * C], s.p[rows, 2 * C:3 * C]
        scores = dot(stack_pairs(k, pair), stack_groups(q, group), NT)
        which = (w >= 24).astype(jnp.int32)
        vt = v.T
        lows = []
        for j in range(HALF):
            t = scores[j * WROWS:(j + 1) * WROWS] * (scale * LOG2E) + s.bias[which, j * WROWS:(j + 1) * WROWS]
            e = jnp.exp2(t - jnp.max(t, 0, keepdims=True))
            att = e * (1.0 / jnp.sum(e, 0, keepdims=True))
            low = att.astype(BF)
            s.att[pl.ds(arows + j * WROWS, WROWS), :] = low
            lows.append(low)
        s.mixed[rows, :] = down_keys(vt, jnp.concatenate(lows, 0)).astype(BF)

    def phase_a(step, _):
        i = jnp.where(step < 3, 2 * step, jnp.where(step < 6, 2 * step - 5, step))
        pl.when(step == 3)(rest)
        rows = pl.ds(pl.multiple_of(i * CH, CH), CH)
        x = s.z[rows, :].astype(F32)
        _, _, hidden1 = layer_norm(x, s.gains[0:1], s.shifts[0:1])
        s.p[rows, :] = (dot(hidden1, s.w_qkv[...]) + s.b_qkv[...]).astype(BF)

        def win(w, _):
            for u in range(4):
                forward_window(i * chunk_windows + 4 * w + u)
            return 0
        lax.fori_loop(0, chunk_windows // 4, win, 0)

        mixed = s.mixed[rows, :]
        resid = s.z[rows, :].astype(F32) + dot(mixed, s.w_proj[...])
        xhat2, istd2, hidden2 = layer_norm(resid, s.gains[1:2], s.shifts[1:2])
        gr = s.gz[rows, :]
        gr_t, hid_t = gr.T, hidden2.T
        out, gh = resid, None
        for f in range(4):
            cols = slice(f * 256, f * 256 + 256)
            act, slope = gelu_both(dot(hidden2, s.w_in[:, cols]))
            act = act.astype(BF)
            out = out + dot(act, s.w_out[cols, :])
            s.acc[:, 1024 + f * 256:1280 + f * 256] += dot(gr_t, act)
            gp = (dot(gr, s.w_out[cols, :], NT) * slope).astype(BF)
            s.acc[:, cols] += dot(hid_t, gp)
            part = dot(gp, s.w_in[:, cols], NT)
            gh = part if gh is None else gh + part
        s.gz[rows, :] = out.astype(BF)
        s.small[19:20] += jnp.sum(gh * xhat2, 0, keepdims=True)
        s.small[20:21] += jnp.sum(gh, 0, keepdims=True)
        gres = gr.astype(F32) + norm_backward(gh, xhat2, istd2, s.gains[1:2])
        s.gres[rows, :] = gres
        low = gres.astype(BF)
        s.acc[:, W_PROJ] += dot(mixed, low, TN)
        s.mixed[rows, :] = dot(low, s.w_proj[...], NT).astype(BF)
        return 0

    lax.fori_loop(0, 8, phase_a, 0)
    for f in range(4):
        cols = slice(1024 + f * 256, 1280 + f * 256)
        s.acc[:, cols] = s.acc[:, cols].T
    first, second, late = Exchange(s, FIRST, 0), Exchange(s, SECOND, 1), Exchange(s, LATE, 2, small=True)
    first.core_start()
    second.core_start()
    scatter_all(s, s.gz, s.res, 0)

    def backward_window(w):
        rows = pl.ds(pl.multiple_of(w * WROWS, WROWS), WROWS)
        arows = pl.multiple_of(w * (HALF * WROWS), HALF * WROWS)
        q, k, v = s.p[rows, 0:C], s.p[rows, C:2 * C], s.p[rows, 2 * C:3 * C]
        gm2 = stack_groups(s.mixed[rows, :], group)
        ga = dot(stack_pairs(v, pair), gm2, NT)
        lows, dlows = [], []
        for j in range(HALF):
            low = s.att[pl.ds(arows + j * WROWS, WROWS), :]
            att = low.astype(F32)
            t = att * ga[j * WROWS:(j + 1) * WROWS]
            ds = t - att * jnp.sum(t, 0, keepdims=True)
            s.dbias[j * WROWS:(j + 1) * WROWS] += ds
            lows.append(low)
            dlows.append((ds * scale).astype(BF))
        low, dlow = jnp.concatenate(lows, 0), jnp.concatenate(dlows, 0)
        gv = pick_pairs(dot(low, gm2), pair).astype(BF)
        gk = pick_pairs(dot(dlow, stack_groups(q, group)), pair).astype(BF)
        gq = down_keys(k.T, dlow).astype(BF)
        s.p[rows, 0:C] = gq
        s.p[rows, C:2 * C] = gk
        s.p[rows, 2 * C:3 * C] = gv

    def phase_b(i, _):
        rows = pl.ds(pl.multiple_of(i * CH, CH), CH)
        steps = (
            first.lon_start, second.lon_start, first.lat_start, second.lat_start,
            first.gather_start, second.gather_start, first.pair_start,
        )
        for at, step in enumerate(steps):
            pl.when(i == at + 1)(step)

        def win(w, _):
            for u in range(4):
                backward_window(i * chunk_windows + 4 * w + u)
            return 0
        lax.fori_loop(0, chunk_windows // 4, win, 0)
        _, _, hidden = layer_norm(s.z[rows, :].astype(F32), s.gains[0:1], s.shifts[0:1])
        gp = s.p[rows, :]
        s.acc[:, W_QKV] += dot(hidden, gp, TN)
        sums = jnp.sum(gp.astype(F32), 0, keepdims=True)
        for part in range(3):
            s.small[16 + part:17 + part] += sums[:, part * C:(part + 1) * C]
        return 0

    lax.fori_loop(0, 8, phase_b, 0)
    collect_table(s)
    late.core_start()
    halo_out_done(s, s.res, 0)

    def phase_c(step, _):
        i = jnp.where(step < 2, 7 - step, jnp.where(step < 5, 9 - 2 * step, 14 - 2 * step))
        for at, action in (
            (2, late.lon_start), (3, second.pair_start), (5, lambda: scatter_sent(s, s.z, s.ing, 1)), (6, late.lat_start),
        ):
            pl.when(step == at)(action)
        rows = pl.ds(pl.multiple_of(i * CH, CH), CH)
        xhat, istd, _ = layer_norm(s.z[rows, :].astype(F32), s.gains[0:1], s.shifts[0:1])
        gh = dot(s.p[rows, :], s.w_qkv[...], NT)
        s.tail[0:1] += jnp.sum(gh * xhat, 0, keepdims=True)
        s.tail[1:2] += jnp.sum(gh, 0, keepdims=True)
        s.z[rows, :] = (s.gres[rows, :] + norm_backward(gh, xhat, istd, s.gains[0:1])).astype(BF)
        return 0

    lax.fori_loop(0, 8, phase_c, 0)
    tail_lon_start(s)
    scatter_own(s, s.z, s.ing)
    late.gather_start()
    tail_lat_start(s)
    first.pair_done()
    second.pair_done()
    s.o_in[...] = s.total[:, W_IN]
    for f in range(4):
        s.o_out[f * 256:(f + 1) * 256] = s.total[:, 1024 + f * 256:1280 + f * 256]
    s.o_proj[...] = s.total[:, W_PROJ]
    halo_out_done(s, s.ing, 1)
    late.pair_start()
    tail_done(s)
    late.pair_done()
    s.o_qkv[...] = s.total[:, W_QKV]


class Refs:
    pass


T = 32 * WROWS
GRID = (LEV, C)
INS = ("x_in", "g_in", "pm", "index", "gains", "shifts", "w_qkv", "b_qkv", "w_proj", "w_in", "w_out", "rel_bias")
OUTS = {
    "res": ((28, 28) + GRID, BF), "ing": ((28, 28) + GRID, BF), "o_in": ((C, FF), BF), "o_out": ((FF, C), BF),
    "o_qkv": ((C, 3 * C), BF), "o_proj": ((C, C), BF), "small_out": ((24, C), F32), "tail_out": ((8, C), F32),
}
SCRATCH = {
    "x": ((31, 32) + GRID, BF), "g": ((31, 32) + GRID, BF),
    "z": ((T, C), BF), "gz": ((T, C), BF), "p": ((T, 3 * C), BF), "att": ((T * HALF, 256), BF), "mixed": ((T, C), BF),
    "gres": ((T, C), F32), "bias": ((2, HALF * WROWS, 256), F32), "dbias": ((HALF * WROWS, 256), F32),
    "rel": ((8, 512), F32), "strip": ((SLAB, 8, 256), F32), "dstrip": ((8, SLAB, 256), F32),
    "acc": ((256, COLS), F32), "small": ((24, C), F32), "small_core": ((24, C), F32), "small_lon": ((8, 24, C), F32),
    "small_lat": ((8, 24, C), F32), "sent": ((256, COLS), BF), "land_core": ((128, COLS), BF), "part": ((128, COLS), BF),
    "land_lon": ((8, 16, COLS), BF), "land_lat": ((8, 16, COLS), BF), "total": ((256, COLS), BF),
    "side": ((2, 28, 4) + GRID, BF), "foot": ((2, 3, 32) + GRID, BF), "land_side": ((2, 28, 4) + GRID, BF),
    "land_foot": ((2, 3, 28) + GRID, BF),
    "tail": ((8, C), F32), "tail_lon": ((16, 8, C), F32), "tail_lat": ((8, 8, C), F32),
}
SEMS = (2, 12, 12, 24, 24, 24, 24, 40, 40, 23, 23)


def kernel(*refs):
    s = Refs()
    names = INS + tuple(OUTS) + tuple(SCRATCH)
    for name, ref in zip(names, refs):
        setattr(s, name, ref)
    sems = refs[len(names):]
    s.near_sem, s.halo, s.tails = sems[0], sems[1:3], sems[9:11]
    s.sums = (sems[3:5], sems[5:7], sems[7:9])
    s.lat, s.lon = lax.axis_index("lat"), lax.axis_index("lon")
    s.last = s.lat == 7
    compute(s)


def fused(*args):
    vm = pl.BlockSpec(memory_space=pltpu.VMEM)
    return pl.pallas_call(
        kernel,
        out_shape=tuple(jax.ShapeDtypeStruct(*v) for v in OUTS.values()),
        in_specs=[pl.BlockSpec(memory_space=pl.ANY)] * 2 + [vm] * (len(INS) - 2),
        out_specs=[vm] * len(OUTS),
        scratch_shapes=[pltpu.VMEM(*v) for v in SCRATCH.values()] + [pltpu.SemaphoreType.DMA((n,)) for n in SEMS],
        compiler_params=pltpu.CompilerParams(
            vmem_limit_bytes=63 * 1024 * 1024, collective_id=0, has_side_effects=True
        ),
        name="windows",
    )(*args)


def local(tokens, out_grad, gains, shifts, w_qkv, b_qkv, w_proj, w_in, w_out, rel_bias):
    rows_n, cols_n, levels, channels = tokens.shape
    scale = float(rows_n * lax.axis_size("lat") * cols_n * lax.axis_size("lon") * levels) ** -0.5
    res, ing, o_in, o_out, o_qkv, o_proj, small, tail = fused(
        tokens, out_grad, jnp.asarray(placement(), BF), jnp.asarray(strip_map()), gains, shifts, w_qkv, b_qkv[None],
        w_proj, w_in, w_out, rel_bias,
    )
    def scaled(value):
        return value.astype(F32) * scale
    table = jnp.concatenate([small[0:8], small[8:16]], 1)[:, :NREL]
    return (
        res, ing, scaled(jnp.stack([tail[0], small[19]])), scaled(jnp.stack([tail[1], small[20]])), scaled(o_qkv),
        scaled(small[16:19].reshape(3 * C)), scaled(o_proj), scaled(o_in), scaled(o_out), scaled(table),
    )


def solution(mesh):
    big = P("lat", "lon", None, None)
    return jax.shard_map(
        local, mesh=mesh, in_specs=(big, big) + (P(),) * 8, out_specs=(big, big) + (P(),) * 8, check_vma=False
    )
```

```python
import functools

import jax
import jax.numpy as jnp
import numpy as np
from jax import lax
from jax.experimental import pallas as pl
from jax.experimental.pallas import tpu as pltpu
from jax.sharding import PartitionSpec as P

WIN = 7
LEV = 4
WLEV = 2
SHIFT = 3
EPS = 1e-05
NEG = -1e30
HEADS = 8
HD = 32
C = 256
FF = 1024
SLAB = 16
WROWS = WIN * SLAB
HALF = HEADS // 2
PAIR = 2 * 128
NREL = 507
BF = jnp.bfloat16
F32 = jnp.float32

NN = (((1,), (0,)), ((), ()))
NT = (((1,), (1,)), ((), ()))
TN = (((0,), (0,)), ((), ()))


def dot(a, b, dims=NN):
    return lax.dot_general(a, b, dims, preferred_element_type=F32)


def placement():
    matrix = np.zeros((128, 128), np.float32)
    for wc in range(4):
        for lw in range(2):
            for b in range(WIN):
                for l in range(WLEV):
                    row = (wc * 2 + lw) * SLAB + b * WLEV + l
                    matrix[row, (wc * WIN + SHIFT + b) * LEV + lw * WLEV + l] = 1.0
    return matrix


def strip_map():
    index = np.full((SLAB, 256), -1, np.int32)
    for bk in range(WIN):
        for lk in range(WLEV):
            for da in range(13):
                for bq in range(WIN):
                    for lq in range(WLEV):
                        index[bk * WLEV + lk, da * SLAB + bq * WLEV + lq] = (
                            (da * 13 + bq - bk + 6) * 3 + lq - lk + 1
                        )
    return index


def layer_norm(x, gain, shift):
    center = x - jnp.mean(x, -1, keepdims=True)
    istd = lax.rsqrt(jnp.mean(center * center, -1, keepdims=True) + EPS)
    xhat = center * istd
    return xhat, istd, (xhat * gain + shift).astype(BF)


def norm_backward(up, xhat, istd, gain):
    n = up * gain
    return istd * (n - jnp.mean(n, -1, keepdims=True) - xhat * jnp.mean(n * xhat, -1, keepdims=True))


def gelu_both(p):
    c0 = np.float32(np.sqrt(2.0 / np.pi))
    c1 = np.float32(0.044715 * np.sqrt(2.0 / np.pi))
    p2 = p * p
    t = jnp.tanh(p * (c0 + c1 * p2))
    half = 0.5 + 0.5 * t
    act = p * half
    slope = half + act * (1.0 - half) * ((2.0 * c0) + (6.0 * c1) * p2)
    return act, slope


def head_masks():
    lane = lax.broadcasted_iota(jnp.int32, (1, C), 1) // HD
    pair = [((lane % HALF) == j) for j in range(HALF)]
    group = [((lane // HALF) == g) for g in range(2)]
    return pair, group


def stack_pairs(v, pair):
    return jnp.concatenate([v * m.astype(BF) for m in pair], 0)


def stack_groups(v, group):
    pad = jnp.zeros((128 - WROWS, C), BF)
    return jnp.concatenate([v * group[0].astype(BF), pad, v * group[1].astype(BF), pad], 0)


def pick_pairs(r, pair):
    out = r[3 * WROWS:4 * WROWS]
    for j in range(3):
        out = jnp.where(pair[j], r[j * WROWS:(j + 1) * WROWS], out)
    return out


def down_keys(vt, low):
    parts = [None] * HEADS
    for j in range(HALF):
        lhs = jnp.concatenate([vt[j * HD:(j + 1) * HD], vt[(j + HALF) * HD:(j + HALF + 1) * HD]], 0)
        out = dot(lhs, low[j * WROWS:(j + 1) * WROWS])
        parts[j] = out[:HD, :128]
        parts[j + HALF] = out[HD:, 128:]
    return jnp.concatenate(parts, 0).T[:WROWS]


FIRST, LATE = (0, 2304), (2304, 3200)
W_IN, W_PROJ, W_QKV, SHORT = slice(0, 1024), slice(2048, 2304), slice(2304, 3072), slice(3072, 3200)
COLS = 3200
LOG2E = np.float32(1.4426950408889634)
MESH = pl.DeviceIdType.MESH


def send(src, dst, sems, index, device):
    return pltpu.make_async_remote_copy(
        src_ref=src, dst_ref=dst, send_sem=sems[0].at[index], recv_sem=sems[1].at[index],
        device_id=device, device_id_type=MESH,
    )


def greet(s):
    barrier = pltpu.get_barrier_semaphore()
    peers = [((s.lat + d) % 8, s.lon) for d in range(1, 8)] + [(s.lat, (s.lon + d) % 16) for d in range(1, 16)]
    peers += [((s.lat + d) % 8, (s.lon + d) % 16) for d in (1, -1)]
    for peer in peers:
        pl.semaphore_signal(barrier, inc=1, device_id=peer, device_id_type=MESH)
    pl.semaphore_wait(barrier, len(peers))


def near_copies(s):
    return [
        pltpu.make_async_copy(src, dst.at[0:28, 0:28], s.near_sem.at[n])
        for n, (src, dst) in enumerate(((s.x_in, s.x), (s.g_in, s.g)))
    ]


def halo_in_copies(s):
    west, north = (s.lon + 15) % 16, (s.lat + 7) % 8
    far = []
    for n, (src, dst) in enumerate(((s.x_in, s.x), (s.g_in, s.g))):
        far.append(send(src.at[:, 0:4], dst.at[0:28, 28:32], s.halo, 3 * n, (s.lat, west)))
        far.append(send(src.at[0:SHIFT], dst.at[28:31, 0:28], s.halo, 3 * n + 1, (north, s.lon)))
        far.append(send(src.at[0:SHIFT, 0:4], dst.at[28:31, 28:32], s.halo, 3 * n + 2, (north, west)))
    return far


def halo_start(s):
    for copy in near_copies(s):
        copy.start()
    greet(s)
    for copy in halo_in_copies(s):
        copy.start()


def near_done(s):
    for copy in near_copies(s):
        copy.wait()


def halo_in_done(s):
    for copy in halo_in_copies(s):
        copy.wait()


def slab(r, c):
    wr = r // WIN
    slot = jnp.where(wr < 3, wr * 6 + c if c < 6 else 12 + wr * 2 + c, 24 + c)
    return pl.ds(pl.multiple_of(slot * WROWS + (r % WIN) * SLAB, SLAB), SLAB)


def gather_own(s, src, dst):
    def row(r, _):
        y = dot(s.pm[0:96, 0:112], src[r + SHIFT, 0:28].reshape(112, C)).astype(BF)
        for c in range(6):
            dst[slab(r, c), :] = y[c * SLAB:(c + 1) * SLAB]
        return 0
    lax.fori_loop(0, 25, row, 0, unroll=5)


def gather_rest(s, src, dst):
    def row(r, _):
        y = dot(s.pm[96:128], src[r + SHIFT].reshape(128, C)).astype(BF)
        for c in range(2):
            dst[slab(r, 6 + c), :] = y[c * SLAB:(c + 1) * SLAB]
        return 0
    lax.fori_loop(0, 25, row, 0, unroll=5)
    for r in range(25, 28):
        y = dot(s.pm[...], src[r + SHIFT].reshape(128, C)).astype(BF)
        for c in range(8):
            dst[slab(r, c), :] = y[c * SLAB:(c + 1) * SLAB]


def halo_out_copies(s, n):
    east, south = (s.lon + 1) % 16, (s.lat + 1) % 8
    return [
        send(s.side.at[n, SHIFT:28], s.land_side.at[n, SHIFT:28], s.halo, 6 + 3 * n, (s.lat, east)),
        send(s.foot.at[n, :, 0:28], s.land_foot.at[n], s.halo, 7 + 3 * n, (south, s.lon)),
        send(s.foot.at[n, :, 28:32], s.land_side.at[n, 0:SHIFT], s.halo, 8 + 3 * n, (south, east)),
    ]


def grid_row(s, src, r, low, high):
    y = jnp.concatenate([src[slab(r, c), :] for c in range(low, high)], 0)
    return dot(s.pm[low * SLAB:high * SLAB], y, TN).astype(BF).reshape(32, LEV, C)


def scatter_foot(s, src, n):
    for r in range(25, 28):
        s.foot[n, r - 25] = grid_row(s, src, r, 0, 8)


def scatter_all(s, src, dst, n):
    scatter_foot(s, src, n)

    def row(r, _):
        y = grid_row(s, src, r, 0, 8)
        dst[r + SHIFT] = y[:28]
        s.side[n, r + SHIFT] = y[28:]
        return 0
    lax.fori_loop(0, 25, row, 0, unroll=5)
    for copy in halo_out_copies(s, n):
        copy.start()


def scatter_sent(s, src, dst, n):
    scatter_foot(s, src, n)

    def row(r, _):
        y = grid_row(s, src, r, 6, 8)
        dst[r + SHIFT, 24:28] = y[24:28]
        s.side[n, r + SHIFT] = y[28:]
        return 0
    lax.fori_loop(0, 25, row, 0, unroll=5)
    for copy in halo_out_copies(s, n):
        copy.start()


def scatter_own(s, src, dst):
    def row(r, _):
        dst[r + SHIFT, 0:24] = grid_row(s, src, r, 0, 6)[0:24]
        return 0
    lax.fori_loop(0, 25, row, 0, unroll=5)


def halo_out_done(s, dst, n):
    for copy in halo_out_copies(s, n):
        copy.wait()
    dst[0:SHIFT] = s.land_foot[n]

    def row(r, _):
        both = dst[r, 0:4].reshape(16, C) + s.land_side[n, r].reshape(16, C)
        dst[r, 0:4] = both.reshape(4, LEV, C)
        return 0
    lax.fori_loop(0, 28, row, 0, unroll=7)


def thirds(value):
    high = value.astype(BF)
    rest = value - high.astype(F32)
    mid = rest.astype(BF)
    return jnp.concatenate([v.astype(F32) for v in (high, mid, (rest - mid.astype(F32)))], 0).astype(BF)


def chosen(s, i):
    slots = lax.broadcasted_iota(jnp.int32, (512, 256), 0)
    return jnp.where(slots == s.index[i:i + 1, :], 1.0, 0.0).astype(BF)


def expand_table(s):
    s.rel[...] = jnp.zeros_like(s.rel)
    s.rel[:, 0:NREL] = s.rel_bias[...]
    table = thirds(s.rel[...])
    s.strip[...] = jnp.zeros_like(s.strip)
    for i in range(WIN * WLEV):
        out = dot(table, chosen(s, i))
        s.strip[i] = out[0:8] + out[8:16] + out[16:24]


def collect_table(s):
    for h in range(HEADS):
        j, g = h % HALF, h // HALF
        total = None
        for ak in range(WIN):
            piece = s.dbias[j * WROWS + ak * SLAB:j * WROWS + (ak + 1) * SLAB, g * 128:g * 128 + WROWS]
            before = (6 - ak) * SLAB
            parts = [jnp.zeros((SLAB, before), F32)] if before else []
            moved = jnp.concatenate(parts + [piece, jnp.zeros((SLAB, 256 - before - WROWS), F32)], 1)
            total = moved if total is None else total + moved
        s.dstrip[h] = total
    table = None
    for i in range(WIN * WLEV):
        part = dot(thirds(s.dstrip[:, i, :]), chosen(s, i), NT)
        table = part if table is None else table + part
    table = table[0:8] + table[8:16] + table[16:24]
    s.small[0:8] = table[:, 0:256]
    s.small[8:16] = table[:, 256:512]
    s.acc[:, SHORT] = jnp.zeros((C, 128), F32)
    s.acc[0:32, SHORT] = s.small[:, 0:128]
    s.acc[32:64, SHORT] = s.small[:, 128:256]


def tail_lon_copies(s):
    mine, out = s.tail_lon.at[s.lon], []
    for d in range(1, 16):
        out.append(send(mine, mine, s.tails, d, (s.lat, (s.lon + d) % 16)))
    return out


def tail_lat_copies(s):
    mine, out = s.tail_lat.at[s.lat], []
    for d in range(1, 8):
        out.append(send(mine, mine, s.tails, 15 + d, ((s.lat + d) % 8, s.lon)))
    return out


def tail_lon_start(s):
    s.tail_lon[s.lon] = s.tail[...]
    for copy in tail_lon_copies(s):
        copy.start()


def tail_lat_start(s):
    for copy in tail_lon_copies(s):
        copy.wait()
    s.tail_lat[s.lat] = sum(s.tail_lon[i] for i in range(16))
    for copy in tail_lat_copies(s):
        copy.start()


def tail_done(s):
    for copy in tail_lat_copies(s):
        copy.wait()
    return sum(s.tail_lat[i] for i in range(8))


class Exchange:
    def __init__(self, s, cols, number):
        self.s, self.cols, self.sems = s, slice(*cols), s.sums[number]
        self.core, self.chip = s.lon % 2, s.lon // 2
        self.half = pl.ds(pl.multiple_of(self.core * 128, 128), 128)
        self.other = pl.ds(pl.multiple_of((1 - self.core) * 128, 128), 128)
        self.share = pl.ds(pl.multiple_of(self.core * 128 + self.chip * 16, 16), 16)
        self.twin = (s.lat, s.lon + 1 - 2 * self.core)

    def core_copies(self):
        s = self.s
        out = [send(s.sent.at[self.other, self.cols], s.land_core.at[:, self.cols], self.sems, 0, self.twin)]
        return out

    def lon_copies(self):
        s, out = self.s, []
        for d in range(1, 8):
            peer = (self.chip + d) % 8
            to = (s.lat, peer * 2 + self.core)
            rows = pl.ds(pl.multiple_of(peer * 16, 16), 16)
            out.append(send(s.part.at[rows, self.cols], s.land_lon.at[self.chip, :, self.cols], self.sems, d, to))
        return out

    def lat_copies(self):
        s, out = self.s, []
        for d in range(1, 8):
            to = ((s.lat + d) % 8, s.lon)
            mine = s.land_lat.at[s.lat, :, self.cols]
            out.append(send(mine, mine, self.sems, 8 + d, to))
        return out

    def gather_copies(self):
        s, out = self.s, []
        for d in range(1, 8):
            to = (s.lat, ((self.chip + d) % 8) * 2 + self.core)
            mine = s.total.at[self.share, self.cols]
            out.append(send(mine, mine, self.sems, 16 + d, to))
        return out

    def pair_copies(self):
        mine = self.s.total.at[self.half, self.cols]
        return [send(mine, mine, self.sems, 16, self.twin)]

    def core_start(self):
        s = self.s
        s.sent[self.other, self.cols] = s.acc[self.other, self.cols].astype(BF)
        for copy in self.core_copies():
            copy.start()

    def lon_start(self):
        s = self.s
        for copy in self.core_copies():
            copy.wait()
        both = s.acc[self.half, self.cols] + s.land_core[:, self.cols].astype(F32)
        s.acc[self.half, self.cols] = both
        s.part[:, self.cols] = both.astype(BF)
        for copy in self.lon_copies():
            copy.start()

    def lat_start(self):
        s = self.s
        for copy in self.lon_copies():
            copy.wait()
        total = s.acc[self.share, self.cols]
        for d in range(1, 8):
            total += s.land_lon[(self.chip + d) % 8, :, self.cols].astype(F32)
        s.land_lat[s.lat, :, self.cols] = total.astype(BF)
        for copy in self.lat_copies():
            copy.start()

    def gather_start(self):
        s = self.s
        for copy in self.lat_copies():
            copy.wait()
        total = s.land_lat[0, :, self.cols].astype(F32)
        for i in range(1, 8):
            total += s.land_lat[i, :, self.cols].astype(F32)
        s.total[self.share, self.cols] = total.astype(BF)
        for copy in self.gather_copies():
            copy.start()

    def pair_start(self):
        for copy in self.gather_copies():
            copy.wait()
        for copy in self.pair_copies():
            copy.start()

    def pair_done(self):
        for copy in self.pair_copies():
            copy.wait()


def compute(s, chunk_windows=8):
    pair, group = head_masks()
    scale = np.float32(HD ** -0.5)
    CH = chunk_windows * WROWS
    nwin = 32

    halo_start(s)

    expand_table(s)
    key_row = lax.broadcasted_iota(jnp.int32, (WROWS, 256), 0)
    lane = lax.broadcasted_iota(jnp.int32, (WROWS, 256), 1)
    qa, ka = (lane % 128) // SLAB, key_row // SLAB
    empty = (key_row % SLAB) >= WIN * WLEV
    cut = jnp.logical_and((qa >= WIN - SHIFT) != (ka >= WIN - SHIFT), s.last)
    for j in range(HALF):
        tiles = []
        for g in range(2):
            strip = s.strip[:, j + HALF * g, :] * LOG2E
            rows = [strip[:, (6 - ak) * SLAB:(6 - ak) * SLAB + WROWS] for ak in range(WIN)]
            tile = jnp.concatenate(rows, 0)
            tiles.append(jnp.concatenate([tile, jnp.zeros((WROWS, 128 - WROWS), F32)], 1))
        full = jnp.where(empty, NEG, jnp.concatenate(tiles, 1))
        s.bias[0, j * WROWS:(j + 1) * WROWS] = full
        s.bias[1, j * WROWS:(j + 1) * WROWS] = jnp.where(cut, NEG, full)
    s.dbias[...] = jnp.zeros_like(s.dbias)
    s.tail[...] = jnp.zeros_like(s.tail)
    s.acc[...] = jnp.zeros_like(s.acc)
    s.small[...] = jnp.zeros_like(s.small)
    near_done(s)
    for src, dst in ((s.x, s.z), (s.g, s.gz)):
        gather_own(s, src, dst)

    def rest():
        halo_in_done(s)
        for src, dst in ((s.x, s.z), (s.g, s.gz)):
            gather_rest(s, src, dst)

    def forward_window(w):
        rows = pl.ds(pl.multiple_of(w * WROWS, WROWS), WROWS)
        arows = pl.multiple_of(w * (HALF * WROWS), HALF * WROWS)
        q, k, v = s.p[rows, 0:C], s.p[rows, C:2 * C], s.p[rows, 2 * C:3 * C]
        scores = dot(stack_pairs(k, pair), stack_groups(q, group), NT)
        which = (w >= 24).astype(jnp.int32)
        vt = v.T
        lows = []
        for j in range(HALF):
            t = scores[j * WROWS:(j + 1) * WROWS] * (scale * LOG2E) + s.bias[which, j * WROWS:(j + 1) * WROWS]
            e = jnp.exp2(t - jnp.max(t, 0, keepdims=True))
            att = e * (1.0 / jnp.sum(e, 0, keepdims=True))
            low = att.astype(BF)
            s.att[pl.ds(arows + j * WROWS, WROWS), :] = low
            lows.append(low)
        s.mixed[rows, :] = down_keys(vt, jnp.concatenate(lows, 0)).astype(BF)

    def phase_a(step, _):
        i = step
        pl.when(step == 2)(rest)
        rows = pl.ds(pl.multiple_of(i * CH, CH), CH)
        x = s.z[rows, :].astype(F32)
        _, _, hidden1 = layer_norm(x, s.gains[0:1], s.shifts[0:1])
        s.p[rows, :] = (dot(hidden1, s.w_qkv[...]) + s.b_qkv[...]).astype(BF)

        def win(w, _):
            for u in range(4):
                forward_window(i * chunk_windows + 4 * w + u)
            return 0
        lax.fori_loop(0, chunk_windows // 4, win, 0)

        mixed = s.mixed[rows, :]
        resid = s.z[rows, :].astype(F32) + dot(mixed, s.w_proj[...])
        xhat2, istd2, hidden2 = layer_norm(resid, s.gains[1:2], s.shifts[1:2])
        gr = s.gz[rows, :]
        gr_t, hid_t = gr.T, hidden2.T
        out, gh = resid, None
        for f in range(4):
            cols = slice(f * 256, f * 256 + 256)
            act, slope = gelu_both(dot(hidden2, s.w_in[:, cols]))
            act = act.astype(BF)
            out = out + dot(act, s.w_out[cols, :])
            s.acc[:, 1024 + f * 256:1280 + f * 256] += dot(gr_t, act)
            gp = (dot(gr, s.w_out[cols, :], NT) * slope).astype(BF)
            s.acc[:, cols] += dot(hid_t, gp)
            part = dot(gp, s.w_in[:, cols], NT)
            gh = part if gh is None else gh + part
        s.gz[rows, :] = out.astype(BF)
        s.small[19:20] += jnp.sum(gh * xhat2, 0, keepdims=True)
        s.small[20:21] += jnp.sum(gh, 0, keepdims=True)
        gres = gr.astype(F32) + norm_backward(gh, xhat2, istd2, s.gains[1:2])
        s.gres[rows, :] = gres
        low = gres.astype(BF)
        s.acc[:, W_PROJ] += dot(mixed, low, TN)
        s.mixed[rows, :] = dot(low, s.w_proj[...], NT).astype(BF)
        return 0

    lax.fori_loop(0, 4, phase_a, 0)
    for f in range(4):
        cols = slice(1024 + f * 256, 1280 + f * 256)
        s.acc[:, cols] = s.acc[:, cols].T
    first, late = Exchange(s, FIRST, 0), Direct(s, LATE, 2)
    first.core_start()
    scatter_all(s, s.gz, s.res, 0)

    def backward_window(w):
        rows = pl.ds(pl.multiple_of(w * WROWS, WROWS), WROWS)
        arows = pl.multiple_of(w * (HALF * WROWS), HALF * WROWS)
        q, k, v = s.p[rows, 0:C], s.p[rows, C:2 * C], s.p[rows, 2 * C:3 * C]
        gm2 = stack_groups(s.mixed[rows, :], group)
        ga = dot(stack_pairs(v, pair), gm2, NT)
        lows, dlows = [], []
        for j in range(HALF):
            low = s.att[pl.ds(arows + j * WROWS, WROWS), :]
            att = low.astype(F32)
            t = att * ga[j * WROWS:(j + 1) * WROWS]
            ds = t - att * jnp.sum(t, 0, keepdims=True)
            s.dbias[j * WROWS:(j + 1) * WROWS] += ds
            lows.append(low)
            dlows.append((ds * scale).astype(BF))
        low, dlow = jnp.concatenate(lows, 0), jnp.concatenate(dlows, 0)
        gv = pick_pairs(dot(low, gm2), pair).astype(BF)
        gk = pick_pairs(dot(dlow, stack_groups(q, group)), pair).astype(BF)
        gq = down_keys(k.T, dlow).astype(BF)
        s.p[rows, 0:C] = gq
        s.p[rows, C:2 * C] = gk
        s.p[rows, 2 * C:3 * C] = gv

    def phase_b(i, _):
        rows = pl.ds(pl.multiple_of(i * CH, CH), CH)
        for at, step in ((1, first.lon_start), (2, first.lat_start), (3, first.gather_start)):
            pl.when(i == at)(step)

        def win(w, _):
            for u in range(4):
                backward_window(i * chunk_windows + 4 * w + u)
            return 0
        lax.fori_loop(0, chunk_windows // 4, win, 0)
        _, _, hidden = layer_norm(s.z[rows, :].astype(F32), s.gains[0:1], s.shifts[0:1])
        gp = s.p[rows, :]
        s.acc[:, W_QKV] += dot(hidden, gp, TN)
        sums = jnp.sum(gp.astype(F32), 0, keepdims=True)
        for part in range(3):
            s.small[16 + part:17 + part] += sums[:, part * C:(part + 1) * C]
        return 0

    lax.fori_loop(0, 4, phase_b, 0)
    collect_table(s)
    late.lon_start()
    halo_out_done(s, s.res, 0)

    def phase_c(step, _):
        i = 3 - step
        for at, action in (
            (1, first.pair_start), (2, lambda: scatter_sent(s, s.z, s.ing, 1)), (3, late.lat_start),
        ):
            pl.when(step == at)(action)
        rows = pl.ds(pl.multiple_of(i * CH, CH), CH)
        xhat, istd, _ = layer_norm(s.z[rows, :].astype(F32), s.gains[0:1], s.shifts[0:1])
        gh = dot(s.p[rows, :], s.w_qkv[...], NT)
        s.tail[0:1] += jnp.sum(gh * xhat, 0, keepdims=True)
        s.tail[1:2] += jnp.sum(gh, 0, keepdims=True)
        s.z[rows, :] = (s.gres[rows, :] + norm_backward(gh, xhat, istd, s.gains[0:1])).astype(BF)
        return 0

    lax.fori_loop(0, 4, phase_c, 0)
    tail_lon_start(s)
    late.gather_start()
    scatter_own(s, s.z, s.ing)
    tail_lat_start(s)
    first.pair_done()
    def scaled(value):
        return value.astype(F32) * s.scale

    s.o_in[...] = scaled(s.total[:, W_IN])
    for f in range(4):
        s.o_out[f * 256:(f + 1) * 256] = scaled(s.total[:, 1024 + f * 256:1280 + f * 256])
    s.o_proj[...] = scaled(s.total[:, W_PROJ])
    halo_out_done(s, s.ing, 1)
    late.done()
    s.o_qkv[...] = scaled(s.total[:, W_QKV])
    short = [scaled(s.total[0:32, SHORT]), scaled(s.total[32:64, SHORT])]
    for side in range(2):
        lanes = slice(side * 128, side * 128 + 128)
        s.o_table[:, lanes] = short[side][0:8]
        s.o_gains[1:2, lanes] = short[side][19:20]
        s.o_shifts[1:2, lanes] = short[side][20:21]
        for part in range(3):
            s.o_bias[part * C + side * 128:part * C + side * 128 + 128] = short[side][16 + part]
    s.o_table[:, 256:384] = short[0][8:16]
    s.o_table[:, 384:NREL] = short[1][8:16][:, :NREL - 384]
    tail = tail_done(s) * s.scale
    s.o_gains[0:1] = tail[0:1]
    s.o_shifts[0:1] = tail[1:2]


class Direct:
    def __init__(self, s, cols, number):
        self.s, self.cols, self.sems = s, slice(*cols), s.sums[number]
        self.share = pl.ds(pl.multiple_of(s.lon * 16, 16), 16)

    def lon_copies(self):
        s, out = self.s, []
        for d in range(1, 16):
            peer = (s.lon + d) % 16
            rows = pl.ds(pl.multiple_of(peer * 16, 16), 16)
            out.append(send(s.sent.at[rows, self.cols], s.land_late.at[s.lon], self.sems, d, (s.lat, peer)))
        return out

    def lat_copies(self):
        s, out = self.s, []
        mine = s.land_lat.at[s.lat, :, self.cols]
        for d in range(1, 8):
            out.append(send(mine, mine, self.sems, 15 + d, ((s.lat + d) % 8, s.lon)))
        return out

    def gather_copies(self):
        s, out = self.s, []
        mine = s.total.at[self.share, self.cols]
        for d in range(1, 16):
            out.append(send(mine, mine, self.sems, 22 + d, (s.lat, (s.lon + d) % 16)))
        return out

    def lon_start(self):
        s = self.s
        s.sent[:, self.cols] = s.acc[:, self.cols].astype(BF)
        for copy in self.lon_copies():
            copy.start()

    def lat_start(self):
        s = self.s
        for copy in self.lon_copies():
            copy.wait()
        total = s.acc[self.share, self.cols]
        for d in range(1, 16):
            total += s.land_late[(s.lon + d) % 16].astype(F32)
        s.land_lat[s.lat, :, self.cols] = total.astype(BF)
        for copy in self.lat_copies():
            copy.start()

    def gather_start(self):
        s = self.s
        for copy in self.lat_copies():
            copy.wait()
        total = s.land_lat[0, :, self.cols].astype(F32)
        for i in range(1, 8):
            total += s.land_lat[i, :, self.cols].astype(F32)
        s.total[self.share, self.cols] = total.astype(BF)
        for copy in self.gather_copies():
            copy.start()

    def done(self):
        for copy in self.gather_copies():
            copy.wait()


class Refs:
    pass


T = 32 * WROWS
GRID = (LEV, C)
INS = ("x_in", "g_in", "pm", "index", "gains", "shifts", "w_qkv", "b_qkv", "w_proj", "w_in", "w_out", "rel_bias")
OUTS = {
    "res": ((28, 28) + GRID, BF), "ing": ((28, 28) + GRID, BF), "o_gains": ((2, C), F32), "o_shifts": ((2, C), F32),
    "o_qkv": ((C, 3 * C), F32), "o_bias": ((3 * C,), F32), "o_proj": ((C, C), F32), "o_in": ((C, FF), F32),
    "o_out": ((FF, C), F32), "o_table": ((HEADS, NREL), F32),
}
SCRATCH = {
    "x": ((31, 32) + GRID, BF), "g": ((31, 32) + GRID, BF),
    "z": ((T, C), BF), "gz": ((T, C), BF), "p": ((T, 3 * C), BF), "att": ((T * HALF, 256), BF), "mixed": ((T, C), BF),
    "gres": ((T, C), F32), "bias": ((2, HALF * WROWS, 256), F32), "dbias": ((HALF * WROWS, 256), F32),
    "rel": ((8, 512), F32), "strip": ((SLAB, 8, 256), F32), "dstrip": ((8, SLAB, 256), F32),
    "acc": ((256, COLS), F32), "small": ((32, C), F32), "land_late": ((16, 16, 896), BF), "sent": ((256, COLS), BF), "land_core": ((128, COLS), BF), "part": ((128, COLS), BF),
    "land_lon": ((8, 16, COLS), BF), "land_lat": ((8, 16, COLS), BF), "total": ((256, COLS), BF),
    "side": ((2, 28, 4) + GRID, BF), "foot": ((2, 3, 32) + GRID, BF), "land_side": ((2, 28, 4) + GRID, BF),
    "land_foot": ((2, 3, 28) + GRID, BF),
    "tail": ((8, C), F32), "tail_lon": ((16, 8, C), F32), "tail_lat": ((8, 8, C), F32),
}
SEMS = (2, 12, 12, 24, 24, 24, 24, 38, 38, 23, 23)


def kernel(scale, *refs):
    s = Refs()
    names = INS + tuple(OUTS) + tuple(SCRATCH)
    for name, ref in zip(names, refs):
        setattr(s, name, ref)
    sems = refs[len(names):]
    s.near_sem, s.halo, s.tails = sems[0], sems[1:3], sems[9:11]
    s.sums = (sems[3:5], sems[5:7], sems[7:9])
    s.lat, s.lon = lax.axis_index("lat"), lax.axis_index("lon")
    s.last, s.scale = s.lat == 7, scale
    compute(s)


def fused(scale, *args):
    vm = pl.BlockSpec(memory_space=pltpu.VMEM)
    return pl.pallas_call(
        functools.partial(kernel, scale),
        out_shape=tuple(jax.ShapeDtypeStruct(*v) for v in OUTS.values()),
        in_specs=[pl.BlockSpec(memory_space=pl.ANY)] * 2 + [vm] * (len(INS) - 2),
        out_specs=[vm] * len(OUTS),
        scratch_shapes=[pltpu.VMEM(*v) for v in SCRATCH.values()] + [pltpu.SemaphoreType.DMA((n,)) for n in SEMS],
        compiler_params=pltpu.CompilerParams(
            vmem_limit_bytes=63 * 1024 * 1024, collective_id=0, has_side_effects=True
        ),
        name="windows",
    )(*args)


def deliver(arrays):
    count = len(arrays)

    def body(*refs):
        ins, outs, held, sems = refs[:count], refs[count:2 * count], refs[2 * count:3 * count], refs[3 * count]
        come = [pltpu.make_async_copy(ins[i], held[i], sems.at[0, i]) for i in range(count)]
        leave = [pltpu.make_async_copy(held[i], outs[i], sems.at[1, i]) for i in range(count)]
        for copy in come:
            copy.start()
        for i in range(count):
            come[i].wait()
            leave[i].start()
        for copy in leave:
            copy.wait()

    some = pl.BlockSpec(memory_space=pl.ANY)
    return pl.pallas_call(
        body,
        out_shape=tuple(jax.ShapeDtypeStruct(v.shape, v.dtype) for v in arrays),
        in_specs=[some] * count,
        out_specs=[some] * count,
        scratch_shapes=[pltpu.VMEM(v.shape, v.dtype) for v in arrays] + [pltpu.SemaphoreType.DMA((2, count))],
        compiler_params=pltpu.CompilerParams(vmem_limit_bytes=62 * 1024 * 1024),
        name="deliver",
    )(*arrays)


def local(tokens, out_grad, gains, shifts, w_qkv, b_qkv, w_proj, w_in, w_out, rel_bias):
    rows_n, cols_n, levels, channels = tokens.shape
    scale = float(rows_n * lax.axis_size("lat") * cols_n * lax.axis_size("lon") * levels) ** -0.5
    outs = fused(
        scale, tokens, out_grad, jnp.asarray(placement(), BF), jnp.asarray(strip_map()), gains, shifts, w_qkv, b_qkv,
        w_proj, w_in, w_out, rel_bias,
    )
    return deliver(outs)


def solution(mesh):
    big = P("lat", "lon", None, None)
    return jax.shard_map(
        local, mesh=mesh, in_specs=(big, big) + (P(),) * 8, out_specs=(big, big) + (P(),) * 8, check_vma=False
    )
```

```python
import functools

import jax
import jax.numpy as jnp
import numpy as np
from jax import lax
from jax.experimental import pallas as pl
from jax.experimental.pallas import tpu as pltpu
from jax.sharding import PartitionSpec as P

WIN = 7
LEV = 4
WLEV = 2
SHIFT = 3
EPS = 1e-05
NEG = -1e30
HEADS = 8
HD = 32
C = 256
FF = 1024
SLAB = 16
WROWS = WIN * SLAB
HALF = HEADS // 2
PAIR = 2 * 128
NREL = 507
BF = jnp.bfloat16
F32 = jnp.float32

NN = (((1,), (0,)), ((), ()))
NT = (((1,), (1,)), ((), ()))
TN = (((0,), (0,)), ((), ()))


def dot(a, b, dims=NN):
    return lax.dot_general(a, b, dims, preferred_element_type=F32)


def placement():
    matrix = np.zeros((128, 128), np.float32)
    for wc in range(4):
        for lw in range(2):
            for b in range(WIN):
                for l in range(WLEV):
                    row = (wc * 2 + lw) * SLAB + b * WLEV + l
                    matrix[row, (wc * WIN + SHIFT + b) * LEV + lw * WLEV + l] = 1.0
    return matrix


def strip_map():
    index = np.full((SLAB, 256), -1, np.int32)
    for bk in range(WIN):
        for lk in range(WLEV):
            for da in range(13):
                for bq in range(WIN):
                    for lq in range(WLEV):
                        index[bk * WLEV + lk, da * SLAB + bq * WLEV + lq] = (
                            (da * 13 + bq - bk + 6) * 3 + lq - lk + 1
                        )
    return index


def layer_norm(x, gain, shift):
    center = x - jnp.mean(x, -1, keepdims=True)
    istd = lax.rsqrt(jnp.mean(center * center, -1, keepdims=True) + EPS)
    xhat = center * istd
    return xhat, istd, (xhat * gain + shift).astype(BF)


def norm_backward(up, xhat, istd, gain):
    n = up * gain
    return istd * (n - jnp.mean(n, -1, keepdims=True) - xhat * jnp.mean(n * xhat, -1, keepdims=True))


def gelu_both(p):
    c0 = np.float32(np.sqrt(2.0 / np.pi))
    c1 = np.float32(0.044715 * np.sqrt(2.0 / np.pi))
    p2 = p * p
    t = jnp.tanh(p * (c0 + c1 * p2))
    half = 0.5 + 0.5 * t
    act = p * half
    slope = half + act * (1.0 - half) * ((2.0 * c0) + (6.0 * c1) * p2)
    return act, slope


def head_masks():
    lane = lax.broadcasted_iota(jnp.int32, (1, C), 1) // HD
    pair = [((lane % HALF) == j) for j in range(HALF)]
    group = [((lane // HALF) == g) for g in range(2)]
    return pair, group


def stack_pairs(v, pair):
    return jnp.concatenate([v * m.astype(BF) for m in pair], 0)


def stack_groups(v, group):
    pad = jnp.zeros((128 - WROWS, C), BF)
    return jnp.concatenate([v * group[0].astype(BF), pad, v * group[1].astype(BF), pad], 0)


def pick_pairs(r, pair):
    out = r[3 * WROWS:4 * WROWS]
    for j in range(3):
        out = jnp.where(pair[j], r[j * WROWS:(j + 1) * WROWS], out)
    return out


def down_keys(vt, low):
    parts = [None] * HEADS
    for j in range(HALF):
        lhs = jnp.concatenate([vt[j * HD:(j + 1) * HD], vt[(j + HALF) * HD:(j + HALF + 1) * HD]], 0)
        out = dot(lhs, low[j * WROWS:(j + 1) * WROWS])
        parts[j] = out[:HD, :128]
        parts[j + HALF] = out[HD:, 128:]
    return jnp.concatenate(parts, 0).T[:WROWS]


FIRST, LATE = (0, 2304), (2304, 3200)
W_IN, W_PROJ, W_QKV, SHORT = slice(0, 1024), slice(2048, 2304), slice(2304, 3072), slice(3072, 3200)
COLS = 3200
LOG2E = np.float32(1.4426950408889634)
MESH = pl.DeviceIdType.MESH


def send(src, dst, sems, index, device):
    return pltpu.make_async_remote_copy(
        src_ref=src, dst_ref=dst, send_sem=sems[0].at[index], recv_sem=sems[1].at[index],
        device_id=device, device_id_type=MESH,
    )


def greet(s):
    barrier = pltpu.get_barrier_semaphore()
    peers = [((s.lat + d) % 8, s.lon) for d in range(1, 8)] + [(s.lat, (s.lon + d) % 16) for d in range(1, 16)]
    peers += [((s.lat + d) % 8, (s.lon + d) % 16) for d in (1, -1)]
    for peer in peers:
        pl.semaphore_signal(barrier, inc=1, device_id=peer, device_id_type=MESH)
    pl.semaphore_wait(barrier, len(peers))


def near_copies(s):
    return [
        pltpu.make_async_copy(src, dst.at[0:28, 0:28], s.near_sem.at[n])
        for n, (src, dst) in enumerate(((s.x_in, s.x), (s.g_in, s.g)))
    ]


def halo_in_copies(s):
    west, north = (s.lon + 15) % 16, (s.lat + 7) % 8
    far = []
    for n, (src, dst) in enumerate(((s.x_in, s.x), (s.g_in, s.g))):
        far.append(send(src.at[:, 0:4], dst.at[0:28, 28:32], s.halo, 3 * n, (s.lat, west)))
        far.append(send(src.at[0:SHIFT], dst.at[28:31, 0:28], s.halo, 3 * n + 1, (north, s.lon)))
        far.append(send(src.at[0:SHIFT, 0:4], dst.at[28:31, 28:32], s.halo, 3 * n + 2, (north, west)))
    return far


def halo_start(s):
    for copy in near_copies(s):
        copy.start()
    greet(s)
    for copy in halo_in_copies(s):
        copy.start()


def near_done(s):
    for copy in near_copies(s):
        copy.wait()


def halo_in_done(s):
    for copy in halo_in_copies(s):
        copy.wait()


def slab(r, c):
    wr = r // WIN
    slot = jnp.where(wr < 3, wr * 6 + c if c < 6 else 12 + wr * 2 + c, 24 + c)
    return pl.ds(pl.multiple_of(slot * WROWS + (r % WIN) * SLAB, SLAB), SLAB)


def gather_own(s, src, dst):
    def row(r, _):
        y = dot(s.pm[0:96, 0:112], src[r + SHIFT, 0:28].reshape(112, C)).astype(BF)
        for c in range(6):
            dst[slab(r, c), :] = y[c * SLAB:(c + 1) * SLAB]
        return 0
    lax.fori_loop(0, 25, row, 0, unroll=25)


def gather_rest(s, src, dst):
    def row(r, _):
        y = dot(s.pm[96:128], src[r + SHIFT].reshape(128, C)).astype(BF)
        for c in range(2):
            dst[slab(r, 6 + c), :] = y[c * SLAB:(c + 1) * SLAB]
        return 0
    lax.fori_loop(0, 25, row, 0, unroll=25)
    for r in range(25, 28):
        y = dot(s.pm[...], src[r + SHIFT].reshape(128, C)).astype(BF)
        for c in range(8):
            dst[slab(r, c), :] = y[c * SLAB:(c + 1) * SLAB]


def halo_out_copies(s, n):
    east, south = (s.lon + 1) % 16, (s.lat + 1) % 8
    return [
        send(s.side.at[n, SHIFT:28], s.land_side.at[n, SHIFT:28], s.halo, 6 + 3 * n, (s.lat, east)),
        send(s.foot.at[n, :, 0:28], s.land_foot.at[n], s.halo, 7 + 3 * n, (south, s.lon)),
        send(s.foot.at[n, :, 28:32], s.land_side.at[n, 0:SHIFT], s.halo, 8 + 3 * n, (south, east)),
    ]


def grid_row(s, src, r, low, high):
    y = jnp.concatenate([src[slab(r, c), :] for c in range(low, high)], 0)
    return dot(s.pm[low * SLAB:high * SLAB], y, TN).astype(BF).reshape(32, LEV, C)


def scatter_foot(s, src, n):
    for r in range(25, 28):
        s.foot[n, r - 25] = grid_row(s, src, r, 0, 8)


def scatter_all(s, src, dst, n):
    scatter_foot(s, src, n)

    def row(r, _):
        y = grid_row(s, src, r, 0, 8)
        dst[r + SHIFT] = y[:28]
        s.side[n, r + SHIFT] = y[28:]
        return 0
    lax.fori_loop(0, 25, row, 0, unroll=25)
    for copy in halo_out_copies(s, n):
        copy.start()


def scatter_sent(s, src, dst, n):
    scatter_foot(s, src, n)

    def row(r, _):
        y = grid_row(s, src, r, 6, 8)
        dst[r + SHIFT, 24:28] = y[24:28]
        s.side[n, r + SHIFT] = y[28:]
        return 0
    lax.fori_loop(0, 25, row, 0, unroll=25)
    for copy in halo_out_copies(s, n):
        copy.start()


def scatter_own(s, src, dst):
    def row(r, _):
        dst[r + SHIFT, 0:24] = grid_row(s, src, r, 0, 6)[0:24]
        return 0
    lax.fori_loop(0, 25, row, 0, unroll=25)


def halo_out_done(s, dst, n):
    for copy in halo_out_copies(s, n):
        copy.wait()
    dst[0:SHIFT] = s.land_foot[n]

    def row(r, _):
        both = dst[r, 0:4].reshape(16, C) + s.land_side[n, r].reshape(16, C)
        dst[r, 0:4] = both.reshape(4, LEV, C)
        return 0
    lax.fori_loop(0, 28, row, 0, unroll=28)


def thirds(value):
    high = value.astype(BF)
    rest = value - high.astype(F32)
    mid = rest.astype(BF)
    return jnp.concatenate([v.astype(F32) for v in (high, mid, (rest - mid.astype(F32)))], 0).astype(BF)


def chosen(s, i):
    slots = lax.broadcasted_iota(jnp.int32, (512, 256), 0)
    return jnp.where(slots == s.index[i:i + 1, :], 1.0, 0.0).astype(BF)


def expand_table(s):
    s.rel[...] = jnp.zeros_like(s.rel)
    s.rel[:, 0:NREL] = s.rel_bias[...]
    table = thirds(s.rel[...])
    s.strip[...] = jnp.zeros_like(s.strip)
    for i in range(WIN * WLEV):
        out = dot(table, chosen(s, i))
        s.strip[i] = out[0:8] + out[8:16] + out[16:24]


def collect_table(s):
    for h in range(HEADS):
        j, g = h % HALF, h // HALF
        total = None
        for ak in range(WIN):
            piece = s.dbias[j * WROWS + ak * SLAB:j * WROWS + (ak + 1) * SLAB, g * 128:g * 128 + WROWS]
            before = (6 - ak) * SLAB
            parts = [jnp.zeros((SLAB, before), F32)] if before else []
            moved = jnp.concatenate(parts + [piece, jnp.zeros((SLAB, 256 - before - WROWS), F32)], 1)
            total = moved if total is None else total + moved
        s.dstrip[h] = total
    table = None
    for i in range(WIN * WLEV):
        part = dot(thirds(s.dstrip[:, i, :]), chosen(s, i), NT)
        table = part if table is None else table + part
    table = table[0:8] + table[8:16] + table[16:24]
    s.small[0:8] = table[:, 0:256]
    s.small[8:16] = table[:, 256:512]
    s.acc[:, SHORT] = jnp.zeros((C, 128), F32)
    s.acc[0:32, SHORT] = s.small[:, 0:128]
    s.acc[32:64, SHORT] = s.small[:, 128:256]


def tail_lon_copies(s):
    mine, out = s.tail_lon.at[s.lon], []
    for d in range(1, 16):
        out.append(send(mine, mine, s.tails, d, (s.lat, (s.lon + d) % 16)))
    return out


def tail_lat_copies(s):
    mine, out = s.tail_lat.at[s.lat], []
    for d in range(1, 8):
        out.append(send(mine, mine, s.tails, 15 + d, ((s.lat + d) % 8, s.lon)))
    return out


def tail_lon_start(s):
    s.tail_lon[s.lon] = s.tail[...]
    for copy in tail_lon_copies(s):
        copy.start()


def tail_lat_start(s):
    for copy in tail_lon_copies(s):
        copy.wait()
    s.tail_lat[s.lat] = sum(s.tail_lon[i] for i in range(16))
    for copy in tail_lat_copies(s):
        copy.start()


def tail_done(s):
    for copy in tail_lat_copies(s):
        copy.wait()
    return sum(s.tail_lat[i] for i in range(8))


class Exchange:
    def __init__(self, s, cols, number):
        self.s, self.cols, self.sems = s, slice(*cols), s.sums[number]
        self.core, self.chip = s.lon % 2, s.lon // 2
        self.half = pl.ds(pl.multiple_of(self.core * 128, 128), 128)
        self.other = pl.ds(pl.multiple_of((1 - self.core) * 128, 128), 128)
        self.share = pl.ds(pl.multiple_of(self.core * 128 + self.chip * 16, 16), 16)
        self.twin = (s.lat, s.lon + 1 - 2 * self.core)

    def core_copies(self):
        s = self.s
        out = [send(s.sent.at[self.other, self.cols], s.land_core.at[:, self.cols], self.sems, 0, self.twin)]
        return out

    def lon_copies(self):
        s, out = self.s, []
        for d in range(1, 8):
            peer = (self.chip + d) % 8
            to = (s.lat, peer * 2 + self.core)
            rows = pl.ds(pl.multiple_of(peer * 16, 16), 16)
            out.append(send(s.part.at[rows, self.cols], s.land_lon.at[self.chip, :, self.cols], self.sems, d, to))
        return out

    def lat_copies(self):
        s, out = self.s, []
        for d in range(1, 8):
            to = ((s.lat + d) % 8, s.lon)
            mine = s.land_lat.at[s.lat, :, self.cols]
            out.append(send(mine, mine, self.sems, 8 + d, to))
        return out

    def gather_copies(self):
        s, out = self.s, []
        for d in range(1, 8):
            to = (s.lat, ((self.chip + d) % 8) * 2 + self.core)
            mine = s.total.at[self.share, self.cols]
            out.append(send(mine, mine, self.sems, 16 + d, to))
        return out

    def pair_copies(self):
        mine = self.s.total.at[self.half, self.cols]
        return [send(mine, mine, self.sems, 16, self.twin)]

    def core_start(self):
        s = self.s
        s.sent[self.other, self.cols] = s.acc[self.other, self.cols].astype(BF)
        for copy in self.core_copies():
            copy.start()

    def lon_start(self):
        s = self.s
        for copy in self.core_copies():
            copy.wait()
        both = s.acc[self.half, self.cols] + s.land_core[:, self.cols].astype(F32)
        s.acc[self.half, self.cols] = both
        s.part[:, self.cols] = both.astype(BF)
        for copy in self.lon_copies():
            copy.start()

    def lat_start(self):
        s = self.s
        for copy in self.lon_copies():
            copy.wait()
        total = s.acc[self.share, self.cols]
        for d in range(1, 8):
            total += s.land_lon[(self.chip + d) % 8, :, self.cols].astype(F32)
        s.land_lat[s.lat, :, self.cols] = total.astype(BF)
        for copy in self.lat_copies():
            copy.start()

    def gather_start(self):
        s = self.s
        for copy in self.lat_copies():
            copy.wait()
        total = s.land_lat[0, :, self.cols].astype(F32)
        for i in range(1, 8):
            total += s.land_lat[i, :, self.cols].astype(F32)
        s.total[self.share, self.cols] = total.astype(BF)
        for copy in self.gather_copies():
            copy.start()

    def pair_start(self):
        for copy in self.gather_copies():
            copy.wait()
        for copy in self.pair_copies():
            copy.start()

    def pair_done(self):
        for copy in self.pair_copies():
            copy.wait()


def compute(s, chunk_windows=8):
    pair, group = head_masks()
    scale = np.float32(HD ** -0.5)
    CH = chunk_windows * WROWS
    nwin = 32

    halo_start(s)

    expand_table(s)
    key_row = lax.broadcasted_iota(jnp.int32, (WROWS, 256), 0)
    lane = lax.broadcasted_iota(jnp.int32, (WROWS, 256), 1)
    qa, ka = (lane % 128) // SLAB, key_row // SLAB
    empty = (key_row % SLAB) >= WIN * WLEV
    cut = jnp.logical_and((qa >= WIN - SHIFT) != (ka >= WIN - SHIFT), s.last)
    for j in range(HALF):
        tiles = []
        for g in range(2):
            strip = s.strip[:, j + HALF * g, :] * LOG2E
            rows = [strip[:, (6 - ak) * SLAB:(6 - ak) * SLAB + WROWS] for ak in range(WIN)]
            tile = jnp.concatenate(rows, 0)
            tiles.append(jnp.concatenate([tile, jnp.zeros((WROWS, 128 - WROWS), F32)], 1))
        full = jnp.where(empty, NEG, jnp.concatenate(tiles, 1))
        s.bias[0, j * WROWS:(j + 1) * WROWS] = full
        s.bias[1, j * WROWS:(j + 1) * WROWS] = jnp.where(cut, NEG, full)
    s.dbias[...] = jnp.zeros_like(s.dbias)
    s.tail[...] = jnp.zeros_like(s.tail)
    s.acc[...] = jnp.zeros_like(s.acc)
    s.small[...] = jnp.zeros_like(s.small)
    near_done(s)
    for src, dst in ((s.x, s.z), (s.g, s.gz)):
        gather_own(s, src, dst)

    def rest():
        halo_in_done(s)
        for src, dst in ((s.x, s.z), (s.g, s.gz)):
            gather_rest(s, src, dst)

    def forward_window(w):
        rows = pl.ds(pl.multiple_of(w * WROWS, WROWS), WROWS)
        arows = pl.multiple_of(w * (HALF * WROWS), HALF * WROWS)
        q, k, v = s.p[rows, 0:C], s.p[rows, C:2 * C], s.p[rows, 2 * C:3 * C]
        scores = dot(stack_pairs(k, pair), stack_groups(q, group), NT)
        which = (w >= 24).astype(jnp.int32)
        vt = v.T
        lows = []
        for j in range(HALF):
            t = scores[j * WROWS:(j + 1) * WROWS] * (scale * LOG2E) + s.bias[which, j * WROWS:(j + 1) * WROWS]
            e = jnp.exp2(t - jnp.max(t, 0, keepdims=True))
            att = e * (1.0 / jnp.sum(e, 0, keepdims=True))
            low = att.astype(BF)
            s.att[pl.ds(arows + j * WROWS, WROWS), :] = low
            lows.append(low)
        s.mixed[rows, :] = down_keys(vt, jnp.concatenate(lows, 0)).astype(BF)

    def phase_a(step, _):
        i = step
        pl.when(step == 1)(rest)
        rows = pl.ds(pl.multiple_of(i * (2 * CH), CH), 2 * CH)
        x = s.z[rows, :].astype(F32)
        _, _, hidden1 = layer_norm(x, s.gains[0:1], s.shifts[0:1])
        s.p[rows, :] = (dot(hidden1, s.w_qkv[...]) + s.b_qkv[...]).astype(BF)

        def win(w, _):
            for u in range(4):
                forward_window(i * (2 * chunk_windows) + 4 * w + u)
            return 0
        lax.fori_loop(0, 4, win, 0)

        mixed = s.mixed[rows, :]
        resid = s.z[rows, :].astype(F32) + dot(mixed, s.w_proj[...])
        xhat2, istd2, hidden2 = layer_norm(resid, s.gains[1:2], s.shifts[1:2])
        gr = s.gz[rows, :]
        gr_t, hid_t = gr.T, hidden2.T
        out, gh = resid, None
        for f in range(4):
            cols = slice(f * 256, f * 256 + 256)
            act, slope = gelu_both(dot(hidden2, s.w_in[:, cols]))
            act = act.astype(BF)
            out = out + dot(act, s.w_out[cols, :])
            s.acc[:, 1024 + f * 256:1280 + f * 256] += dot(gr_t, act)
            gp = (dot(gr, s.w_out[cols, :], NT) * slope).astype(BF)
            s.acc[:, cols] += dot(hid_t, gp)
            part = dot(gp, s.w_in[:, cols], NT)
            gh = part if gh is None else gh + part
        s.gz[rows, :] = out.astype(BF)
        s.small[19:20] += jnp.sum(gh * xhat2, 0, keepdims=True)
        s.small[20:21] += jnp.sum(gh, 0, keepdims=True)
        gres = gr.astype(F32) + norm_backward(gh, xhat2, istd2, s.gains[1:2])
        s.gres[rows, :] = gres
        low = gres.astype(BF)
        s.acc[:, W_PROJ] += dot(mixed, low, TN)
        s.mixed[rows, :] = dot(low, s.w_proj[...], NT).astype(BF)
        return 0

    lax.fori_loop(0, 2, phase_a, 0)
    for f in range(4):
        cols = slice(1024 + f * 256, 1280 + f * 256)
        s.acc[:, cols] = s.acc[:, cols].T
    first, late = Exchange(s, FIRST, 0), Direct(s, LATE, 2)
    first.core_start()
    scatter_all(s, s.gz, s.res, 0)

    def backward_window(w):
        rows = pl.ds(pl.multiple_of(w * WROWS, WROWS), WROWS)
        arows = pl.multiple_of(w * (HALF * WROWS), HALF * WROWS)
        q, k, v = s.p[rows, 0:C], s.p[rows, C:2 * C], s.p[rows, 2 * C:3 * C]
        gm2 = stack_groups(s.mixed[rows, :], group)
        ga = dot(stack_pairs(v, pair), gm2, NT)
        lows, dlows = [], []
        for j in range(HALF):
            low = s.att[pl.ds(arows + j * WROWS, WROWS), :]
            att = low.astype(F32)
            t = att * ga[j * WROWS:(j + 1) * WROWS]
            ds = t - att * jnp.sum(t, 0, keepdims=True)
            s.dbias[j * WROWS:(j + 1) * WROWS] += ds
            lows.append(low)
            dlows.append((ds * scale).astype(BF))
        low, dlow = jnp.concatenate(lows, 0), jnp.concatenate(dlows, 0)
        gv = pick_pairs(dot(low, gm2), pair).astype(BF)
        gk = pick_pairs(dot(dlow, stack_groups(q, group)), pair).astype(BF)
        gq = down_keys(k.T, dlow).astype(BF)
        s.p[rows, 0:C] = gq
        s.p[rows, C:2 * C] = gk
        s.p[rows, 2 * C:3 * C] = gv

    def phase_b(i, _):
        rows = pl.ds(pl.multiple_of(i * CH, CH), CH)
        for at, step in ((1, first.lon_start), (2, first.lat_start), (3, first.gather_start)):
            pl.when(i == at)(step)

        def win(w, _):
            for u in range(4):
                backward_window(i * chunk_windows + 4 * w + u)
            return 0
        lax.fori_loop(0, chunk_windows // 4, win, 0)
        _, _, hidden = layer_norm(s.z[rows, :].astype(F32), s.gains[0:1], s.shifts[0:1])
        gp = s.p[rows, :]
        s.acc[:, W_QKV] += dot(hidden, gp, TN)
        sums = jnp.sum(gp.astype(F32), 0, keepdims=True)
        for part in range(3):
            s.small[16 + part:17 + part] += sums[:, part * C:(part + 1) * C]
        return 0

    lax.fori_loop(0, 4, phase_b, 0)
    collect_table(s)
    late.lon_start()
    halo_out_done(s, s.res, 0)
    s.leave["res"].start()

    def phase_c(step, _):
        i = 3 - step
        for at, action in (
            (1, first.pair_start), (2, lambda: scatter_sent(s, s.z, s.ing, 1)), (3, late.lat_start),
        ):
            pl.when(step == at)(action)
        rows = pl.ds(pl.multiple_of(i * CH, CH), CH)
        xhat, istd, _ = layer_norm(s.z[rows, :].astype(F32), s.gains[0:1], s.shifts[0:1])
        gh = dot(s.p[rows, :], s.w_qkv[...], NT)
        s.tail[0:1] += jnp.sum(gh * xhat, 0, keepdims=True)
        s.tail[1:2] += jnp.sum(gh, 0, keepdims=True)
        s.z[rows, :] = (s.gres[rows, :] + norm_backward(gh, xhat, istd, s.gains[0:1])).astype(BF)
        return 0

    lax.fori_loop(0, 4, phase_c, 0)
    tail_lon_start(s)
    late.gather_start()
    scatter_own(s, s.z, s.ing)
    tail_lat_start(s)
    first.pair_done()
    def scaled(value):
        return value.astype(F32) * s.scale

    s.o_in[...] = scaled(s.total[:, W_IN])
    for f in range(4):
        s.o_out[f * 256:(f + 1) * 256] = scaled(s.total[:, 1024 + f * 256:1280 + f * 256])
    s.o_proj[...] = scaled(s.total[:, W_PROJ])
    for name in ("o_in", "o_out", "o_proj"):
        s.leave[name].start()
    halo_out_done(s, s.ing, 1)
    s.leave["ing"].start()
    late.done()
    s.o_qkv[...] = scaled(s.total[:, W_QKV])
    s.leave["o_qkv"].start()
    short = [scaled(s.total[0:32, SHORT]), scaled(s.total[32:64, SHORT])]
    for side in range(2):
        lanes = slice(side * 128, side * 128 + 128)
        s.o_table[:, lanes] = short[side][0:8]
        s.o_gains[1:2, lanes] = short[side][19:20]
        s.o_shifts[1:2, lanes] = short[side][20:21]
        for part in range(3):
            s.o_bias[part * C + side * 128:part * C + side * 128 + 128] = short[side][16 + part]
    s.o_table[:, 256:384] = short[0][8:16]
    s.o_table[:, 384:NREL] = short[1][8:16][:, :NREL - 384]
    tail = tail_done(s) * s.scale
    s.o_gains[0:1] = tail[0:1]
    s.o_shifts[0:1] = tail[1:2]
    for name in BIG:
        s.leave[name].wait()


class Direct:
    def __init__(self, s, cols, number):
        self.s, self.cols, self.sems = s, slice(*cols), s.sums[number]
        self.share = pl.ds(pl.multiple_of(s.lon * 16, 16), 16)

    def lon_copies(self):
        s, out = self.s, []
        for d in range(1, 16):
            peer = (s.lon + d) % 16
            rows = pl.ds(pl.multiple_of(peer * 16, 16), 16)
            out.append(send(s.sent.at[rows, self.cols], s.land_late.at[s.lon], self.sems, d, (s.lat, peer)))
        return out

    def lat_copies(self):
        s, out = self.s, []
        mine = s.land_lat.at[s.lat, :, self.cols]
        for d in range(1, 8):
            out.append(send(mine, mine, self.sems, 15 + d, ((s.lat + d) % 8, s.lon)))
        return out

    def gather_copies(self):
        s, out = self.s, []
        mine = s.total.at[self.share, self.cols]
        for d in range(1, 16):
            out.append(send(mine, mine, self.sems, 22 + d, (s.lat, (s.lon + d) % 16)))
        return out

    def lon_start(self):
        s = self.s
        s.sent[:, self.cols] = s.acc[:, self.cols].astype(BF)
        for copy in self.lon_copies():
            copy.start()

    def lat_start(self):
        s = self.s
        for copy in self.lon_copies():
            copy.wait()
        total = s.acc[self.share, self.cols]
        for d in range(1, 16):
            total += s.land_late[(s.lon + d) % 16].astype(F32)
        s.land_lat[s.lat, :, self.cols] = total.astype(BF)
        for copy in self.lat_copies():
            copy.start()

    def gather_start(self):
        s = self.s
        for copy in self.lat_copies():
            copy.wait()
        total = s.land_lat[0, :, self.cols].astype(F32)
        for i in range(1, 8):
            total += s.land_lat[i, :, self.cols].astype(F32)
        s.total[self.share, self.cols] = total.astype(BF)
        for copy in self.gather_copies():
            copy.start()

    def done(self):
        for copy in self.gather_copies():
            copy.wait()


class Refs:
    pass


T = 32 * WROWS
GRID = (LEV, C)
INS = ("x_in", "g_in", "pm", "index", "gains", "shifts", "w_qkv", "b_qkv", "w_proj", "w_in", "w_out", "rel_bias")
OUTS = {
    "res": ((28, 28) + GRID, BF), "ing": ((28, 28) + GRID, BF), "o_gains": ((2, C), F32), "o_shifts": ((2, C), F32),
    "o_qkv": ((C, 3 * C), F32), "o_bias": ((3 * C,), F32), "o_proj": ((C, C), F32), "o_in": ((C, FF), F32),
    "o_out": ((FF, C), F32), "o_table": ((HEADS, NREL), F32),
}
SCRATCH = {
    "x": ((31, 32) + GRID, BF), "g": ((31, 32) + GRID, BF),
    "z": ((T, C), BF), "gz": ((T, C), BF), "p": ((T, 3 * C), BF), "att": ((T * HALF, 256), BF), "mixed": ((T, C), BF),
    "gres": ((T, C), F32), "bias": ((2, HALF * WROWS, 256), F32), "dbias": ((HALF * WROWS, 256), F32),
    "rel": ((8, 512), F32), "strip": ((SLAB, 8, 256), F32), "dstrip": ((8, SLAB, 256), F32),
    "acc": ((256, COLS), F32), "small": ((32, C), F32), "land_late": ((16, 16, 896), BF), "sent": ((256, COLS), BF), "land_core": ((128, COLS), BF), "part": ((128, COLS), BF),
    "land_lon": ((8, 16, COLS), BF), "land_lat": ((8, 16, COLS), BF), "total": ((256, COLS), BF),
    "side": ((2, 28, 4) + GRID, BF), "foot": ((2, 3, 32) + GRID, BF), "land_side": ((2, 28, 4) + GRID, BF),
    "land_foot": ((2, 3, 28) + GRID, BF),
    "tail": ((8, C), F32), "tail_lon": ((16, 8, C), F32), "tail_lat": ((8, 8, C), F32),
}
SEMS = (2, 12, 12, 24, 24, 24, 24, 38, 38, 23, 23, 6)


BIG = ("res", "ing", "o_qkv", "o_proj", "o_in", "o_out")


def kernel(scale, *refs):
    s = Refs()
    names = INS + tuple(OUTS) + tuple(SCRATCH)
    for name, ref in zip(names, refs):
        setattr(s, name, ref)
    held = refs[len(names):len(names) + len(BIG)]
    s.leave = {}
    sems = refs[len(names) + len(BIG):]
    for i, name in enumerate(BIG):
        s.leave[name] = pltpu.make_async_copy(held[i], getattr(s, name), sems[11].at[i])
        setattr(s, name, held[i])
    s.near_sem, s.halo, s.tails = sems[0], sems[1:3], sems[9:11]
    s.sums = (sems[3:5], sems[5:7], sems[7:9])
    s.lat, s.lon = lax.axis_index("lat"), lax.axis_index("lon")
    s.last, s.scale = s.lat == 7, scale
    compute(s)


def fused(scale, *args):
    vm = pl.BlockSpec(memory_space=pltpu.VMEM)
    return pl.pallas_call(
        functools.partial(kernel, scale),
        out_shape=tuple(jax.ShapeDtypeStruct(*v) for v in OUTS.values()),
        in_specs=[pl.BlockSpec(memory_space=pl.ANY)] * 2 + [vm] * (len(INS) - 2),
        out_specs=[pl.BlockSpec(memory_space=pl.ANY) if name in BIG else vm for name in OUTS],
        scratch_shapes=[pltpu.VMEM(*v) for v in SCRATCH.values()] + [pltpu.VMEM(*OUTS[name]) for name in BIG] + [pltpu.SemaphoreType.DMA((n,)) for n in SEMS],
        compiler_params=pltpu.CompilerParams(
            vmem_limit_bytes=63 * 1024 * 1024, collective_id=0, has_side_effects=True
        ),
        name="windows",
    )(*args)


def deliver(arrays):
    count = len(arrays)

    def body(*refs):
        ins, outs, held, sems = refs[:count], refs[count:2 * count], refs[2 * count:3 * count], refs[3 * count]
        come = [pltpu.make_async_copy(ins[i], held[i], sems.at[0, i]) for i in range(count)]
        leave = [pltpu.make_async_copy(held[i], outs[i], sems.at[1, i]) for i in range(count)]
        for copy in come:
            copy.start()
        for i in range(count):
            come[i].wait()
            leave[i].start()
        for copy in leave:
            copy.wait()

    some = pl.BlockSpec(memory_space=pl.ANY)
    return pl.pallas_call(
        body,
        out_shape=tuple(jax.ShapeDtypeStruct(v.shape, v.dtype) for v in arrays),
        in_specs=[some] * count,
        out_specs=[some] * count,
        scratch_shapes=[pltpu.VMEM(v.shape, v.dtype) for v in arrays] + [pltpu.SemaphoreType.DMA((2, count))],
        compiler_params=pltpu.CompilerParams(vmem_limit_bytes=62 * 1024 * 1024),
        name="deliver",
    )(*arrays)


def local(tokens, out_grad, gains, shifts, w_qkv, b_qkv, w_proj, w_in, w_out, rel_bias):
    rows_n, cols_n, levels, channels = tokens.shape
    scale = float(rows_n * lax.axis_size("lat") * cols_n * lax.axis_size("lon") * levels) ** -0.5
    outs = fused(
        scale, tokens, out_grad, jnp.asarray(placement(), BF), jnp.asarray(strip_map()), gains, shifts, w_qkv, b_qkv,
        w_proj, w_in, w_out, rel_bias,
    )
    return deliver(outs)


def solution(mesh):
    big = P("lat", "lon", None, None)
    return jax.shard_map(
        local, mesh=mesh, in_specs=(big, big) + (P(),) * 8, out_specs=(big, big) + (P(),) * 8, check_vma=False
    )
```

```python
import functools

import jax
import jax.numpy as jnp
import numpy as np
from jax import lax
from jax.experimental import pallas as pl
from jax.experimental.pallas import tpu as pltpu
from jax.sharding import PartitionSpec as P

WIN = 7
LEV = 4
WLEV = 2
SHIFT = 3
EPS = 1e-05
NEG = -1e30
HEADS = 8
HD = 32
C = 256
FF = 1024
SLAB = 16
WROWS = WIN * SLAB
HALF = HEADS // 2
PAIR = 2 * 128
NREL = 507
BF = jnp.bfloat16
F32 = jnp.float32

NN = (((1,), (0,)), ((), ()))
NT = (((1,), (1,)), ((), ()))
TN = (((0,), (0,)), ((), ()))


def dot(a, b, dims=NN):
    return lax.dot_general(a, b, dims, preferred_element_type=F32)


def placement():
    matrix = np.zeros((128, 128), np.float32)
    for wc in range(4):
        for lw in range(2):
            for b in range(WIN):
                for l in range(WLEV):
                    row = (wc * 2 + lw) * SLAB + b * WLEV + l
                    matrix[row, (wc * WIN + SHIFT + b) * LEV + lw * WLEV + l] = 1.0
    return matrix


def strip_map():
    index = np.full((SLAB, 256), -1, np.int32)
    for bk in range(WIN):
        for lk in range(WLEV):
            for da in range(13):
                for bq in range(WIN):
                    for lq in range(WLEV):
                        index[bk * WLEV + lk, da * SLAB + bq * WLEV + lq] = (
                            (da * 13 + bq - bk + 6) * 3 + lq - lk + 1
                        )
    return index


def layer_norm(x, gain, shift):
    center = x - jnp.mean(x, -1, keepdims=True)
    istd = lax.rsqrt(jnp.mean(center * center, -1, keepdims=True) + EPS)
    xhat = center * istd
    return xhat, istd, (xhat * gain + shift).astype(BF)


def norm_backward(up, xhat, istd, gain):
    n = up * gain
    return istd * (n - jnp.mean(n, -1, keepdims=True) - xhat * jnp.mean(n * xhat, -1, keepdims=True))


def gelu_both(p):
    c0 = np.float32(np.sqrt(2.0 / np.pi))
    c1 = np.float32(0.044715 * np.sqrt(2.0 / np.pi))
    p2 = p * p
    t = jnp.tanh(p * (c0 + c1 * p2))
    half = 0.5 + 0.5 * t
    act = p * half
    slope = half + act * (1.0 - half) * ((2.0 * c0) + (6.0 * c1) * p2)
    return act, slope


def head_masks():
    lane = lax.broadcasted_iota(jnp.int32, (1, C), 1) // HD
    pair = [((lane % HALF) == j) for j in range(HALF)]
    group = [((lane // HALF) == g) for g in range(2)]
    return pair, group


def stack_pairs(v, pair):
    return jnp.concatenate([v * m.astype(BF) for m in pair], 0)


def stack_groups(v, group):
    pad = jnp.zeros((128 - WROWS, C), BF)
    return jnp.concatenate([v * group[0].astype(BF), pad, v * group[1].astype(BF), pad], 0)


def pick_pairs(r, pair):
    out = r[3 * WROWS:4 * WROWS]
    for j in range(3):
        out = jnp.where(pair[j], r[j * WROWS:(j + 1) * WROWS], out)
    return out


def down_keys(vt, low):
    parts = [None] * HEADS
    for j in range(HALF):
        lhs = jnp.concatenate([vt[j * HD:(j + 1) * HD], vt[(j + HALF) * HD:(j + HALF + 1) * HD]], 0)
        out = dot(lhs, low[j * WROWS:(j + 1) * WROWS])
        parts[j] = out[:HD, :128]
        parts[j + HALF] = out[HD:, 128:]
    return jnp.concatenate(parts, 0).T[:WROWS]


FIRST, LATE = (0, 2304), (2304, 3200)
W_IN, W_PROJ, W_QKV, SHORT = slice(0, 1024), slice(2048, 2304), slice(2304, 3072), slice(3072, 3200)
COLS = 3200
LOG2E = np.float32(1.4426950408889634)
MESH = pl.DeviceIdType.MESH


def send(src, dst, sems, index, device):
    return pltpu.make_async_remote_copy(
        src_ref=src, dst_ref=dst, send_sem=sems[0].at[index], recv_sem=sems[1].at[index],
        device_id=device, device_id_type=MESH,
    )


def greet_peers(s):
    peers = [((s.lat + d) % 8, s.lon) for d in range(1, 8)] + [(s.lat, (s.lon + d) % 16) for d in range(1, 16)]
    return peers + [((s.lat + d) % 8, (s.lon + d) % 16) for d in (1, -1)]


def near_copies(s):
    return [
        pltpu.make_async_copy(src, dst.at[0:28, 0:28], s.near_sem.at[n])
        for n, (src, dst) in enumerate(((s.x_in, s.x), (s.g_in, s.g)))
    ]


def halo_in_copies(s):
    west, north = (s.lon + 15) % 16, (s.lat + 7) % 8
    far = []
    for n, (src, dst) in enumerate(((s.x_in, s.x), (s.g_in, s.g))):
        far.append(send(src.at[:, 0:4], dst.at[0:28, 28:32], s.halo, 3 * n, (s.lat, west)))
        far.append(send(src.at[0:SHIFT], dst.at[28:31, 0:28], s.halo, 3 * n + 1, (north, s.lon)))
        far.append(send(src.at[0:SHIFT, 0:4], dst.at[28:31, 28:32], s.halo, 3 * n + 2, (north, west)))
    return far


def enter(s):
    for copy in near_copies(s) + s.weights:
        copy.start()
    barrier = pltpu.get_barrier_semaphore()
    for peer in greet_peers(s):
        pl.semaphore_signal(barrier, inc=1, device_id=peer, device_id_type=MESH)


def halo_start(s):
    pl.semaphore_wait(pltpu.get_barrier_semaphore(), len(greet_peers(s)))
    for copy in halo_in_copies(s):
        copy.start()


def near_done(s):
    for copy in near_copies(s):
        copy.wait()


def halo_in_done(s):
    for copy in halo_in_copies(s):
        copy.wait()


def slab(r, c):
    wr = r // WIN
    slot = jnp.where(wr < 3, wr * 6 + c if c < 6 else 12 + wr * 2 + c, 24 + c)
    return pl.ds(pl.multiple_of(slot * WROWS + (r % WIN) * SLAB, SLAB), SLAB)


def gather_own(s, src, dst):
    def row(r, _):
        y = dot(s.pm[0:96, 0:112], src[r + SHIFT, 0:28].reshape(112, C)).astype(BF)
        for c in range(6):
            dst[slab(r, c), :] = y[c * SLAB:(c + 1) * SLAB]
        return 0
    lax.fori_loop(0, 25, row, 0, unroll=25)


def gather_rest(s, src, dst):
    def row(r, _):
        y = dot(s.pm[96:128], src[r + SHIFT].reshape(128, C)).astype(BF)
        for c in range(2):
            dst[slab(r, 6 + c), :] = y[c * SLAB:(c + 1) * SLAB]
        return 0
    lax.fori_loop(0, 25, row, 0, unroll=25)
    for r in range(25, 28):
        y = dot(s.pm[...], src[r + SHIFT].reshape(128, C)).astype(BF)
        for c in range(8):
            dst[slab(r, c), :] = y[c * SLAB:(c + 1) * SLAB]


def halo_out_copies(s, n):
    east, south = (s.lon + 1) % 16, (s.lat + 1) % 8
    return [
        send(s.side.at[n, SHIFT:28], s.land_side.at[n, SHIFT:28], s.halo, 6 + 3 * n, (s.lat, east)),
        send(s.foot.at[n, :, 0:28], s.land_foot.at[n], s.halo, 7 + 3 * n, (south, s.lon)),
        send(s.foot.at[n, :, 28:32], s.land_side.at[n, 0:SHIFT], s.halo, 8 + 3 * n, (south, east)),
    ]


def grid_row(s, src, r, low, high):
    y = jnp.concatenate([src[slab(r, c), :] for c in range(low, high)], 0)
    return dot(s.pm[low * SLAB:high * SLAB], y, TN).astype(BF).reshape(32, LEV, C)


def scatter_foot(s, src, n):
    for r in range(25, 28):
        s.foot[n, r - 25] = grid_row(s, src, r, 0, 8)


def scatter_all(s, src, dst, n):
    scatter_foot(s, src, n)

    def row(r, _):
        y = grid_row(s, src, r, 0, 8)
        dst[r + SHIFT] = y[:28]
        s.side[n, r + SHIFT] = y[28:]
        return 0
    lax.fori_loop(0, 25, row, 0, unroll=25)
    for copy in halo_out_copies(s, n):
        copy.start()


def scatter_sent(s, src, dst, n):
    scatter_foot(s, src, n)

    def row(r, _):
        y = grid_row(s, src, r, 6, 8)
        dst[r + SHIFT, 24:28] = y[24:28]
        s.side[n, r + SHIFT] = y[28:]
        return 0
    lax.fori_loop(0, 25, row, 0, unroll=25)
    for copy in halo_out_copies(s, n):
        copy.start()


def scatter_own(s, src, dst):
    def row(r, _):
        dst[r + SHIFT, 0:24] = grid_row(s, src, r, 0, 6)[0:24]
        return 0
    lax.fori_loop(0, 25, row, 0, unroll=25)


def halo_out_done(s, dst, n):
    for copy in halo_out_copies(s, n):
        copy.wait()
    dst[0:SHIFT] = s.land_foot[n]

    def row(r, _):
        both = dst[r, 0:4].reshape(16, C) + s.land_side[n, r].reshape(16, C)
        dst[r, 0:4] = both.reshape(4, LEV, C)
        return 0
    lax.fori_loop(0, 28, row, 0, unroll=28)


def thirds(value):
    high = value.astype(BF)
    rest = value - high.astype(F32)
    mid = rest.astype(BF)
    return jnp.concatenate([v.astype(F32) for v in (high, mid, (rest - mid.astype(F32)))], 0).astype(BF)


def chosen(s, i):
    slots = lax.broadcasted_iota(jnp.int32, (512, 256), 0)
    return jnp.where(slots == s.index[i:i + 1, :], 1.0, 0.0).astype(BF)


def expand_table(s):
    s.rel[...] = jnp.zeros_like(s.rel)
    s.rel[:, 0:NREL] = s.rel_bias[...]
    table = thirds(s.rel[...])
    s.strip[...] = jnp.zeros_like(s.strip)
    for i in range(WIN * WLEV):
        out = dot(table, chosen(s, i))
        s.strip[i] = out[0:8] + out[8:16] + out[16:24]


def collect_table(s):
    for h in range(HEADS):
        j, g = h % HALF, h // HALF
        total = None
        for ak in range(WIN):
            piece = s.dbias[j * WROWS + ak * SLAB:j * WROWS + (ak + 1) * SLAB, g * 128:g * 128 + WROWS]
            before = (6 - ak) * SLAB
            parts = [jnp.zeros((SLAB, before), F32)] if before else []
            moved = jnp.concatenate(parts + [piece, jnp.zeros((SLAB, 256 - before - WROWS), F32)], 1)
            total = moved if total is None else total + moved
        s.dstrip[h] = total
    table = None
    for i in range(WIN * WLEV):
        part = dot(thirds(s.dstrip[:, i, :]), chosen(s, i), NT)
        table = part if table is None else table + part
    table = table[0:8] + table[8:16] + table[16:24]
    s.small[0:8] = table[:, 0:256]
    s.small[8:16] = table[:, 256:512]
    s.acc[:, SHORT] = jnp.zeros((C, 128), F32)
    s.acc[0:32, SHORT] = s.small[:, 0:128]
    s.acc[32:64, SHORT] = s.small[:, 128:256]


def tail_lon_copies(s):
    mine, out = s.tail_lon.at[s.lon], []
    for d in range(1, 16):
        out.append(send(mine, mine, s.tails, d, (s.lat, (s.lon + d) % 16)))
    return out


def tail_lat_copies(s):
    mine, out = s.tail_lat.at[s.lat], []
    for d in range(1, 8):
        out.append(send(mine, mine, s.tails, 15 + d, ((s.lat + d) % 8, s.lon)))
    return out


def tail_lon_start(s):
    s.tail_lon[s.lon] = s.tail[...]
    for copy in tail_lon_copies(s):
        copy.start()


def tail_lat_start(s):
    for copy in tail_lon_copies(s):
        copy.wait()
    s.tail_lat[s.lat] = sum(s.tail_lon[i] for i in range(16))
    for copy in tail_lat_copies(s):
        copy.start()


def tail_done(s):
    for copy in tail_lat_copies(s):
        copy.wait()
    return sum(s.tail_lat[i] for i in range(8))


class Exchange:
    def __init__(self, s, cols, number):
        self.s, self.cols, self.sems = s, slice(*cols), s.sums[number]
        self.core, self.chip = s.lon % 2, s.lon // 2
        self.half = pl.ds(pl.multiple_of(self.core * 128, 128), 128)
        self.other = pl.ds(pl.multiple_of((1 - self.core) * 128, 128), 128)
        self.share = pl.ds(pl.multiple_of(self.core * 128 + self.chip * 16, 16), 16)
        self.twin = (s.lat, s.lon + 1 - 2 * self.core)

    def core_copies(self):
        s = self.s
        out = [send(s.sent.at[self.other, self.cols], s.land_core.at[:, self.cols], self.sems, 0, self.twin)]
        return out

    def lon_copies(self):
        s, out = self.s, []
        for d in range(1, 8):
            peer = (self.chip + d) % 8
            to = (s.lat, peer * 2 + self.core)
            rows = pl.ds(pl.multiple_of(peer * 16, 16), 16)
            out.append(send(s.part.at[rows, self.cols], s.land_lon.at[self.chip, :, self.cols], self.sems, d, to))
        return out

    def lat_copies(self):
        s, out = self.s, []
        for d in range(1, 8):
            to = ((s.lat + d) % 8, s.lon)
            mine = s.land_lat.at[s.lat, :, self.cols]
            out.append(send(mine, mine, self.sems, 8 + d, to))
        return out

    def gather_copies(self):
        s, out = self.s, []
        for d in range(1, 8):
            to = (s.lat, ((self.chip + d) % 8) * 2 + self.core)
            mine = s.total.at[self.share, self.cols]
            out.append(send(mine, mine, self.sems, 16 + d, to))
        return out

    def pair_copies(self):
        mine = self.s.total.at[self.half, self.cols]
        return [send(mine, mine, self.sems, 16, self.twin)]

    def core_start(self):
        s = self.s
        s.sent[self.other, self.cols] = s.acc[self.other, self.cols].astype(BF)
        for copy in self.core_copies():
            copy.start()

    def lon_start(self):
        s = self.s
        for copy in self.core_copies():
            copy.wait()
        both = s.acc[self.half, self.cols] + s.land_core[:, self.cols].astype(F32)
        s.acc[self.half, self.cols] = both
        s.part[:, self.cols] = both.astype(BF)
        for copy in self.lon_copies():
            copy.start()

    def lat_start(self):
        s = self.s
        for copy in self.lon_copies():
            copy.wait()
        total = s.acc[self.share, self.cols]
        for d in range(1, 8):
            total += s.land_lon[(self.chip + d) % 8, :, self.cols].astype(F32)
        s.land_lat[s.lat, :, self.cols] = total.astype(BF)
        for copy in self.lat_copies():
            copy.start()

    def gather_start(self):
        s = self.s
        for copy in self.lat_copies():
            copy.wait()
        total = s.land_lat[0, :, self.cols].astype(F32)
        for i in range(1, 8):
            total += s.land_lat[i, :, self.cols].astype(F32)
        s.total[self.share, self.cols] = total.astype(BF)
        for copy in self.gather_copies():
            copy.start()

    def pair_start(self):
        for copy in self.gather_copies():
            copy.wait()
        for copy in self.pair_copies():
            copy.start()

    def pair_done(self):
        for copy in self.pair_copies():
            copy.wait()


def compute(s, chunk_windows=8):
    pair, group = head_masks()
    scale = np.float32(HD ** -0.5)
    CH = chunk_windows * WROWS
    nwin = 32

    enter(s)

    expand_table(s)
    key_row = lax.broadcasted_iota(jnp.int32, (WROWS, 256), 0)
    lane = lax.broadcasted_iota(jnp.int32, (WROWS, 256), 1)
    qa, ka = (lane % 128) // SLAB, key_row // SLAB
    empty = (key_row % SLAB) >= WIN * WLEV
    cut = jnp.logical_and((qa >= WIN - SHIFT) != (ka >= WIN - SHIFT), s.last)
    for j in range(HALF):
        tiles = []
        for g in range(2):
            strip = s.strip[:, j + HALF * g, :] * LOG2E
            rows = [strip[:, (6 - ak) * SLAB:(6 - ak) * SLAB + WROWS] for ak in range(WIN)]
            tile = jnp.concatenate(rows, 0)
            tiles.append(jnp.concatenate([tile, jnp.zeros((WROWS, 128 - WROWS), F32)], 1))
        full = jnp.where(empty, NEG, jnp.concatenate(tiles, 1))
        s.bias[0, j * WROWS:(j + 1) * WROWS] = full
        s.bias[1, j * WROWS:(j + 1) * WROWS] = jnp.where(cut, NEG, full)
    s.dbias[...] = jnp.zeros_like(s.dbias)
    s.tail[...] = jnp.zeros_like(s.tail)
    s.acc[...] = jnp.zeros_like(s.acc)
    s.small[...] = jnp.zeros_like(s.small)
    near_done(s)
    for src, dst in ((s.x, s.z), (s.g, s.gz)):
        gather_own(s, src, dst)
    halo_start(s)
    for copy in s.weights:
        copy.wait()

    def rest():
        halo_in_done(s)
        for src, dst in ((s.x, s.z), (s.g, s.gz)):
            gather_rest(s, src, dst)

    def forward_window(w):
        rows = pl.ds(pl.multiple_of(w * WROWS, WROWS), WROWS)
        arows = pl.multiple_of(w * (HALF * WROWS), HALF * WROWS)
        q, k, v = s.p[rows, 0:C], s.p[rows, C:2 * C], s.p[rows, 2 * C:3 * C]
        scores = dot(stack_pairs(k, pair), stack_groups(q, group), NT)
        which = (w >= 24).astype(jnp.int32)
        vt = v.T
        lows = []
        for j in range(HALF):
            t = scores[j * WROWS:(j + 1) * WROWS] * (scale * LOG2E) + s.bias[which, j * WROWS:(j + 1) * WROWS]
            e = jnp.exp2(t - jnp.max(t, 0, keepdims=True))
            att = e * (1.0 / jnp.sum(e, 0, keepdims=True))
            low = att.astype(BF)
            s.att[pl.ds(arows + j * WROWS, WROWS), :] = low
            lows.append(low)
        s.mixed[rows, :] = down_keys(vt, jnp.concatenate(lows, 0)).astype(BF)

    def phase_a(step, _):
        i = step
        pl.when(step == 1)(rest)
        rows = pl.ds(pl.multiple_of(i * (2 * CH), CH), 2 * CH)
        x = s.z[rows, :].astype(F32)
        _, _, hidden1 = layer_norm(x, s.gains[0:1], s.shifts[0:1])
        s.p[rows, :] = (dot(hidden1, s.w_qkv[...]) + s.b_qkv[...]).astype(BF)

        def win(w, _):
            for u in range(4):
                forward_window(i * (2 * chunk_windows) + 4 * w + u)
            return 0
        lax.fori_loop(0, 4, win, 0)

        mixed = s.mixed[rows, :]
        resid = s.z[rows, :].astype(F32) + dot(mixed, s.w_proj[...])
        xhat2, istd2, hidden2 = layer_norm(resid, s.gains[1:2], s.shifts[1:2])
        gr = s.gz[rows, :]
        gr_t, hid_t = gr.T, hidden2.T
        out, gh = resid, None
        for f in range(4):
            cols = slice(f * 256, f * 256 + 256)
            act, slope = gelu_both(dot(hidden2, s.w_in[:, cols]))
            act = act.astype(BF)
            out = out + dot(act, s.w_out[cols, :])
            s.acc[:, 1024 + f * 256:1280 + f * 256] += dot(gr_t, act)
            gp = (dot(gr, s.w_out[cols, :], NT) * slope).astype(BF)
            s.acc[:, cols] += dot(hid_t, gp)
            part = dot(gp, s.w_in[:, cols], NT)
            gh = part if gh is None else gh + part
        s.gz[rows, :] = out.astype(BF)
        s.small[19:20] += jnp.sum(gh * xhat2, 0, keepdims=True)
        s.small[20:21] += jnp.sum(gh, 0, keepdims=True)
        gres = gr.astype(F32) + norm_backward(gh, xhat2, istd2, s.gains[1:2])
        s.gres[rows, :] = gres
        low = gres.astype(BF)
        s.acc[:, W_PROJ] += dot(mixed, low, TN)
        s.mixed[rows, :] = dot(low, s.w_proj[...], NT).astype(BF)
        return 0

    lax.fori_loop(0, 2, phase_a, 0)
    for f in range(4):
        cols = slice(1024 + f * 256, 1280 + f * 256)
        s.acc[:, cols] = s.acc[:, cols].T
    first, late = Exchange(s, FIRST, 0), Direct(s, LATE, 2)
    first.core_start()
    scatter_all(s, s.gz, s.res, 0)

    def backward_window(w):
        rows = pl.ds(pl.multiple_of(w * WROWS, WROWS), WROWS)
        arows = pl.multiple_of(w * (HALF * WROWS), HALF * WROWS)
        q, k, v = s.p[rows, 0:C], s.p[rows, C:2 * C], s.p[rows, 2 * C:3 * C]
        gm2 = stack_groups(s.mixed[rows, :], group)
        ga = dot(stack_pairs(v, pair), gm2, NT)
        lows, dlows = [], []
        for j in range(HALF):
            low = s.att[pl.ds(arows + j * WROWS, WROWS), :]
            att = low.astype(F32)
            t = att * ga[j * WROWS:(j + 1) * WROWS]
            ds = t - att * jnp.sum(t, 0, keepdims=True)
            s.dbias[j * WROWS:(j + 1) * WROWS] += ds
            lows.append(low)
            dlows.append((ds * scale).astype(BF))
        low, dlow = jnp.concatenate(lows, 0), jnp.concatenate(dlows, 0)
        gv = pick_pairs(dot(low, gm2), pair).astype(BF)
        gk = pick_pairs(dot(dlow, stack_groups(q, group)), pair).astype(BF)
        gq = down_keys(k.T, dlow).astype(BF)
        s.p[rows, 0:C] = gq
        s.p[rows, C:2 * C] = gk
        s.p[rows, 2 * C:3 * C] = gv

    def phase_b(i, _):
        rows = pl.ds(pl.multiple_of(i * CH, CH), CH)
        for at, step in ((1, first.lon_start), (2, first.lat_start), (3, first.gather_start)):
            pl.when(i == at)(step)

        def win(w, _):
            for u in range(4):
                backward_window(i * chunk_windows + 4 * w + u)
            return 0
        lax.fori_loop(0, chunk_windows // 4, win, 0)
        _, _, hidden = layer_norm(s.z[rows, :].astype(F32), s.gains[0:1], s.shifts[0:1])
        gp = s.p[rows, :]
        s.acc[:, W_QKV] += dot(hidden, gp, TN)
        sums = jnp.sum(gp.astype(F32), 0, keepdims=True)
        for part in range(3):
            s.small[16 + part:17 + part] += sums[:, part * C:(part + 1) * C]
        return 0

    lax.fori_loop(0, 4, phase_b, 0)
    collect_table(s)
    late.lon_start()
    halo_out_done(s, s.res, 0)
    s.leave["res"].start()

    def phase_c(step, _):
        i = 3 - step
        for at, action in (
            (1, first.pair_start), (2, lambda: scatter_sent(s, s.z, s.ing, 1)), (3, late.lat_start),
        ):
            pl.when(step == at)(action)
        rows = pl.ds(pl.multiple_of(i * CH, CH), CH)
        xhat, istd, _ = layer_norm(s.z[rows, :].astype(F32), s.gains[0:1], s.shifts[0:1])
        gh = dot(s.p[rows, :], s.w_qkv[...], NT)
        s.tail[0:1] += jnp.sum(gh * xhat, 0, keepdims=True)
        s.tail[1:2] += jnp.sum(gh, 0, keepdims=True)
        s.z[rows, :] = (s.gres[rows, :] + norm_backward(gh, xhat, istd, s.gains[0:1])).astype(BF)
        return 0

    lax.fori_loop(0, 4, phase_c, 0)
    tail_lon_start(s)
    late.gather_start()
    scatter_own(s, s.z, s.ing)
    tail_lat_start(s)
    first.pair_done()
    def scaled(value):
        return value.astype(F32) * s.scale

    s.o_in[...] = scaled(s.total[:, W_IN])
    for f in range(4):
        s.o_out[f * 256:(f + 1) * 256] = scaled(s.total[:, 1024 + f * 256:1280 + f * 256])
    s.o_proj[...] = scaled(s.total[:, W_PROJ])
    for name in ("o_in", "o_out", "o_proj"):
        s.leave[name].start()
    halo_out_done(s, s.ing, 1)
    s.leave["ing"].start()
    late.done()
    s.o_qkv[...] = scaled(s.total[:, W_QKV])
    s.leave["o_qkv"].start()
    short = [scaled(s.total[0:32, SHORT]), scaled(s.total[32:64, SHORT])]
    for side in range(2):
        lanes = slice(side * 128, side * 128 + 128)
        s.o_table[:, lanes] = short[side][0:8]
        s.o_gains[1:2, lanes] = short[side][19:20]
        s.o_shifts[1:2, lanes] = short[side][20:21]
        for part in range(3):
            s.o_bias[part * C + side * 128:part * C + side * 128 + 128] = short[side][16 + part]
    s.o_table[:, 256:384] = short[0][8:16]
    s.o_table[:, 384:NREL] = short[1][8:16][:, :NREL - 384]
    tail = tail_done(s) * s.scale
    s.o_gains[0:1] = tail[0:1]
    s.o_shifts[0:1] = tail[1:2]
    for name in BIG:
        s.leave[name].wait()


class Direct:
    def __init__(self, s, cols, number):
        self.s, self.cols, self.sems = s, slice(*cols), s.sums[number]
        self.share = pl.ds(pl.multiple_of(s.lon * 16, 16), 16)

    def lon_copies(self):
        s, out = self.s, []
        for d in range(1, 16):
            peer = (s.lon + d) % 16
            rows = pl.ds(pl.multiple_of(peer * 16, 16), 16)
            out.append(send(s.sent.at[rows, self.cols], s.land_late.at[s.lon], self.sems, d, (s.lat, peer)))
        return out

    def lat_copies(self):
        s, out = self.s, []
        mine = s.land_lat.at[s.lat, :, self.cols]
        for d in range(1, 8):
            out.append(send(mine, mine, self.sems, 15 + d, ((s.lat + d) % 8, s.lon)))
        return out

    def gather_copies(self):
        s, out = self.s, []
        mine = s.total.at[self.share, self.cols]
        for d in range(1, 16):
            out.append(send(mine, mine, self.sems, 22 + d, (s.lat, (s.lon + d) % 16)))
        return out

    def lon_start(self):
        s = self.s
        s.sent[:, self.cols] = s.acc[:, self.cols].astype(BF)
        for copy in self.lon_copies():
            copy.start()

    def lat_start(self):
        s = self.s
        for copy in self.lon_copies():
            copy.wait()
        total = s.acc[self.share, self.cols]
        for d in range(1, 16):
            total += s.land_late[(s.lon + d) % 16].astype(F32)
        s.land_lat[s.lat, :, self.cols] = total.astype(BF)
        for copy in self.lat_copies():
            copy.start()

    def gather_start(self):
        s = self.s
        for copy in self.lat_copies():
            copy.wait()
        total = s.land_lat[0, :, self.cols].astype(F32)
        for i in range(1, 8):
            total += s.land_lat[i, :, self.cols].astype(F32)
        s.total[self.share, self.cols] = total.astype(BF)
        for copy in self.gather_copies():
            copy.start()

    def done(self):
        for copy in self.gather_copies():
            copy.wait()


class Refs:
    pass


T = 32 * WROWS
GRID = (LEV, C)
INS = ("x_in", "g_in", "pm", "index", "gains", "shifts", "w_qkv", "b_qkv", "w_proj", "w_in", "w_out", "rel_bias")
OUTS = {
    "res": ((28, 28) + GRID, BF), "ing": ((28, 28) + GRID, BF), "o_gains": ((2, C), F32), "o_shifts": ((2, C), F32),
    "o_qkv": ((C, 3 * C), F32), "o_bias": ((3 * C,), F32), "o_proj": ((C, C), F32), "o_in": ((C, FF), F32),
    "o_out": ((FF, C), F32), "o_table": ((HEADS, NREL), F32),
}
SCRATCH = {
    "x": ((31, 32) + GRID, BF), "g": ((31, 32) + GRID, BF),
    "z": ((T, C), BF), "gz": ((T, C), BF), "p": ((T, 3 * C), BF), "att": ((T * HALF, 256), BF), "mixed": ((T, C), BF),
    "gres": ((T, C), F32), "bias": ((2, HALF * WROWS, 256), F32), "dbias": ((HALF * WROWS, 256), F32),
    "rel": ((8, 512), F32), "strip": ((SLAB, 8, 256), F32), "dstrip": ((8, SLAB, 256), F32),
    "acc": ((256, COLS), F32), "small": ((32, C), F32), "land_late": ((16, 16, 896), BF), "sent": ((256, COLS), BF), "land_core": ((128, COLS), BF), "part": ((128, COLS), BF),
    "land_lon": ((8, 16, COLS), BF), "land_lat": ((8, 16, COLS), BF), "total": ((256, COLS), BF),
    "side": ((2, 28, 4) + GRID, BF), "foot": ((2, 3, 32) + GRID, BF), "land_side": ((2, 28, 4) + GRID, BF),
    "land_foot": ((2, 3, 28) + GRID, BF),
    "tail": ((8, C), F32), "tail_lon": ((16, 8, C), F32), "tail_lat": ((8, 8, C), F32),
}
SEMS = (2, 12, 12, 24, 24, 24, 24, 38, 38, 23, 23, 6, 4)


WEIGHTS = {"w_qkv": ((C, 3 * C), BF), "w_proj": ((C, C), BF), "w_in": ((C, FF), BF), "w_out": ((FF, C), BF)}
BIG = ("res", "ing", "o_qkv", "o_proj", "o_in", "o_out")


def kernel(scale, *refs):
    s = Refs()
    names = INS + tuple(OUTS) + tuple(SCRATCH)
    for name, ref in zip(names, refs):
        setattr(s, name, ref)
    held = refs[len(names):len(names) + len(BIG)]
    s.leave = {}
    local_weights = refs[len(names) + len(BIG):len(names) + len(BIG) + len(WEIGHTS)]
    sems = refs[len(names) + len(BIG) + len(WEIGHTS):]
    s.weights = []
    for i, name in enumerate(WEIGHTS):
        s.weights.append(pltpu.make_async_copy(getattr(s, name), local_weights[i], sems[12].at[i]))
        setattr(s, name, local_weights[i])
    for i, name in enumerate(BIG):
        s.leave[name] = pltpu.make_async_copy(held[i], getattr(s, name), sems[11].at[i])
        setattr(s, name, held[i])
    s.near_sem, s.halo, s.tails = sems[0], sems[1:3], sems[9:11]
    s.sums = (sems[3:5], sems[5:7], sems[7:9])
    s.lat, s.lon = lax.axis_index("lat"), lax.axis_index("lon")
    s.last, s.scale = s.lat == 7, scale
    compute(s)


def fused(scale, *args):
    vm = pl.BlockSpec(memory_space=pltpu.VMEM)
    return pl.pallas_call(
        functools.partial(kernel, scale),
        out_shape=tuple(jax.ShapeDtypeStruct(*v) for v in OUTS.values()),
        in_specs=[
            pl.BlockSpec(memory_space=pl.ANY) if name in WEIGHTS or name in ("x_in", "g_in") else vm for name in INS
        ],
        out_specs=[pl.BlockSpec(memory_space=pl.ANY) if name in BIG else vm for name in OUTS],
        scratch_shapes=[pltpu.VMEM(*v) for v in SCRATCH.values()] + [pltpu.VMEM(*OUTS[name]) for name in BIG] + [
            pltpu.VMEM(*v) for v in WEIGHTS.values()
        ] + [pltpu.SemaphoreType.DMA((n,)) for n in SEMS],
        compiler_params=pltpu.CompilerParams(
            vmem_limit_bytes=63 * 1024 * 1024, collective_id=0, has_side_effects=True
        ),
        name="windows",
    )(*args)


def deliver(arrays):
    count = len(arrays)

    def body(*refs):
        ins, outs, held, sems = refs[:count], refs[count:2 * count], refs[2 * count:3 * count], refs[3 * count]
        come = [pltpu.make_async_copy(ins[i], held[i], sems.at[0, i]) for i in range(count)]
        leave = [pltpu.make_async_copy(held[i], outs[i], sems.at[1, i]) for i in range(count)]
        for copy in come:
            copy.start()
        for i in range(count):
            come[i].wait()
            leave[i].start()
        for copy in leave:
            copy.wait()

    some = pl.BlockSpec(memory_space=pl.ANY)
    return pl.pallas_call(
        body,
        out_shape=tuple(jax.ShapeDtypeStruct(v.shape, v.dtype) for v in arrays),
        in_specs=[some] * count,
        out_specs=[some] * count,
        scratch_shapes=[pltpu.VMEM(v.shape, v.dtype) for v in arrays] + [pltpu.SemaphoreType.DMA((2, count))],
        compiler_params=pltpu.CompilerParams(vmem_limit_bytes=62 * 1024 * 1024),
        name="deliver",
    )(*arrays)


def local(tokens, out_grad, gains, shifts, w_qkv, b_qkv, w_proj, w_in, w_out, rel_bias):
    rows_n, cols_n, levels, channels = tokens.shape
    scale = float(rows_n * lax.axis_size("lat") * cols_n * lax.axis_size("lon") * levels) ** -0.5
    outs = fused(
        scale, tokens, out_grad, jnp.asarray(placement(), BF), jnp.asarray(strip_map()), gains, shifts, w_qkv, b_qkv,
        w_proj, w_in, w_out, rel_bias,
    )
    return deliver(outs)


def solution(mesh):
    big = P("lat", "lon", None, None)
    return jax.shard_map(
        local, mesh=mesh, in_specs=(big, big) + (P(),) * 8, out_specs=(big, big) + (P(),) * 8, check_vma=False
    )
```

```python
import functools

import jax
import jax.numpy as jnp
import numpy as np
from jax import lax
from jax.experimental import pallas as pl
from jax.experimental.pallas import tpu as pltpu
from jax.sharding import PartitionSpec as P

WIN = 7
LEV = 4
WLEV = 2
SHIFT = 3
EPS = 1e-05
NEG = -1e30
HEADS = 8
HD = 32
C = 256
FF = 1024
SLAB = 16
WROWS = WIN * SLAB
HALF = HEADS // 2
PAIR = 2 * 128
NREL = 507
BF = jnp.bfloat16
F32 = jnp.float32

NN = (((1,), (0,)), ((), ()))
NT = (((1,), (1,)), ((), ()))
TN = (((0,), (0,)), ((), ()))


def dot(a, b, dims=NN):
    return lax.dot_general(a, b, dims, preferred_element_type=F32)


def placement():
    matrix = np.zeros((128, 128), np.float32)
    for wc in range(4):
        for lw in range(2):
            for b in range(WIN):
                for l in range(WLEV):
                    row = (wc * 2 + lw) * SLAB + b * WLEV + l
                    matrix[row, (wc * WIN + SHIFT + b) * LEV + lw * WLEV + l] = 1.0
    return matrix


def strip_map():
    index = np.full((SLAB, 256), -1, np.int32)
    for bk in range(WIN):
        for lk in range(WLEV):
            for da in range(13):
                for bq in range(WIN):
                    for lq in range(WLEV):
                        index[bk * WLEV + lk, da * SLAB + bq * WLEV + lq] = (
                            (da * 13 + bq - bk + 6) * 3 + lq - lk + 1
                        )
    return index


def layer_norm(x, gain, shift):
    center = x - jnp.mean(x, -1, keepdims=True)
    istd = lax.rsqrt(jnp.mean(center * center, -1, keepdims=True) + EPS)
    xhat = center * istd
    return xhat, istd, (xhat * gain + shift).astype(BF)


def norm_backward(up, xhat, istd, gain):
    n = up * gain
    return istd * (n - jnp.mean(n, -1, keepdims=True) - xhat * jnp.mean(n * xhat, -1, keepdims=True))


def gelu_both(p):
    c0 = np.float32(np.sqrt(2.0 / np.pi))
    c1 = np.float32(0.044715 * np.sqrt(2.0 / np.pi))
    p2 = p * p
    t = jnp.tanh(p * (c0 + c1 * p2))
    half = 0.5 + 0.5 * t
    act = p * half
    slope = half + act * (1.0 - half) * ((2.0 * c0) + (6.0 * c1) * p2)
    return act, slope


def head_masks():
    lane = lax.broadcasted_iota(jnp.int32, (1, C), 1) // HD
    pair = [((lane % HALF) == j) for j in range(HALF)]
    group = [((lane // HALF) == g) for g in range(2)]
    return pair, group


def stack_pairs(v, pair):
    return jnp.concatenate([v * m.astype(BF) for m in pair], 0)


def stack_groups(v, group):
    pad = jnp.zeros((128 - WROWS, C), BF)
    return jnp.concatenate([v * group[0].astype(BF), pad, v * group[1].astype(BF), pad], 0)


def pick_pairs(r, pair):
    out = r[3 * WROWS:4 * WROWS]
    for j in range(3):
        out = jnp.where(pair[j], r[j * WROWS:(j + 1) * WROWS], out)
    return out


def down_keys(vt, low):
    parts = [None] * HEADS
    for j in range(HALF):
        lhs = jnp.concatenate([vt[j * HD:(j + 1) * HD], vt[(j + HALF) * HD:(j + HALF + 1) * HD]], 0)
        out = dot(lhs, low[j * WROWS:(j + 1) * WROWS])
        parts[j] = out[:HD, :128]
        parts[j + HALF] = out[HD:, 128:]
    return jnp.concatenate(parts, 0).T[:WROWS]


FIRST, LATE = (0, 2304), (2304, 3200)
W_IN, W_PROJ, W_QKV, SHORT = slice(0, 1024), slice(2048, 2304), slice(2304, 3072), slice(3072, 3200)
COLS = 3200
LOG2E = np.float32(1.4426950408889634)
MESH = pl.DeviceIdType.MESH


def send(src, dst, sems, index, device):
    return pltpu.make_async_remote_copy(
        src_ref=src, dst_ref=dst, send_sem=sems[0].at[index], recv_sem=sems[1].at[index],
        device_id=device, device_id_type=MESH,
    )


def greet_peers(s):
    peers = [((s.lat + d) % 8, s.lon) for d in range(1, 8)] + [(s.lat, (s.lon + d) % 16) for d in range(1, 16)]
    return peers + [((s.lat + d) % 8, (s.lon + d) % 16) for d in (1, -1)]


def near_copies(s):
    return [
        pltpu.make_async_copy(src, dst.at[0:28, 0:28], s.near_sem.at[n])
        for n, (src, dst) in enumerate(((s.x_in, s.x), (s.g_in, s.g)))
    ]


def halo_in_copies(s):
    west, north = (s.lon + 15) % 16, (s.lat + 7) % 8
    far = []
    for n, (src, dst) in enumerate(((s.x_in, s.x), (s.g_in, s.g))):
        far.append(send(src.at[:, 0:4], dst.at[0:28, 28:32], s.halo, 3 * n, (s.lat, west)))
        far.append(send(src.at[0:SHIFT], dst.at[28:31, 0:28], s.halo, 3 * n + 1, (north, s.lon)))
        far.append(send(src.at[0:SHIFT, 0:4], dst.at[28:31, 28:32], s.halo, 3 * n + 2, (north, west)))
    return far


def enter(s):
    for copy in near_copies(s) + s.weights:
        copy.start()
    barrier = pltpu.get_barrier_semaphore()
    for peer in greet_peers(s):
        pl.semaphore_signal(barrier, inc=1, device_id=peer, device_id_type=MESH)


def halo_start(s):
    pl.semaphore_wait(pltpu.get_barrier_semaphore(), len(greet_peers(s)))
    for copy in halo_in_copies(s):
        copy.start()


def near_done(s):
    for copy in near_copies(s):
        copy.wait()


def halo_in_done(s):
    for copy in halo_in_copies(s):
        copy.wait()


def slab(r, c):
    wr = r // WIN
    slot = jnp.where(wr < 3, wr * 6 + c if c < 6 else 12 + wr * 2 + c, 24 + c)
    return pl.ds(pl.multiple_of(slot * WROWS + (r % WIN) * SLAB, SLAB), SLAB)


def gather_own(s, src, dst):
    def row(r, _):
        y = dot(s.pm[0:96, 0:112], src[r + SHIFT, 0:28].reshape(112, C)).astype(BF)
        for c in range(6):
            dst[slab(r, c), :] = y[c * SLAB:(c + 1) * SLAB]
        return 0
    lax.fori_loop(0, 25, row, 0, unroll=25)


def gather_rest(s, src, dst):
    def row(r, _):
        y = dot(s.pm[96:128], src[r + SHIFT].reshape(128, C)).astype(BF)
        for c in range(2):
            dst[slab(r, 6 + c), :] = y[c * SLAB:(c + 1) * SLAB]
        return 0
    lax.fori_loop(0, 25, row, 0, unroll=25)
    for r in range(25, 28):
        y = dot(s.pm[...], src[r + SHIFT].reshape(128, C)).astype(BF)
        for c in range(8):
            dst[slab(r, c), :] = y[c * SLAB:(c + 1) * SLAB]


def halo_out_copies(s, n):
    east, south = (s.lon + 1) % 16, (s.lat + 1) % 8
    return [
        send(s.side.at[n, SHIFT:28], s.land_side.at[n, SHIFT:28], s.halo, 6 + 3 * n, (s.lat, east)),
        send(s.foot.at[n, :, 0:28], s.land_foot.at[n], s.halo, 7 + 3 * n, (south, s.lon)),
        send(s.foot.at[n, :, 28:32], s.land_side.at[n, 0:SHIFT], s.halo, 8 + 3 * n, (south, east)),
    ]


def grid_row(s, src, r, low, high):
    y = jnp.concatenate([src[slab(r, c), :] for c in range(low, high)], 0)
    return dot(s.pm[low * SLAB:high * SLAB], y, TN).astype(BF).reshape(32, LEV, C)


def scatter_foot(s, src, n):
    for r in range(25, 28):
        s.foot[n, r - 25] = grid_row(s, src, r, 0, 8)


def scatter_all(s, src, dst, n):
    scatter_foot(s, src, n)

    def row(r, _):
        y = grid_row(s, src, r, 0, 8)
        dst[r + SHIFT] = y[:28]
        s.side[n, r + SHIFT] = y[28:]
        return 0
    lax.fori_loop(0, 25, row, 0, unroll=25)
    for copy in halo_out_copies(s, n):
        copy.start()


def scatter_sent(s, src, dst, n):
    scatter_foot(s, src, n)

    def row(r, _):
        y = grid_row(s, src, r, 6, 8)
        dst[r + SHIFT, 24:28] = y[24:28]
        s.side[n, r + SHIFT] = y[28:]
        return 0
    lax.fori_loop(0, 25, row, 0, unroll=25)
    for copy in halo_out_copies(s, n):
        copy.start()


def scatter_own(s, src, dst):
    def row(r, _):
        dst[r + SHIFT, 0:24] = grid_row(s, src, r, 0, 6)[0:24]
        return 0
    lax.fori_loop(0, 25, row, 0, unroll=25)


def halo_out_done(s, dst, n):
    for copy in halo_out_copies(s, n):
        copy.wait()
    dst[0:SHIFT] = s.land_foot[n]

    def row(r, _):
        both = dst[r, 0:4].reshape(16, C) + s.land_side[n, r].reshape(16, C)
        dst[r, 0:4] = both.reshape(4, LEV, C)
        return 0
    lax.fori_loop(0, 28, row, 0, unroll=28)


def thirds(value):
    high = value.astype(BF)
    rest = value - high.astype(F32)
    mid = rest.astype(BF)
    return jnp.concatenate([v.astype(F32) for v in (high, mid, (rest - mid.astype(F32)))], 0).astype(BF)


def chosen(s, i):
    slots = lax.broadcasted_iota(jnp.int32, (512, 256), 0)
    return jnp.where(slots == s.index[i:i + 1, :], 1.0, 0.0).astype(BF)


def expand_table(s):
    s.rel[...] = jnp.zeros_like(s.rel)
    s.rel[:, 0:NREL] = s.rel_bias[...]
    table = thirds(s.rel[...])
    s.strip[...] = jnp.zeros_like(s.strip)
    for i in range(WIN * WLEV):
        out = dot(table, chosen(s, i))
        s.strip[i] = out[0:8] + out[8:16] + out[16:24]


def collect_table(s):
    for h in range(HEADS):
        j, g = h % HALF, h // HALF
        total = None
        for ak in range(WIN):
            piece = s.dbias[j * WROWS + ak * SLAB:j * WROWS + (ak + 1) * SLAB, g * 128:g * 128 + WROWS]
            before = (6 - ak) * SLAB
            parts = [jnp.zeros((SLAB, before), F32)] if before else []
            moved = jnp.concatenate(parts + [piece, jnp.zeros((SLAB, 256 - before - WROWS), F32)], 1)
            total = moved if total is None else total + moved
        s.dstrip[h] = total
    table = None
    for i in range(WIN * WLEV):
        part = dot(thirds(s.dstrip[:, i, :]), chosen(s, i), NT)
        table = part if table is None else table + part
    table = table[0:8] + table[8:16] + table[16:24]
    s.small[0:8] = table[:, 0:256]
    s.small[8:16] = table[:, 256:512]
    s.acc[:, SHORT] = jnp.zeros((C, 128), F32)
    s.acc[0:32, SHORT] = s.small[:, 0:128]
    s.acc[32:64, SHORT] = s.small[:, 128:256]


def tail_lon_copies(s):
    mine, out = s.tail_lon.at[s.lon], []
    for d in range(1, 16):
        out.append(send(mine, mine, s.tails, d, (s.lat, (s.lon + d) % 16)))
    return out


def tail_lat_copies(s):
    mine, out = s.tail_lat.at[s.lat], []
    for d in range(1, 8):
        out.append(send(mine, mine, s.tails, 15 + d, ((s.lat + d) % 8, s.lon)))
    return out


def tail_lon_start(s):
    s.tail_lon[s.lon] = s.tail[...]
    for copy in tail_lon_copies(s):
        copy.start()


def tail_lat_start(s):
    for copy in tail_lon_copies(s):
        copy.wait()
    s.tail_lat[s.lat] = sum(s.tail_lon[i] for i in range(16))
    for copy in tail_lat_copies(s):
        copy.start()


def tail_done(s):
    for copy in tail_lat_copies(s):
        copy.wait()
    return sum(s.tail_lat[i] for i in range(8))


class Exchange:
    def __init__(self, s, cols, number):
        self.s, self.cols, self.sems = s, slice(*cols), s.sums[number]
        self.core, self.chip = s.lon % 2, s.lon // 2
        self.half = pl.ds(pl.multiple_of(self.core * 128, 128), 128)
        self.other = pl.ds(pl.multiple_of((1 - self.core) * 128, 128), 128)
        self.share = pl.ds(pl.multiple_of(self.core * 128 + self.chip * 16, 16), 16)
        self.twin = (s.lat, s.lon + 1 - 2 * self.core)

    def core_copies(self):
        s = self.s
        out = [send(s.sent.at[self.other, self.cols], s.land_core.at[:, self.cols], self.sems, 0, self.twin)]
        return out

    def lon_copies(self):
        s, out = self.s, []
        for d in range(1, 8):
            peer = (self.chip + d) % 8
            to = (s.lat, peer * 2 + self.core)
            rows = pl.ds(pl.multiple_of(peer * 16, 16), 16)
            out.append(send(s.part.at[rows, self.cols], s.land_lon.at[self.chip, :, self.cols], self.sems, d, to))
        return out

    def lat_copies(self):
        s, out = self.s, []
        for d in range(1, 8):
            to = ((s.lat + d) % 8, s.lon)
            mine = s.land_lat.at[s.lat, :, self.cols]
            out.append(send(mine, mine, self.sems, 8 + d, to))
        return out

    def gather_copies(self):
        s, out = self.s, []
        for d in range(1, 8):
            to = (s.lat, ((self.chip + d) % 8) * 2 + self.core)
            mine = s.total.at[self.share, self.cols]
            out.append(send(mine, mine, self.sems, 16 + d, to))
        return out

    def pair_copies(self):
        mine = self.s.total.at[self.half, self.cols]
        return [send(mine, mine, self.sems, 16, self.twin)]

    def core_start(self):
        s = self.s
        s.sent[self.other, self.cols] = s.acc[self.other, self.cols].astype(BF)
        for copy in self.core_copies():
            copy.start()

    def lon_start(self):
        s = self.s
        for copy in self.core_copies():
            copy.wait()
        both = s.acc[self.half, self.cols] + s.land_core[:, self.cols].astype(F32)
        s.acc[self.half, self.cols] = both
        s.part[:, self.cols] = both.astype(BF)
        for copy in self.lon_copies():
            copy.start()

    def lat_start(self):
        s = self.s
        for copy in self.lon_copies():
            copy.wait()
        total = s.acc[self.share, self.cols]
        for d in range(1, 8):
            total += s.land_lon[(self.chip + d) % 8, :, self.cols].astype(F32)
        s.land_lat[s.lat, :, self.cols] = total.astype(BF)
        for copy in self.lat_copies():
            copy.start()

    def gather_start(self):
        s = self.s
        for copy in self.lat_copies():
            copy.wait()
        total = s.land_lat[0, :, self.cols].astype(F32)
        for i in range(1, 8):
            total += s.land_lat[i, :, self.cols].astype(F32)
        s.total[self.share, self.cols] = total.astype(BF)
        for copy in self.gather_copies():
            copy.start()

    def pair_start(self):
        for copy in self.gather_copies():
            copy.wait()
        for copy in self.pair_copies():
            copy.start()

    def pair_done(self):
        for copy in self.pair_copies():
            copy.wait()


def compute(s, chunk_windows=8):
    pair, group = head_masks()
    scale = np.float32(HD ** -0.5)
    CH = chunk_windows * WROWS
    nwin = 32

    enter(s)

    expand_table(s)
    key_row = lax.broadcasted_iota(jnp.int32, (WROWS, 256), 0)
    lane = lax.broadcasted_iota(jnp.int32, (WROWS, 256), 1)
    qa, ka = (lane % 128) // SLAB, key_row // SLAB
    empty = (key_row % SLAB) >= WIN * WLEV
    cut = jnp.logical_and((qa >= WIN - SHIFT) != (ka >= WIN - SHIFT), s.last)
    for j in range(HALF):
        tiles = []
        for g in range(2):
            strip = s.strip[:, j + HALF * g, :] * LOG2E
            rows = [strip[:, (6 - ak) * SLAB:(6 - ak) * SLAB + WROWS] for ak in range(WIN)]
            tile = jnp.concatenate(rows, 0)
            tiles.append(jnp.concatenate([tile, jnp.zeros((WROWS, 128 - WROWS), F32)], 1))
        full = jnp.where(empty, NEG, jnp.concatenate(tiles, 1))
        s.bias[0, j * WROWS:(j + 1) * WROWS] = full
        s.bias[1, j * WROWS:(j + 1) * WROWS] = jnp.where(cut, NEG, full)
    s.dbias[...] = jnp.zeros_like(s.dbias)
    s.tail[...] = jnp.zeros_like(s.tail)
    s.acc[...] = jnp.zeros_like(s.acc)
    s.small[...] = jnp.zeros_like(s.small)
    near_done(s)
    for src, dst in ((s.x, s.z), (s.g, s.gz)):
        gather_own(s, src, dst)
    halo_start(s)
    for copy in s.weights:
        copy.wait()

    def rest():
        halo_in_done(s)
        for src, dst in ((s.x, s.z), (s.g, s.gz)):
            gather_rest(s, src, dst)

    def forward_window(w):
        rows = pl.ds(pl.multiple_of(w * WROWS, WROWS), WROWS)
        arows = pl.multiple_of(w * (HALF * WROWS), HALF * WROWS)
        q, k, v = s.p[rows, 0:C], s.p[rows, C:2 * C], s.p[rows, 2 * C:3 * C]
        scores = dot(stack_pairs(k, pair), stack_groups(q, group), NT)
        which = (w >= 24).astype(jnp.int32)
        vt = v.T
        lows = []
        for j in range(HALF):
            t = scores[j * WROWS:(j + 1) * WROWS] * (scale * LOG2E) + s.bias[which, j * WROWS:(j + 1) * WROWS]
            e = jnp.exp2(t - jnp.max(t, 0, keepdims=True))
            att = e * (1.0 / jnp.sum(e, 0, keepdims=True))
            low = att.astype(BF)
            s.att[pl.ds(arows + j * WROWS, WROWS), :] = low
            lows.append(low)
        s.mixed[rows, :] = down_keys(vt, jnp.concatenate(lows, 0)).astype(BF)

    def phase_a(step, _):
        i = step
        pl.when(step == 1)(rest)
        rows = pl.ds(pl.multiple_of(i * (2 * CH), CH), 2 * CH)
        x = s.z[rows, :].astype(F32)
        _, _, hidden1 = layer_norm(x, s.gains[0:1], s.shifts[0:1])
        s.p[rows, :] = (dot(hidden1, s.w_qkv[...]) + s.b_qkv[...]).astype(BF)

        def win(w, _):
            for u in range(4):
                forward_window(i * (2 * chunk_windows) + 4 * w + u)
            return 0
        lax.fori_loop(0, 4, win, 0)

        mixed = s.mixed[rows, :]
        resid = s.z[rows, :].astype(F32) + dot(mixed, s.w_proj[...])
        xhat2, istd2, hidden2 = layer_norm(resid, s.gains[1:2], s.shifts[1:2])
        gr = s.gz[rows, :]
        gr_t, hid_t = gr.T, hidden2.T
        out, gh = resid, None
        for f in range(4):
            cols = slice(f * 256, f * 256 + 256)
            act, slope = gelu_both(dot(hidden2, s.w_in[:, cols]))
            act = act.astype(BF)
            out = out + dot(act, s.w_out[cols, :])
            s.acc[:, 1024 + f * 256:1280 + f * 256] += dot(gr_t, act)
            gp = (dot(gr, s.w_out[cols, :], NT) * slope).astype(BF)
            s.acc[:, cols] += dot(hid_t, gp)
            part = dot(gp, s.w_in[:, cols], NT)
            gh = part if gh is None else gh + part
        s.gz[rows, :] = out.astype(BF)
        s.small[19:20] += jnp.sum(gh * xhat2, 0, keepdims=True)
        s.small[20:21] += jnp.sum(gh, 0, keepdims=True)
        gres = gr.astype(F32) + norm_backward(gh, xhat2, istd2, s.gains[1:2])
        s.gres[rows, :] = gres
        low = gres.astype(BF)
        s.acc[:, W_PROJ] += dot(mixed, low, TN)
        s.mixed[rows, :] = dot(low, s.w_proj[...], NT).astype(BF)
        return 0

    lax.fori_loop(0, 2, phase_a, 0)
    for f in range(4):
        cols = slice(1024 + f * 256, 1280 + f * 256)
        s.acc[:, cols] = s.acc[:, cols].T
    first, late = Exchange(s, FIRST, 0), Direct(s, LATE, 2)
    first.core_start()
    scatter_all(s, s.gz, s.res, 0)

    def backward_window(w):
        rows = pl.ds(pl.multiple_of(w * WROWS, WROWS), WROWS)
        arows = pl.multiple_of(w * (HALF * WROWS), HALF * WROWS)
        q, k, v = s.p[rows, 0:C], s.p[rows, C:2 * C], s.p[rows, 2 * C:3 * C]
        gm2 = stack_groups(s.mixed[rows, :], group)
        ga = dot(stack_pairs(v, pair), gm2, NT)
        lows, dlows = [], []
        for j in range(HALF):
            low = s.att[pl.ds(arows + j * WROWS, WROWS), :]
            att = low.astype(F32)
            t = att * ga[j * WROWS:(j + 1) * WROWS]
            ds = t - att * jnp.sum(t, 0, keepdims=True)
            s.dbias[j * WROWS:(j + 1) * WROWS] += ds
            lows.append(low)
            dlows.append((ds * scale).astype(BF))
        low, dlow = jnp.concatenate(lows, 0), jnp.concatenate(dlows, 0)
        gv = pick_pairs(dot(low, gm2), pair).astype(BF)
        gk = pick_pairs(dot(dlow, stack_groups(q, group)), pair).astype(BF)
        gq = down_keys(k.T, dlow).astype(BF)
        s.p[rows, 0:C] = gq
        s.p[rows, C:2 * C] = gk
        s.p[rows, 2 * C:3 * C] = gv

    def phase_b(i, _):
        rows = pl.ds(pl.multiple_of(i * CH, CH), CH)
        for at, step in ((1, first.lon_start), (2, first.lat_start), (3, first.gather_start)):
            pl.when(i == at)(step)

        def win(w, _):
            for u in range(4):
                backward_window(i * chunk_windows + 4 * w + u)
            return 0
        lax.fori_loop(0, chunk_windows // 4, win, 0)
        _, _, hidden = layer_norm(s.z[rows, :].astype(F32), s.gains[0:1], s.shifts[0:1])
        gp = s.p[rows, :]
        s.acc[:, W_QKV] += dot(hidden, gp, TN)
        sums = jnp.sum(gp.astype(F32), 0, keepdims=True)
        for part in range(3):
            s.small[16 + part:17 + part] += sums[:, part * C:(part + 1) * C]
        return 0

    lax.fori_loop(0, 4, phase_b, 0)
    collect_table(s)
    late.lon_start()
    halo_out_done(s, s.res, 0)
    s.leave["res"].start()

    def phase_c(step, _):
        i = 3 - step
        for at, action in (
            (1, first.pair_start), (2, lambda: scatter_sent(s, s.z, s.ing, 1)), (2, late.lat_start),
        ):
            pl.when(step == at)(action)
        rows = pl.ds(pl.multiple_of(i * CH, CH), CH)
        xhat, istd, _ = layer_norm(s.z[rows, :].astype(F32), s.gains[0:1], s.shifts[0:1])
        gh = dot(s.p[rows, :], s.w_qkv[...], NT)
        s.tail[0:1] += jnp.sum(gh * xhat, 0, keepdims=True)
        s.tail[1:2] += jnp.sum(gh, 0, keepdims=True)
        s.z[rows, :] = (s.gres[rows, :] + norm_backward(gh, xhat, istd, s.gains[0:1])).astype(BF)
        return 0

    lax.fori_loop(0, 4, phase_c, 0)
    tail_lon_start(s)
    late.gather_start()
    scatter_own(s, s.z, s.ing)
    tail_lat_start(s)
    first.pair_done()
    def scaled(value):
        return value.astype(F32) * s.scale

    s.o_in[...] = scaled(s.total[:, W_IN])
    for f in range(4):
        s.o_out[f * 256:(f + 1) * 256] = scaled(s.total[:, 1024 + f * 256:1280 + f * 256])
    s.o_proj[...] = scaled(s.total[:, W_PROJ])
    for name in ("o_in", "o_out", "o_proj"):
        s.leave[name].start()
    halo_out_done(s, s.ing, 1)
    s.leave["ing"].start()
    late.done()
    s.o_qkv[...] = scaled(s.total[:, W_QKV])
    s.leave["o_qkv"].start()
    short = [scaled(s.total[0:32, SHORT]), scaled(s.total[32:64, SHORT])]
    for side in range(2):
        lanes = slice(side * 128, side * 128 + 128)
        s.o_table[:, lanes] = short[side][0:8]
        s.o_gains[1:2, lanes] = short[side][19:20]
        s.o_shifts[1:2, lanes] = short[side][20:21]
        for part in range(3):
            s.o_bias[part * C + side * 128:part * C + side * 128 + 128] = short[side][16 + part]
    s.o_table[:, 256:384] = short[0][8:16]
    s.o_table[:, 384:NREL] = short[1][8:16][:, :NREL - 384]
    tail = tail_done(s) * s.scale
    s.o_gains[0:1] = tail[0:1]
    s.o_shifts[0:1] = tail[1:2]
    for name in BIG:
        s.leave[name].wait()


class Direct:
    def __init__(self, s, cols, number):
        self.s, self.cols, self.sems = s, slice(*cols), s.sums[number]
        self.share = pl.ds(pl.multiple_of(s.lon * 16, 16), 16)

    def lon_copies(self):
        s, out = self.s, []
        for d in range(1, 16):
            peer = (s.lon + d) % 16
            rows = pl.ds(pl.multiple_of(peer * 16, 16), 16)
            out.append(send(s.sent.at[rows, self.cols], s.land_late.at[s.lon], self.sems, d, (s.lat, peer)))
        return out

    def lat_copies(self):
        s, out = self.s, []
        mine = s.land_lat.at[s.lat, :, self.cols]
        for d in range(1, 8):
            out.append(send(mine, mine, self.sems, 15 + d, ((s.lat + d) % 8, s.lon)))
        return out

    def gather_copies(self):
        s, out = self.s, []
        mine = s.total.at[self.share, self.cols]
        for d in range(1, 16):
            out.append(send(mine, mine, self.sems, 22 + d, (s.lat, (s.lon + d) % 16)))
        return out

    def lon_start(self):
        s = self.s
        s.sent[:, self.cols] = s.acc[:, self.cols].astype(BF)
        for copy in self.lon_copies():
            copy.start()

    def lat_start(self):
        s = self.s
        for copy in self.lon_copies():
            copy.wait()
        total = s.acc[self.share, self.cols]
        for d in range(1, 16):
            total += s.land_late[(s.lon + d) % 16].astype(F32)
        s.land_lat[s.lat, :, self.cols] = total.astype(BF)
        for copy in self.lat_copies():
            copy.start()

    def gather_start(self):
        s = self.s
        for copy in self.lat_copies():
            copy.wait()
        total = s.land_lat[0, :, self.cols].astype(F32)
        for i in range(1, 8):
            total += s.land_lat[i, :, self.cols].astype(F32)
        s.total[self.share, self.cols] = total.astype(BF)
        for copy in self.gather_copies():
            copy.start()

    def done(self):
        for copy in self.gather_copies():
            copy.wait()


class Refs:
    pass


T = 32 * WROWS
GRID = (LEV, C)
INS = ("x_in", "g_in", "pm", "index", "gains", "shifts", "w_qkv", "b_qkv", "w_proj", "w_in", "w_out", "rel_bias")
OUTS = {
    "res": ((28, 28) + GRID, BF), "ing": ((28, 28) + GRID, BF), "o_gains": ((2, C), F32), "o_shifts": ((2, C), F32),
    "o_qkv": ((C, 3 * C), F32), "o_bias": ((3 * C,), F32), "o_proj": ((C, C), F32), "o_in": ((C, FF), F32),
    "o_out": ((FF, C), F32), "o_table": ((HEADS, NREL), F32),
}
SCRATCH = {
    "x": ((31, 32) + GRID, BF), "g": ((31, 32) + GRID, BF),
    "z": ((T, C), BF), "gz": ((T, C), BF), "p": ((T, 3 * C), BF), "att": ((T * HALF, 256), BF), "mixed": ((T, C), BF),
    "gres": ((T, C), F32), "bias": ((2, HALF * WROWS, 256), F32), "dbias": ((HALF * WROWS, 256), F32),
    "rel": ((8, 512), F32), "strip": ((SLAB, 8, 256), F32), "dstrip": ((8, SLAB, 256), F32),
    "acc": ((256, COLS), F32), "small": ((32, C), F32), "land_late": ((16, 16, 896), BF), "sent": ((256, COLS), BF), "land_core": ((128, COLS), BF), "part": ((128, COLS), BF),
    "land_lon": ((8, 16, COLS), BF), "land_lat": ((8, 16, COLS), BF), "total": ((256, COLS), BF),
    "side": ((2, 28, 4) + GRID, BF), "foot": ((2, 3, 32) + GRID, BF), "land_side": ((2, 28, 4) + GRID, BF),
    "land_foot": ((2, 3, 28) + GRID, BF),
    "tail": ((8, C), F32), "tail_lon": ((16, 8, C), F32), "tail_lat": ((8, 8, C), F32),
}
SEMS = (2, 12, 12, 24, 24, 24, 24, 38, 38, 23, 23, 6, 4)


WEIGHTS = {"w_qkv": ((C, 3 * C), BF), "w_proj": ((C, C), BF), "w_in": ((C, FF), BF), "w_out": ((FF, C), BF)}
BIG = ("res", "ing", "o_qkv", "o_proj", "o_in", "o_out")


def kernel(scale, *refs):
    s = Refs()
    names = INS + tuple(OUTS) + tuple(SCRATCH)
    for name, ref in zip(names, refs):
        setattr(s, name, ref)
    held = refs[len(names):len(names) + len(BIG)]
    s.leave = {}
    local_weights = refs[len(names) + len(BIG):len(names) + len(BIG) + len(WEIGHTS)]
    sems = refs[len(names) + len(BIG) + len(WEIGHTS):]
    s.weights = []
    for i, name in enumerate(WEIGHTS):
        s.weights.append(pltpu.make_async_copy(getattr(s, name), local_weights[i], sems[12].at[i]))
        setattr(s, name, local_weights[i])
    for i, name in enumerate(BIG):
        s.leave[name] = pltpu.make_async_copy(held[i], getattr(s, name), sems[11].at[i])
        setattr(s, name, held[i])
    s.near_sem, s.halo, s.tails = sems[0], sems[1:3], sems[9:11]
    s.sums = (sems[3:5], sems[5:7], sems[7:9])
    s.lat, s.lon = lax.axis_index("lat"), lax.axis_index("lon")
    s.last, s.scale = s.lat == 7, scale
    compute(s)


def fused(scale, *args):
    vm = pl.BlockSpec(memory_space=pltpu.VMEM)
    return pl.pallas_call(
        functools.partial(kernel, scale),
        out_shape=tuple(jax.ShapeDtypeStruct(*v) for v in OUTS.values()),
        in_specs=[
            pl.BlockSpec(memory_space=pl.ANY) if name in WEIGHTS or name in ("x_in", "g_in") else vm for name in INS
        ],
        out_specs=[pl.BlockSpec(memory_space=pl.ANY) if name in BIG else vm for name in OUTS],
        scratch_shapes=[pltpu.VMEM(*v) for v in SCRATCH.values()] + [pltpu.VMEM(*OUTS[name]) for name in BIG] + [
            pltpu.VMEM(*v) for v in WEIGHTS.values()
        ] + [pltpu.SemaphoreType.DMA((n,)) for n in SEMS],
        compiler_params=pltpu.CompilerParams(
            vmem_limit_bytes=63 * 1024 * 1024, collective_id=0, has_side_effects=True
        ),
        name="windows",
    )(*args)


def deliver(arrays):
    count = len(arrays)

    def body(*refs):
        ins, outs, held, sems = refs[:count], refs[count:2 * count], refs[2 * count:3 * count], refs[3 * count]
        come = [pltpu.make_async_copy(ins[i], held[i], sems.at[0, i]) for i in range(count)]
        leave = [pltpu.make_async_copy(held[i], outs[i], sems.at[1, i]) for i in range(count)]
        for copy in come:
            copy.start()
        for i in range(count):
            come[i].wait()
            leave[i].start()
        for copy in leave:
            copy.wait()

    some = pl.BlockSpec(memory_space=pl.ANY)
    return pl.pallas_call(
        body,
        out_shape=tuple(jax.ShapeDtypeStruct(v.shape, v.dtype) for v in arrays),
        in_specs=[some] * count,
        out_specs=[some] * count,
        scratch_shapes=[pltpu.VMEM(v.shape, v.dtype) for v in arrays] + [pltpu.SemaphoreType.DMA((2, count))],
        compiler_params=pltpu.CompilerParams(vmem_limit_bytes=62 * 1024 * 1024),
        name="deliver",
    )(*arrays)


def local(tokens, out_grad, gains, shifts, w_qkv, b_qkv, w_proj, w_in, w_out, rel_bias):
    rows_n, cols_n, levels, channels = tokens.shape
    scale = float(rows_n * lax.axis_size("lat") * cols_n * lax.axis_size("lon") * levels) ** -0.5
    outs = fused(
        scale, tokens, out_grad, jnp.asarray(placement(), BF), jnp.asarray(strip_map()), gains, shifts, w_qkv, b_qkv,
        w_proj, w_in, w_out, rel_bias,
    )
    return deliver(outs)


def solution(mesh):
    big = P("lat", "lon", None, None)
    return jax.shard_map(
        local, mesh=mesh, in_specs=(big, big) + (P(),) * 8, out_specs=(big, big) + (P(),) * 8, check_vma=False
    )
```
